256 devices in a mesh: tile: 64 (over y, x_lo, z), src: 4 (over x_hi, core).
Axes of the slice: x: 4 (x_hi: 2, x_lo: 2; x = x_hi * 2 + x_lo), y: 4, z: 8, core: 2. Of those that a mesh axis runs over, the one named last changes fastest.
Arguments:
- excitation: bfloat16 [2, 512, 65536], P(None, 'src', 'tile'), may hold values from -6 to 6
- near_blocks: bfloat16 [128, 3, 2, 512, 512], P('tile'), may hold values from -0.02734375 to 0.02734375
- source_basis: bfloat16 [128, 2, 24, 512], P('tile'), may hold values from -0.1875 to 0.1875
- target_basis: bfloat16 [128, 2, 24, 512], P('tile'), may hold values from -0.625 to 0.625
- coupling: bfloat16 [2, 3072, 3072], P(None, None, 'tile'), may hold values from -0.0390625 to 0.0390625
- pair_rank: int32 [128, 128], P(None, 'tile'), may hold values from 2 to 24
- far_link: int32 [128, 128], P(None, 'tile'), may hold values 0 or 1
- focal_kernel: bfloat16 [2, 512, 65536], P(None, None, 'tile'), may hold values from -0.015625 to 0.015625
- focal_target: float32 [512], replicated, may hold values from 0.3 to 0.9
- focal_owner: int32 [512], replicated, may hold values from 0 to 511, each once
Outputs:
- field: float32 [2, 512, 65536], P(None, 'src', 'tile')
- focal_residual: float32 [512], P('tile')
- adjoint: float32 [2, 512, 65536], P(None, 'src', 'tile')
The draws below stay inside these ranges and needn't reach their ends.
Inputs may be any that keep to these rules, and one draw needn't show every extreme that they name: `focal_owner`: each focal point has its own slot; slot k belongs to index k // 8 of tile.
All inputs are finite; a program needn't handle non-finite values. No bound on the sum of `far_link` on one device may be relied on, other than what follows from the above.
Results may differ from the reference program's by a relative error of at most 0.006.
Values may be sent and summed in bfloat16 or wider, within the bound.
A program may use at most 64 MiB of HBM per device.

```python
import jax
import jax.numpy as jnp

TILE = 512
RANK = 24
TILES = 128
UNK = 65536
SOURCES = 512
FOCAL = 512


def plant(result, stream_key, low, top_value):
    spot = [jax.random.randint(jax.random.fold_in(stream_key, axis), (), 0, length) for axis, length in enumerate(result.shape)]
    widest = result.shape.index(max(result.shape))
    next_to = spot[:widest] + [(spot[widest] + 1) % result.shape[widest]] + spot[widest + 1:]
    return result.at[tuple(spot)].set(low).at[tuple(next_to)].set(top_value)


def steps_of(own_key, shape, shards, least, high):
    def one(position, shards_of):
        steps = jax.random.uniform(jax.random.fold_in(jax.random.fold_in(own_key, 6), position), (shards_of,), jnp.float32, least / len(shards), high / len(shards))
        return jnp.repeat(jnp.exp(steps), shape[position] // shards_of).reshape((-1,) + (1,) * (len(shape) - position - 1))

    gain = one(*shards[0])
    for cut in shards[1:]:
        gain = gain * one(*cut)
    return gain


def gaussian(rng, shape, deviation, limit, shards=(), kind=jnp.bfloat16):
    result = deviation * jax.random.normal(rng, shape, jnp.float32)
    if shards:
        result = result * steps_of(rng, shape, shards, -0.22, 0.18)
    return jnp.clip(result, -limit, limit).astype(kind)


def setup_inputs(seed: int = 0) -> dict:
    streams_of = jax.random.split(jax.random.key(seed), 11)
    return {
        "excitation": gaussian(streams_of[0], (2, SOURCES, UNK), 1.0, 6.0, ((1, 4), (2, 64))),
        "near_blocks": gaussian(streams_of[1], (TILES, 3, 2, TILE, TILE), (96 * TILE) ** -0.5, 0.02734375, ((0, 64),)),
        "source_basis": gaussian(streams_of[2], (TILES, 2, RANK, TILE), (2 * TILE) ** -0.5, 0.1875, ((0, 64),)),
        "target_basis": gaussian(streams_of[3], (TILES, 2, RANK, TILE), (4 * RANK) ** -0.5, 0.625, ((0, 64),)),
        "coupling": gaussian(streams_of[4], (2, TILES * RANK, TILES * RANK), (8 * TILES * RANK) ** -0.5, 0.0390625, ((2, 64),)),
        "pair_rank": plant(jax.random.randint(streams_of[5], (TILES, TILES), 2, RANK + 1), jax.random.fold_in(streams_of[5], 1), 2, RANK).astype(jnp.int32),
        "far_link": plant((jax.random.randint(streams_of[6], (TILES, TILES), 0, 4) < 3).astype(jnp.int32), jax.random.fold_in(streams_of[6], 1), 0, 1),
        "focal_kernel": gaussian(streams_of[7], (2, FOCAL, UNK), (2 * UNK) ** -0.5, 0.015625, ((2, 64),)),
        "focal_target": jnp.clip(jax.random.uniform(streams_of[8], (FOCAL,), jnp.float32, 0.3, 0.9), 0.3, 0.9),
        "focal_owner": jax.random.permutation(streams_of[9], FOCAL).astype(jnp.int32),
    }


DAMPING = 0.8


def complex_einsum(formula, left, right):
    left = left.astype(jnp.float32)
    right = right.astype(jnp.float32)
    real_part = jnp.einsum(formula, left[0], right[0]) - jnp.einsum(formula, left[1], right[1])
    imag_part = jnp.einsum(formula, left[0], right[1]) + jnp.einsum(formula, left[1], right[0])
    return jnp.stack([real_part, imag_part])


def masked_coupling(coupling, pair_rank, far_link):
    tiles = pair_rank.shape[0]
    source_tiles = jnp.arange(tiles)[:, None]
    target_tiles = jnp.arange(tiles)[None, :]
    distance = (target_tiles - source_tiles) % tiles
    far_pairs = (far_link == 1) & (distance != 0) & (distance != 1) & (distance != tiles - 1)
    levels = jnp.arange(RANK)
    rank_limit = pair_rank[:, None, :, None]
    rank_mask = far_pairs[:, None, :, None] & (levels[None, :, None, None] < rank_limit) & (levels[None, None, None, :] < rank_limit)
    rank_mask = rank_mask.reshape(tiles * RANK, tiles * RANK)
    return coupling * rank_mask.astype(coupling.dtype)


def apply_forward(field, near_blocks, source_basis, target_basis, masked):
    rows = field.shape[1]
    field_bf = field.astype(jnp.bfloat16).reshape(2, rows, TILES, TILE)
    near_part = jnp.zeros((2, rows, TILES, TILE), jnp.float32)
    for offset in range(3):
        shifted = jnp.roll(field_bf, -(offset - 1), axis=2)
        blocks = jnp.moveaxis(near_blocks[:, offset], 1, 0)
        near_part = near_part + complex_einsum('stn,tnm->stm', shifted, blocks)
    source_moved = jnp.moveaxis(source_basis, 1, 0)
    target_moved = jnp.moveaxis(target_basis, 1, 0)
    coeff = complex_einsum('stn,trn->str', field_bf, source_moved).astype(jnp.bfloat16).reshape(2, rows, TILES * RANK)
    coupled = complex_einsum('sj,ji->si', coeff, masked).astype(jnp.bfloat16).reshape(2, rows, TILES, RANK)
    far_part = complex_einsum('str,trn->stn', coupled, target_moved)
    return field + (near_part + far_part).reshape(2, rows, TILES * TILE)


def apply_transpose(field, near_blocks, source_basis, target_basis, masked):
    rows = field.shape[1]
    field_bf = field.astype(jnp.bfloat16).reshape(2, rows, TILES, TILE)
    near_part = jnp.zeros((2, rows, TILES, TILE), jnp.float32)
    for offset in range(3):
        blocks = jnp.moveaxis(near_blocks[:, offset], 1, 0)
        moved = complex_einsum('sto,tio->sti', field_bf, blocks)
        near_part = near_part + jnp.roll(moved, offset - 1, axis=2)
    source_moved = jnp.moveaxis(source_basis, 1, 0)
    target_moved = jnp.moveaxis(target_basis, 1, 0)
    projected = complex_einsum('stn,trn->str', field_bf, target_moved).astype(jnp.bfloat16).reshape(2, rows, TILES * RANK)
    summed_back = complex_einsum('si,ji->sj', projected, masked).astype(jnp.bfloat16).reshape(2, rows, TILES, RANK)
    far_part = complex_einsum('str,trn->stn', summed_back, source_moved)
    return field + (near_part + far_part).reshape(2, rows, TILES * TILE)


def reference(excitation, near_blocks, source_basis, target_basis, coupling, pair_rank, far_link, focal_kernel, focal_target, focal_owner):
    masked = masked_coupling(coupling, pair_rank, far_link)
    right_side = excitation.astype(jnp.float32)
    field = right_side
    for update in range(2):
        field = field + DAMPING * (right_side - apply_forward(field, near_blocks, source_basis, target_basis, masked))
    focal = complex_einsum('sn,fn->sf', field.astype(jnp.bfloat16), focal_kernel)
    intensity = jnp.sum(focal[0] * focal[0] + focal[1] * focal[1], axis=0)
    sources = focal.shape[1]
    residual_part = jnp.tanh(intensity / (2.0 * sources)) - focal_target
    weights = jnp.stack([residual_part * focal[0], -residual_part * focal[1]]).astype(jnp.bfloat16)
    scale_factor = (TILES * TILE / FOCAL) ** 0.5
    source_term = complex_einsum('sf,fn->sn', weights, focal_kernel) * scale_factor
    adjoint = source_term + DAMPING * (source_term - apply_transpose(source_term, near_blocks, source_basis, target_basis, masked))
    focal_residual = jnp.zeros((FOCAL,), jnp.float32).at[focal_owner].set(residual_part)
    return field, focal_residual, adjoint
```

```python
import functools

import jax
import jax.numpy as jnp
from jax import lax
from jax.experimental import pallas as pl
from jax.experimental.pallas import tpu as pltpu
from jax.sharding import PartitionSpec as P

TILE = 512
RANK = 24
PAIR = 2 * RANK
ROWS = 128
DAMPING = 0.8
HALF = 256
F32 = jnp.float32
BF16 = jnp.bfloat16


def dot(left, right):
    return lax.dot_general(left, right, (((1,), (0,)), ((), ())), preferred_element_type=F32)


def dot_nt(left, right):
    return lax.dot_general(left, right, (((1,), (1,)), ((), ())), preferred_element_type=F32)


def rows_joined(by_re, by_im):
    return jnp.concatenate(
        [by_re[:ROWS] - by_im[ROWS:], by_re[ROWS:] + by_im[:ROWS]], axis=0
    )


def lanes_joined(by_re, by_im):
    return jnp.concatenate(
        [by_re[:, :ROWS] - by_im[:, ROWS:], by_re[:, ROWS:] + by_im[:, :ROWS]], axis=1
    )


def aligned(start, size, unit):
    return pl.ds(pl.multiple_of(start, unit), size)


def kernel(
    nz,
    nq,
    ns,
    exc,
    near_hbm,
    sbasis,
    tbasis,
    coup,
    rank,
    link,
    fk_hbm,
    target,
    owner,
    field_out,
    res_out,
    adj_out,
    near,
    fk,
    vb,
    halo,
    nacc,
    mt_send,
    mt,
    mback,
    gath,
    part,
    parts_in,
    fsend,
    fparts,
    fz,
    fzparts,
    isum,
    iparts,
    wz,
    wg,
    wt,
    rrow,
    rgath,
    edge_send,
    edge_in,
    local_sem,
    s_halo,
    r_halo,
    s_mt,
    r_mt,
    s_gath,
    r_gath,
    s_part,
    r_part,
    s_f,
    r_f,
    s_fz,
    r_fz,
    s_i,
    r_i,
    s_w,
    r_w,
    s_wg,
    r_wg,
    s_rr,
    r_rr,
    s_edge,
    r_edge,
):
    t = lax.axis_index("tile")
    s = lax.axis_index("src")
    nt = nz * nq
    q = t // nz
    z = t - q * nz
    tiles = 2 * nt
    group = nz * PAIR
    spread = nq * PAIR
    fgroup = nz * 8
    focal_count = nt * 8

    def z_peer(d):
        return q * nz + lax.rem(z + d, nz)

    def q_peer(d):
        return lax.rem(q + d, nq) * nz + z

    left = lax.rem(t + nt - 1, nt)
    right = lax.rem(t + 1, nt)

    barrier = pltpu.get_barrier_semaphore()
    count = 0
    for d in range(1, nz):
        pl.semaphore_signal(barrier, inc=1, device_id={"tile": z_peer(d), "src": s})
        count += 1
    for d in range(1, nq):
        pl.semaphore_signal(barrier, inc=1, device_id={"tile": q_peer(d), "src": s})
        count += 1
    for other in (left, right):
        pl.semaphore_signal(barrier, inc=1, device_id={"tile": other, "src": s})
        count += 1
    for d in range(1, ns):
        pl.semaphore_signal(barrier, inc=1, device_id={"tile": t, "src": lax.rem(s + d, ns)})
        count += 1

    near_copy = pltpu.make_async_copy(near_hbm, near, local_sem.at[0])
    near_copy.start()
    fk_copy = pltpu.make_async_copy(fk_hbm, fk, local_sem.at[1])
    fk_copy.start()

    pending = []

    def send(src_ref, dst_ref, send_sem, recv_sem, tile=None, src=None):
        copy = pltpu.make_async_remote_copy(
            src_ref=src_ref,
            dst_ref=dst_ref,
            send_sem=send_sem,
            recv_sem=recv_sem,
            device_id={"tile": t if tile is None else tile, "src": s if src is None else src},
        )
        copy.start()
        pending.append(copy)

    def arrived(ref, send_sem, recv_sem):
        pltpu.make_async_remote_copy(
            src_ref=ref,
            dst_ref=ref,
            send_sem=send_sem,
            recv_sem=recv_sem,
            device_id={"tile": right, "src": s},
        ).wait_recv()

    def far_order(n):
        return sorted(range(1, n), key=lambda d: -min(d, n - d))

    def own_slice(index):
        return aligned(index * PAIR, PAIR, 16)

    def projected(x, basis):
        pieces = []
        for l in range(2):
            both = dot_nt(basis[l], x[:, l * TILE : (l + 1) * TILE])
            pieces.append(lanes_joined(both[:RANK], both[RANK:]))
        return jnp.concatenate(pieces, axis=0).astype(BF16)

    def gather(stage, value, along_z):
        n, mine = (nz, z) if along_z else (nq, q)
        here = gath.at[stage, own_slice(mine)]
        gath[stage, own_slice(mine), :] = value
        for d in far_order(n):
            send(
                here,
                here,
                s_gath.at[stage, d],
                r_gath.at[stage, d],
                tile=z_peer(d) if along_z else q_peer(d),
            )

    def gathered(stage, along_z):
        n, mine = (nz, z) if along_z else (nq, q)
        for d in range(1, n):
            sender = lax.rem(mine + n - d, n)
            arrived(
                gath.at[stage, own_slice(sender)], s_gath.at[stage, d], r_gath.at[stage, d]
            )

    def scatter(stage, value, along_z):
        n, mine = (nz, z) if along_z else (nq, q)
        part[stage] = value.astype(BF16)
        for d in far_order(n):
            owner_of = lax.rem(mine + d, n)
            send(
                part.at[stage, own_slice(owner_of)],
                parts_in.at[stage, d],
                s_part.at[stage, d],
                r_part.at[stage, d],
                tile=z_peer(d) if along_z else q_peer(d),
            )

    def scattered(stage, along_z):
        n, mine = (nz, z) if along_z else (nq, q)
        total = part[stage, own_slice(mine), :].astype(F32)
        for d in range(1, n):
            arrived(parts_in.at[stage, d], s_part.at[stage, d], r_part.at[stage, d])
            total = total + parts_in[stage, d].astype(F32)
        return total.astype(BF16).astype(F32)

    def expanded(coefficients, basis, l):
        piece = coefficients[l * RANK : (l + 1) * RANK]
        turned = jnp.concatenate([-piece[:, ROWS:], piece[:, :ROWS]], axis=1)
        stacked = jnp.concatenate([piece, turned], axis=0)
        return dot(jnp.transpose(stacked).astype(BF16), basis[l])

    def send_halo(stage):
        send(
            vb.at[stage, :, TILE : 2 * TILE],
            halo.at[stage, 0],
            s_halo.at[stage, 0],
            r_halo.at[stage, 0],
            tile=right,
        )
        send(
            vb.at[stage, :, 0:TILE],
            halo.at[stage, 1],
            s_halo.at[stage, 1],
            r_halo.at[stage, 1],
            tile=left,
        )

    vb[0] = exc[...]
    first_coeff = projected(exc[...], sbasis)

    level = lax.broadcasted_iota(jnp.int32, (RANK, tiles), 0)
    source_tile = lax.broadcasted_iota(jnp.int32, (1, tiles), 1)
    limits = []
    for l in range(2):
        gap = t * 2 + l - source_tile
        is_near = (
            (gap == 0)
            | (gap == 1)
            | (gap == -1)
            | (gap == tiles - 1)
            | (gap == 1 - tiles)
        )
        here = jnp.where((link[l : l + 1, :] == 1) & ~is_near, rank[l : l + 1, :], 0)
        wide = jnp.broadcast_to(here, (RANK, tiles))
        limits.append(jnp.where(level < wide, wide, 0).astype(F32))
    limits.append(
        jnp.broadcast_to(source_tile, (16, tiles)).astype(F32)
    )
    limit_rows = jnp.concatenate(limits, axis=0).astype(BF16)

    pl.semaphore_wait(barrier, count)

    gather(0, first_coeff, True)
    send_halo(0)

    tile_row = lax.broadcasted_iota(jnp.int32, (tiles, group), 0)
    lane = lax.broadcasted_iota(jnp.int32, (tiles, group), 1)
    lane_row = lax.broadcasted_iota(jnp.int32, (1, group), 1)
    for d in far_order(nq) + [0]:
        to = lax.rem(q + d, nq)
        offset = lane - (tile_row - to * (2 * nz)) * RANK
        pick = jnp.where((offset >= 0) & (offset < RANK), 1.0, 0.0).astype(BF16)
        limit = dot(limit_rows, pick)
        position = (lane_row + to * group).astype(F32) - limit[PAIR : PAIR + 1, :] * float(RANK)
        keep = position < limit[:PAIR]
        for c in range(2):
            block = coup[c, :, aligned(to * group, group, 128)]
            block = jnp.where(keep, block.astype(F32), 0.0).astype(BF16)
            if d == 0:
                mt[c, own_slice(q), :] = block
            else:
                mt_send[d, c] = block
        if d != 0:
            send(
                mt_send.at[d],
                mt.at[:, own_slice(q), :],
                s_mt.at[d],
                r_mt.at[d],
                tile=q_peer(d),
            )

    def near_own(stage):
        @pl.loop(0, 4)
        def _(step):
            i = step // 2
            cols = aligned((step % 2) * HALF, HALF, HALF)
            by_re = jnp.zeros((2 * ROWS, HALF), F32)
            by_im = jnp.zeros((2 * ROWS, HALF), F32)
            for l in range(2):
                x = vb[stage, :, l * TILE : (l + 1) * TILE]
                by_re = by_re + dot(x, near[i, l - i + 1, 0, :, cols])
                by_im = by_im + dot(x, near[i, l - i + 1, 1, :, cols])
            nacc[:, aligned(step * HALF, HALF, HALF)] = rows_joined(by_re, by_im)

    def near_halo(stage):
        @pl.loop(0, 4)
        def _(step):
            i = step // 2
            cols = aligned((step % 2) * HALF, HALF, HALF)
            x = halo[stage, i]
            by_re = dot(x, near[i, 2 * i, 0, :, cols])
            by_im = dot(x, near[i, 2 * i, 1, :, cols])
            out = aligned(step * HALF, HALF, HALF)
            nacc[:, out] = nacc[:, out] + rows_joined(by_re, by_im)

    near_copy.wait()
    for stage in range(2):
        if stage == 1:
            gather(1, projected(vb[1], sbasis), True)
            send_halo(1)
        near_own(stage)
        gathered(stage, True)
        if stage == 0:
            for d in range(1, nq):
                sender = lax.rem(q + nq - d, nq)
                arrived(mt.at[:, own_slice(sender), :], s_mt.at[d], r_mt.at[d])
        coefficients = gath[stage, :group, :]
        scatter(
            stage,
            lanes_joined(dot(mt[0], coefficients), dot(mt[1], coefficients)),
            False,
        )
        for side in range(2):
            arrived(halo.at[stage, side], s_halo.at[stage, side], r_halo.at[stage, side])
        near_halo(stage)
        if stage == 0:
            for c in range(2):
                mback[c] = jnp.transpose(mt[c].astype(F32)).astype(BF16)
        coupled = scattered(stage, False)
        for l in range(2):
            cols = slice(l * TILE, (l + 1) * TILE)
            added = nacc[:, cols] + expanded(coupled, tbasis, l)
            right_side = exc[:, cols].astype(F32)
            if stage == 0:
                value = right_side - DAMPING * added
            else:
                before = field_out[:, cols]
                value = before + DAMPING * (right_side - (before + added))
            field_out[:, cols] = value
            vb[stage + 1, :, cols] = value.astype(BF16)

    fk_copy.wait()
    x = vb[2]
    fsend[...] = lanes_joined(dot_nt(fk[0], x), dot_nt(fk[1], x))

    def f_rows(index):
        return aligned(index * fgroup, fgroup, 8)

    for d in far_order(nq):
        send(
            fsend.at[f_rows(lax.rem(q + d, nq))],
            fparts.at[d],
            s_f.at[d],
            r_f.at[d],
            tile=q_peer(d),
        )
    total = fsend[f_rows(q), :]
    for d in range(1, nq):
        arrived(fparts.at[d], s_f.at[d], r_f.at[d])
        total = total + fparts[d]
    fz[...] = total

    def z_rows(index):
        return aligned(index * 8, 8, 8)

    for d in far_order(nz):
        send(
            fz.at[z_rows(lax.rem(z + d, nz))],
            fzparts.at[d],
            s_fz.at[d],
            r_fz.at[d],
            tile=z_peer(d),
        )
    focal = fz[z_rows(z), :]
    for d in range(1, nz):
        arrived(fzparts.at[d], s_fz.at[d], r_fz.at[d])
        focal = focal + fzparts[d]
    square = focal * focal
    strength = jnp.sum(square[:, :ROWS] + square[:, ROWS:], axis=1, keepdims=True)
    isum[...] = jnp.broadcast_to(strength, (8, 128))
    for d in range(1, ns):
        send(isum, iparts.at[d], s_i.at[d], r_i.at[d], src=lax.rem(s + d, ns))
    slot = lax.broadcasted_iota(jnp.int32, (8, focal_count), 0)
    spot = lax.broadcasted_iota(jnp.int32, (8, focal_count), 1)
    wanted = jnp.sum(
        jnp.where(spot == slot + t * 8, jnp.broadcast_to(target[...], (8, focal_count)), 0.0),
        axis=1,
        keepdims=True,
    )
    strength = isum[...]
    for d in range(1, ns):
        arrived(iparts.at[d], s_i.at[d], r_i.at[d])
        strength = strength + iparts[d]
    residual = jnp.tanh(strength / (2.0 * ROWS * ns)) - wanted
    wz[z_rows(z), :] = jnp.concatenate(
        [residual * focal[:, :ROWS], -residual * focal[:, ROWS:], residual], axis=1
    )
    for d in far_order(nz):
        here = wz.at[z_rows(z)]
        send(here, here, s_w.at[d], r_w.at[d], tile=z_peer(d))
    for d in range(1, nz):
        sender = lax.rem(z + nz - d, nz)
        arrived(wz.at[z_rows(sender)], s_w.at[d], r_w.at[d])
    f16 = aligned(q * fgroup, fgroup, 16)
    wg[f16, :] = wz[:, : 2 * ROWS].astype(BF16)
    for d in far_order(nq):
        here = wg.at[f16]
        send(here, here, s_wg.at[d], r_wg.at[d], tile=q_peer(d))
    row = lax.broadcasted_iota(jnp.int32, (fgroup, 128), 0)
    lane128 = lax.broadcasted_iota(jnp.int32, (fgroup, 128), 1)
    shift = lax.rem(q * fgroup, 128)
    flat = jnp.sum(
        jnp.where(lane128 == row + shift, wz[:, 2 * ROWS :], 0.0), axis=0, keepdims=True
    )
    rrow[...] = jnp.broadcast_to(flat, (8, 128))
    rgath[q] = jnp.broadcast_to(flat, (8, 128))
    for d in far_order(nq):
        send(rrow, rgath.at[q], s_rr.at[d], r_rr.at[d], tile=q_peer(d))
    for d in range(1, nq):
        sender = lax.rem(q + nq - d, nq)
        arrived(wg.at[aligned(sender * fgroup, fgroup, 16)], s_wg.at[d], r_wg.at[d])
    wt[...] = jnp.transpose(wg[...].astype(F32)).astype(BF16)

    scale = float(tiles * TILE / focal_count) ** 0.5

    @pl.loop(0, 4)
    def _(step):
        cols = aligned(step * HALF, HALF, HALF)
        w = wt[...]
        u = rows_joined(dot(w, fk[0, :, cols]), dot(w, fk[1, :, cols])) * scale
        adj_out[:, cols] = u
        vb[3, :, cols] = u.astype(BF16)

    gather(2, projected(vb[3], tbasis), False)

    @pl.loop(0, 4)
    def _(step):
        i = step // 2
        half = aligned((step % 2) * HALF, HALF, HALF)
        x = vb[3, :, aligned(i * TILE, TILE, TILE)]
        by_re = dot_nt(x, near[i, 2 * i, 0, half, :])
        by_im = dot_nt(x, near[i, 2 * i, 1, half, :])
        edge_send[i, :, half] = rows_joined(by_re, by_im).astype(BF16)

    send(edge_send.at[0], edge_in.at[1], s_edge.at[0], r_edge.at[1], tile=left)
    send(edge_send.at[1], edge_in.at[0], s_edge.at[1], r_edge.at[0], tile=right)

    gathered(2, False)
    coefficients = gath[2, :spread, :]
    scatter(
        2,
        lanes_joined(dot(mback[0], coefficients), dot(mback[1], coefficients)),
        True,
    )

    @pl.loop(0, 4)
    def _(step):
        m = step // 2
        half = aligned((step % 2) * HALF, HALF, HALF)
        by_re = jnp.zeros((2 * ROWS, HALF), F32)
        by_im = jnp.zeros((2 * ROWS, HALF), F32)
        for i in range(2):
            x = vb[3, :, i * TILE : (i + 1) * TILE]
            by_re = by_re + dot_nt(x, near[i, m - i + 1, 0, half, :])
            by_im = by_im + dot_nt(x, near[i, m - i + 1, 1, half, :])
        nacc[:, aligned(step * HALF, HALF, HALF)] = rows_joined(by_re, by_im)

    back = scattered(2, True)
    for side in range(2):
        arrived(edge_in.at[side], s_edge.at[side], r_edge.at[side])
    for l in range(2):
        cols = slice(l * TILE, (l + 1) * TILE)
        added = nacc[:, cols] + edge_in[l].astype(F32) + expanded(back, sbasis, l)
        adj_out[:, cols] = adj_out[:, cols] - DAMPING * added

    lines = (focal_count + 127) // 128
    for d in range(1, nq):
        sender = lax.rem(q + nq - d, nq)
        arrived(rgath.at[sender], s_rr.at[d], r_rr.at[d])
    mine = lax.broadcasted_iota(jnp.int32, (8, 128), 0) + t * 8
    found = jnp.zeros((8, 128), F32)
    for line in range(lines):
        values = jnp.zeros((8, 128), F32)
        for other in range(nq):
            if other * fgroup // 128 == line:
                values = values + rgath[other]
        owners = jnp.broadcast_to(owner[line : line + 1, :], (8, 128))
        found = found + jnp.where(owners == mine, values, 0.0)
    res_out[...] = jnp.broadcast_to(jnp.sum(found, axis=1, keepdims=True), (8, 128))

    for copy in pending:
        copy.wait_send()


def per_device(
    nz,
    excitation,
    near_blocks,
    source_basis,
    target_basis,
    coupling,
    pair_rank,
    far_link,
    focal_kernel,
    focal_target,
    focal_owner,
):
    nt = lax.axis_size("tile")
    ns = lax.axis_size("src")
    nq = nt // nz
    focal_count = focal_target.shape[0]
    group = nz * PAIR
    spread = nq * PAIR
    fgroup = nz * 8
    width = 2 * TILE
    most = max(nz, nq)
    lines = (focal_count + 127) // 128
    owner = jnp.pad(focal_owner, (0, lines * 128 - focal_count), constant_values=-1)
    vmem = pl.BlockSpec(memory_space=pltpu.VMEM)
    anywhere = pl.BlockSpec(memory_space=pl.ANY)
    dma = pltpu.SemaphoreType.DMA
    both = 2 * ROWS
    field, residual, adjoint = pl.pallas_call(
        functools.partial(kernel, nz, nq, ns),
        out_shape=(
            jax.ShapeDtypeStruct((both, width), F32),
            jax.ShapeDtypeStruct((8, 128), F32),
            jax.ShapeDtypeStruct((both, width), F32),
        ),
        in_specs=[vmem, anywhere, vmem, vmem, vmem, vmem, vmem, anywhere, vmem, vmem],
        out_specs=(vmem, vmem, vmem),
        scratch_shapes=[
            pltpu.VMEM((2, 3, 2, TILE, TILE), BF16),
            pltpu.VMEM((2, focal_count, width), BF16),
            pltpu.VMEM((4, both, width), BF16),
            pltpu.VMEM((2, 2, both, TILE), BF16),
            pltpu.VMEM((both, width), F32),
            pltpu.VMEM((nq, 2, PAIR, group), BF16),
            pltpu.VMEM((2, spread, group), BF16),
            pltpu.VMEM((2, group, spread), BF16),
            pltpu.VMEM((3, most * PAIR, both), BF16),
            pltpu.VMEM((3, most * PAIR, both), BF16),
            pltpu.VMEM((3, most, PAIR, both), BF16),
            pltpu.VMEM((focal_count, both), F32),
            pltpu.VMEM((nq, fgroup, both), F32),
            pltpu.VMEM((fgroup, both), F32),
            pltpu.VMEM((nz, 8, both), F32),
            pltpu.VMEM((8, 128), F32),
            pltpu.VMEM((ns, 8, 128), F32),
            pltpu.VMEM((fgroup, 3 * ROWS), F32),
            pltpu.VMEM((focal_count, both), BF16),
            pltpu.VMEM((both, focal_count), BF16),
            pltpu.VMEM((8, 128), F32),
            pltpu.VMEM((nq, 8, 128), F32),
            pltpu.VMEM((2, both, TILE), BF16),
            pltpu.VMEM((2, both, TILE), BF16),
            dma((2,)),
            dma((2, 2)),
            dma((2, 2)),
            dma((nq,)),
            dma((nq,)),
            dma((3, most)),
            dma((3, most)),
            dma((3, most)),
            dma((3, most)),
            dma((nq,)),
            dma((nq,)),
            dma((nz,)),
            dma((nz,)),
            dma((ns,)),
            dma((ns,)),
            dma((nz,)),
            dma((nz,)),
            dma((nq,)),
            dma((nq,)),
            dma((nq,)),
            dma((nq,)),
            dma((2,)),
            dma((2,)),
        ],
        compiler_params=pltpu.CompilerParams(
            collective_id=0, has_side_effects=True, vmem_limit_bytes=48 * 1024 * 1024
        ),
    )(
        excitation.reshape(both, width),
        near_blocks,
        source_basis.reshape(2, PAIR, TILE),
        target_basis.reshape(2, PAIR, TILE),
        jnp.swapaxes(coupling, 1, 2),
        pair_rank.T,
        far_link.T,
        focal_kernel,
        focal_target.reshape(1, focal_count),
        owner.reshape(lines, 128),
    )
    return (
        field.reshape(2, ROWS, width),
        residual[:, 0],
        adjoint.reshape(2, ROWS, width),
    )


def solution(mesh):
    nt = mesh.shape["tile"]
    nz = 8 if nt % 8 == 0 and nt > 8 else 2
    return jax.shard_map(
        functools.partial(per_device, nz),
        mesh=mesh,
        in_specs=(
            P(None, "src", "tile"),
            P("tile", None, None, None, None),
            P("tile", None, None, None),
            P("tile", None, None, None),
            P(None, None, "tile"),
            P(None, "tile"),
            P(None, "tile"),
            P(None, None, "tile"),
            P(),
            P(),
        ),
        out_specs=(P(None, "src", "tile"), P("tile"), P(None, "src", "tile")),
        check_vma=False,
    )
```

```python
import functools

import jax
import jax.numpy as jnp
from jax import lax
from jax.experimental import pallas as pl
from jax.experimental.pallas import tpu as pltpu
from jax.sharding import PartitionSpec as P

TILE = 512
RANK = 24
PAIR = 2 * RANK
ROWS = 128
DAMPING = 0.8
HALF = 256
F32 = jnp.float32
BF16 = jnp.bfloat16


def dot(left, right):
    return lax.dot_general(left, right, (((1,), (0,)), ((), ())), preferred_element_type=F32)


def dot_nt(left, right):
    return lax.dot_general(left, right, (((1,), (1,)), ((), ())), preferred_element_type=F32)


def rows_joined(by_re, by_im):
    return jnp.concatenate(
        [by_re[:ROWS] - by_im[ROWS:], by_re[ROWS:] + by_im[:ROWS]], axis=0
    )


def lanes_joined(by_re, by_im):
    return jnp.concatenate(
        [by_re[:, :ROWS] - by_im[:, ROWS:], by_re[:, ROWS:] + by_im[:, :ROWS]], axis=1
    )


def aligned(start, size, unit):
    return pl.ds(pl.multiple_of(start, unit), size)


def kernel(
    nz,
    nq,
    ns,
    exc_hbm,
    near_hbm,
    sbasis_hbm,
    tbasis_hbm,
    coup_hbm,
    rank_hbm,
    link_hbm,
    fk_hbm,
    target_hbm,
    owner_hbm,
    field_out,
    res_out,
    adj_out,
    field,
    adjoint,
    near,
    fk,
    sbasis,
    tbasis,
    coup,
    rank,
    link,
    target,
    owner,
    vb,
    halo,
    nacc,
    mt_send,
    mt,
    mback,
    gath,
    part,
    parts_in,
    fsend,
    fparts,
    fz,
    fzparts,
    isum,
    iparts,
    fall,
    wg,
    wt,
    rrow,
    rgath,
    edge_send,
    edge_in,
    local_sem,
    s_halo,
    r_halo,
    s_mt,
    r_mt,
    s_gath,
    r_gath,
    s_part,
    r_part,
    s_f,
    r_f,
    s_fz,
    r_fz,
    s_i,
    r_i,
    s_w,
    r_w,
    s_sib,
    r_sib,
    s_wg,
    r_wg,
    s_rr,
    r_rr,
    s_edge,
    r_edge,
):
    t = lax.axis_index("tile")
    s = lax.axis_index("src")
    nt = nz * nq
    q = t // nz
    z = t - q * nz
    tiles = 2 * nt
    group = nz * PAIR
    spread = nq * PAIR
    fgroup = nz * 8
    focal_count = nt * 8

    def z_peer(d):
        return q * nz + lax.rem(z + d, nz)

    def q_peer(d):
        return lax.rem(q + d, nq) * nz + z

    left = lax.rem(t + nt - 1, nt)
    right = lax.rem(t + 1, nt)

    barrier = pltpu.get_barrier_semaphore()
    count = 0
    for d in range(1, nq):
        pl.semaphore_signal(barrier, inc=1, device_id={"tile": q_peer(d), "src": s})
        count += 1
    for other in (left, right):
        pl.semaphore_signal(barrier, inc=1, device_id={"tile": other, "src": s})
        count += 1
    for e in range(ns):
        for d in range(nz):
            if d or e:
                pl.semaphore_signal(
                    barrier,
                    inc=1,
                    device_id={"tile": z_peer(d), "src": lax.rem(s + e, ns)},
                )
                count += 1
    core = lax.rem(s, 2)
    sibling = s + 1 - 2 * core

    loads = {}
    for k, (name, source, place) in enumerate(
        (
            ("exc", exc_hbm, vb.at[0]),
            ("sbasis", sbasis_hbm, sbasis),
            ("rank", rank_hbm, rank),
            ("link", link_hbm, link),
            ("coup", coup_hbm, coup),
            ("near", near_hbm, near),
            ("tbasis", tbasis_hbm, tbasis),
            ("fk", fk_hbm, fk),
            ("target", target_hbm, target),
            ("owner", owner_hbm, owner),
        )
    ):
        loads[name] = pltpu.make_async_copy(source, place, local_sem.at[k])
        loads[name].start()

    pending = []

    def send(src_ref, dst_ref, send_sem, recv_sem, tile=None, src=None):
        copy = pltpu.make_async_remote_copy(
            src_ref=src_ref,
            dst_ref=dst_ref,
            send_sem=send_sem,
            recv_sem=recv_sem,
            device_id={"tile": t if tile is None else tile, "src": s if src is None else src},
        )
        copy.start()
        pending.append(copy)

    def arrived(ref, send_sem, recv_sem):
        pltpu.make_async_remote_copy(
            src_ref=ref,
            dst_ref=ref,
            send_sem=send_sem,
            recv_sem=recv_sem,
            device_id={"tile": right, "src": s},
        ).wait_recv()

    def far_order(n):
        return sorted(range(1, n), key=lambda d: -min(d, n - d))

    def own_slice(index):
        return aligned(index * PAIR, PAIR, 16)

    def projected(x, basis):
        pieces = []
        for l in range(2):
            both = dot_nt(basis[l], x[:, l * TILE : (l + 1) * TILE])
            pieces.append(lanes_joined(both[:RANK], both[RANK:]))
        return jnp.concatenate(pieces, axis=0).astype(BF16)

    def gather(stage, value, along_z):
        n, mine = (nz, z) if along_z else (nq, q)
        here = gath.at[stage, own_slice(mine)]
        gath[stage, own_slice(mine), :] = value
        for d in far_order(n):
            send(
                here,
                here,
                s_gath.at[stage, d],
                r_gath.at[stage, d],
                tile=z_peer(d) if along_z else q_peer(d),
            )

    def gathered(stage, along_z):
        n, mine = (nz, z) if along_z else (nq, q)
        for d in range(1, n):
            sender = lax.rem(mine + n - d, n)
            arrived(
                gath.at[stage, own_slice(sender)], s_gath.at[stage, d], r_gath.at[stage, d]
            )

    def scatter(stage, value, along_z):
        n, mine = (nz, z) if along_z else (nq, q)
        part[stage] = value.astype(BF16)
        for d in far_order(n):
            owner_of = lax.rem(mine + d, n)
            send(
                part.at[stage, own_slice(owner_of)],
                parts_in.at[stage, d],
                s_part.at[stage, d],
                r_part.at[stage, d],
                tile=z_peer(d) if along_z else q_peer(d),
            )

    def scattered(stage, along_z):
        n, mine = (nz, z) if along_z else (nq, q)
        total = part[stage, own_slice(mine), :].astype(F32)
        for d in range(1, n):
            arrived(parts_in.at[stage, d], s_part.at[stage, d], r_part.at[stage, d])
            total = total + parts_in[stage, d].astype(F32)
        return total.astype(BF16).astype(F32)

    def expanded(coefficients, basis, l):
        piece = coefficients[l * RANK : (l + 1) * RANK]
        turned = jnp.concatenate([-piece[:, ROWS:], piece[:, :ROWS]], axis=1)
        stacked = jnp.concatenate([piece, turned], axis=0)
        return dot(jnp.transpose(stacked).astype(BF16), basis[l])

    def send_halo(stage):
        send(
            vb.at[stage, :, TILE : 2 * TILE],
            halo.at[stage, 0],
            s_halo.at[stage, 0],
            r_halo.at[stage, 0],
            tile=right,
        )
        send(
            vb.at[stage, :, 0:TILE],
            halo.at[stage, 1],
            s_halo.at[stage, 1],
            r_halo.at[stage, 1],
            tile=left,
        )

    loads["exc"].wait()
    loads["sbasis"].wait()
    first_coeff = projected(vb[0], sbasis)
    loads["rank"].wait()
    loads["link"].wait()

    level = lax.broadcasted_iota(jnp.int32, (RANK, tiles), 0)
    source_tile = lax.broadcasted_iota(jnp.int32, (1, tiles), 1)
    limits = []
    for l in range(2):
        gap = t * 2 + l - source_tile
        is_near = (
            (gap == 0)
            | (gap == 1)
            | (gap == -1)
            | (gap == tiles - 1)
            | (gap == 1 - tiles)
        )
        here = jnp.where((link[l : l + 1, :] == 1) & ~is_near, rank[l : l + 1, :], 0)
        wide = jnp.broadcast_to(here, (RANK, tiles))
        limits.append(jnp.where(level < wide, wide, 0).astype(F32))
    limits.append(
        jnp.broadcast_to(source_tile, (16, tiles)).astype(F32)
    )
    limit_rows = jnp.concatenate(limits, axis=0).astype(BF16)

    pl.semaphore_wait(barrier, count)

    gather(0, first_coeff, True)
    send_halo(0)

    loads["coup"].wait()
    tile_row = lax.broadcasted_iota(jnp.int32, (tiles, group), 0)
    lane = lax.broadcasted_iota(jnp.int32, (tiles, group), 1)
    lane_row = lax.broadcasted_iota(jnp.int32, (1, group), 1)
    for d in far_order(nq) + [0]:
        to = lax.rem(q + d, nq)
        offset = lane - (tile_row - to * (2 * nz)) * RANK
        pick = jnp.where((offset >= 0) & (offset < RANK), 1.0, 0.0).astype(BF16)
        limit = dot(limit_rows, pick)
        position = (lane_row + to * group).astype(F32) - limit[PAIR : PAIR + 1, :] * float(RANK)
        keep = position < limit[:PAIR]
        for c in range(2) if d == 0 else (core,):
            block = coup[c, :, aligned(to * group, group, 128)]
            block = jnp.where(keep, block.astype(F32), 0.0).astype(BF16)
            if d == 0:
                mt[c, own_slice(q), :] = block
            else:
                mt_send[d] = block
        if d != 0:
            send(
                mt_send.at[d],
                mt.at[core, own_slice(q), :],
                s_mt.at[d],
                r_mt.at[d],
                tile=q_peer(d),
            )

    def near_own(stage):
        @pl.loop(0, 4)
        def _(step):
            i = step // 2
            cols = aligned((step % 2) * HALF, HALF, HALF)
            by_re = jnp.zeros((2 * ROWS, HALF), F32)
            by_im = jnp.zeros((2 * ROWS, HALF), F32)
            for l in range(2):
                x = vb[stage, :, l * TILE : (l + 1) * TILE]
                by_re = by_re + dot(x, near[i, l - i + 1, 0, :, cols])
                by_im = by_im + dot(x, near[i, l - i + 1, 1, :, cols])
            nacc[:, aligned(step * HALF, HALF, HALF)] = rows_joined(by_re, by_im)

    def near_halo(stage):
        @pl.loop(0, 4)
        def _(step):
            i = step // 2
            cols = aligned((step % 2) * HALF, HALF, HALF)
            x = halo[stage, i]
            by_re = dot(x, near[i, 2 * i, 0, :, cols])
            by_im = dot(x, near[i, 2 * i, 1, :, cols])
            out = aligned(step * HALF, HALF, HALF)
            nacc[:, out] = nacc[:, out] + rows_joined(by_re, by_im)

    loads["near"].wait()
    for stage in range(2):
        if stage == 1:
            gather(1, projected(vb[1], sbasis), True)
            send_halo(1)
        near_own(stage)
        if stage == 0:
            for d in range(1, nq):
                here = mt.at[core, own_slice(lax.rem(q + nq - d, nq)), :]
                arrived(here, s_mt.at[d], r_mt.at[d])
                send(here, here, s_sib.at[d], r_sib.at[d], src=sibling)
        gathered(stage, True)
        if stage == 0:
            for d in range(1, nq):
                here = mt.at[1 - core, own_slice(lax.rem(q + nq - d, nq)), :]
                arrived(here, s_sib.at[d], r_sib.at[d])
        coefficients = gath[stage, :group, :]
        scatter(
            stage,
            lanes_joined(dot(mt[0], coefficients), dot(mt[1], coefficients)),
            False,
        )
        for side in range(2):
            arrived(halo.at[stage, side], s_halo.at[stage, side], r_halo.at[stage, side])
        near_halo(stage)
        if stage == 0:
            for c in range(2):
                mback[c] = jnp.transpose(mt[c].astype(F32)).astype(BF16)
            loads["tbasis"].wait()
        coupled = scattered(stage, False)
        for l in range(2):
            cols = slice(l * TILE, (l + 1) * TILE)
            added = nacc[:, cols] + expanded(coupled, tbasis, l)
            right_side = vb[0, :, cols].astype(F32)
            if stage == 0:
                value = right_side - DAMPING * added
            else:
                before = field[:, cols]
                value = before + DAMPING * (right_side - (before + added))
            field[:, cols] = value
            vb[stage + 1, :, cols] = value.astype(BF16)

    field_copy = pltpu.make_async_copy(field, field_out, local_sem.at[10])
    field_copy.start()

    loads["fk"].wait()
    x = vb[2]
    fsend[...] = lanes_joined(dot_nt(fk[0], x), dot_nt(fk[1], x)).astype(BF16)

    def f_rows(index):
        return aligned(index * fgroup, fgroup, 16)

    for d in far_order(nq):
        send(
            fsend.at[f_rows(lax.rem(q + d, nq))],
            fparts.at[d],
            s_f.at[d],
            r_f.at[d],
            tile=q_peer(d),
        )
    total = fsend[f_rows(q), :].astype(F32)
    for d in range(1, nq):
        arrived(fparts.at[d], s_f.at[d], r_f.at[d])
        total = total + fparts[d].astype(F32)
    fz[...] = total

    def z_rows(index):
        return aligned(index * 8, 8, 8)

    for d in far_order(nz):
        send(
            fz.at[z_rows(lax.rem(z + d, nz))],
            fzparts.at[d],
            s_fz.at[d],
            r_fz.at[d],
            tile=z_peer(d),
        )
    focal = fz[z_rows(z), :]
    for d in range(1, nz):
        arrived(fzparts.at[d], s_fz.at[d], r_fz.at[d])
        focal = focal + fzparts[d]
    square = focal * focal
    strength = jnp.sum(square[:, :ROWS] + square[:, ROWS:], axis=1, keepdims=True)
    isum[...] = jnp.broadcast_to(strength, (8, 128))
    fall[z_rows(z), :] = focal
    for d in far_order(nz):
        here = fall.at[z_rows(z)]
        send(here, here, s_w.at[d], r_w.at[d], tile=z_peer(d))
    others = [(e, d) for d in far_order(nz) + [0] for e in range(ns) if d or e]
    for e, d in others:
        send(
            isum,
            iparts.at[e, z_rows(z)],
            s_i.at[e, d],
            r_i.at[e, d],
            tile=z_peer(d),
            src=lax.rem(s + e, ns),
        )
    iparts[0, z_rows(z), :] = isum[...]
    loads["target"].wait()
    spot = lax.broadcasted_iota(jnp.int32, (fgroup, focal_count), 0)
    wide = lax.broadcasted_iota(jnp.int32, (fgroup, focal_count), 1)
    wanted = jnp.sum(
        jnp.where(
            wide == spot + q * fgroup,
            jnp.broadcast_to(target[...], (fgroup, focal_count)),
            0.0,
        ),
        axis=1,
        keepdims=True,
    )
    for e, d in others:
        sender = lax.rem(z + nz - d, nz)
        arrived(iparts.at[e, z_rows(sender)], s_i.at[e, d], r_i.at[e, d])
    strength = iparts[0]
    for e in range(1, ns):
        strength = strength + iparts[e]
    residual = jnp.tanh(strength / (2.0 * ROWS * ns)) - wanted
    for d in range(1, nz):
        sender = lax.rem(z + nz - d, nz)
        arrived(fall.at[z_rows(sender)], s_w.at[d], r_w.at[d])
    f16 = aligned(q * fgroup, fgroup, 16)
    wg[f16, :] = jnp.concatenate(
        [residual * fall[:, :ROWS], -residual * fall[:, ROWS:]], axis=1
    ).astype(BF16)
    for d in far_order(nq):
        here = wg.at[f16]
        send(here, here, s_wg.at[d], r_wg.at[d], tile=q_peer(d))
    row = lax.broadcasted_iota(jnp.int32, (fgroup, 128), 0)
    lane128 = lax.broadcasted_iota(jnp.int32, (fgroup, 128), 1)
    shift = lax.rem(q * fgroup, 128)
    flat = jnp.sum(
        jnp.where(lane128 == row + shift, residual, 0.0), axis=0, keepdims=True
    )
    rrow[...] = jnp.broadcast_to(flat, (8, 128))
    rgath[q] = jnp.broadcast_to(flat, (8, 128))
    for d in far_order(nq):
        send(rrow, rgath.at[q], s_rr.at[d], r_rr.at[d], tile=q_peer(d))
    for d in range(1, nq):
        sender = lax.rem(q + nq - d, nq)
        arrived(wg.at[aligned(sender * fgroup, fgroup, 16)], s_wg.at[d], r_wg.at[d])
    wt[...] = jnp.transpose(wg[...].astype(F32)).astype(BF16)

    scale = float(tiles * TILE / focal_count) ** 0.5

    @pl.loop(0, 4)
    def _(step):
        cols = aligned(step * HALF, HALF, HALF)
        w = wt[...]
        u = rows_joined(dot(w, fk[0, :, cols]), dot(w, fk[1, :, cols])) * scale
        adjoint[:, cols] = u
        vb[3, :, cols] = u.astype(BF16)

    gather(2, projected(vb[3], tbasis), False)

    @pl.loop(0, 4)
    def _(step):
        i = step // 2
        half = aligned((step % 2) * HALF, HALF, HALF)
        x = vb[3, :, aligned(i * TILE, TILE, TILE)]
        by_re = dot_nt(x, near[i, 2 * i, 0, half, :])
        by_im = dot_nt(x, near[i, 2 * i, 1, half, :])
        edge_send[i, :, half] = rows_joined(by_re, by_im).astype(BF16)

    send(edge_send.at[0], edge_in.at[1], s_edge.at[0], r_edge.at[1], tile=left)
    send(edge_send.at[1], edge_in.at[0], s_edge.at[1], r_edge.at[0], tile=right)

    gathered(2, False)
    coefficients = gath[2, :spread, :]
    scatter(
        2,
        lanes_joined(dot(mback[0], coefficients), dot(mback[1], coefficients)),
        True,
    )

    @pl.loop(0, 4)
    def _(step):
        m = step // 2
        half = aligned((step % 2) * HALF, HALF, HALF)
        by_re = jnp.zeros((2 * ROWS, HALF), F32)
        by_im = jnp.zeros((2 * ROWS, HALF), F32)
        for i in range(2):
            x = vb[3, :, i * TILE : (i + 1) * TILE]
            by_re = by_re + dot_nt(x, near[i, m - i + 1, 0, half, :])
            by_im = by_im + dot_nt(x, near[i, m - i + 1, 1, half, :])
        nacc[:, aligned(step * HALF, HALF, HALF)] = rows_joined(by_re, by_im)

    for side in range(2):
        arrived(edge_in.at[side], s_edge.at[side], r_edge.at[side])
    back = scattered(2, True)
    adjoint_copies = []
    for l in range(2):
        cols = slice(l * TILE, (l + 1) * TILE)
        added = nacc[:, cols] + edge_in[l].astype(F32) + expanded(back, sbasis, l)
        adjoint[:, cols] = adjoint[:, cols] - DAMPING * added
        copy = pltpu.make_async_copy(
            adjoint.at[:, cols], adj_out.at[:, cols], local_sem.at[11 + l]
        )
        copy.start()
        adjoint_copies.append(copy)

    lines = (focal_count + 127) // 128
    for d in range(1, nq):
        sender = lax.rem(q + nq - d, nq)
        arrived(rgath.at[sender], s_rr.at[d], r_rr.at[d])
    loads["owner"].wait()
    mine = lax.broadcasted_iota(jnp.int32, (8, 128), 0) + t * 8
    found = jnp.zeros((8, 128), F32)
    for line in range(lines):
        values = jnp.zeros((8, 128), F32)
        for other in range(nq):
            if other * fgroup // 128 == line:
                values = values + rgath[other]
        owners = jnp.broadcast_to(owner[line : line + 1, :], (8, 128))
        found = found + jnp.where(owners == mine, values, 0.0)
    column = jnp.broadcast_to(jnp.sum(found, axis=1, keepdims=True), (8, 128))
    diagonal = lax.broadcasted_iota(jnp.int32, (8, 128), 0) == lax.broadcasted_iota(
        jnp.int32, (8, 128), 1
    )
    line = jnp.sum(jnp.where(diagonal, column, 0.0), axis=0, keepdims=True)
    res_out[...] = line[:, :8]

    for copy in pending:
        copy.wait_send()
    field_copy.wait()
    for copy in adjoint_copies:
        copy.wait()


def hand_out(field, residual, adjoint, field_out, residual_out, adjoint_out, sem):
    copies = [
        pltpu.make_async_copy(field, field_out, sem.at[0]),
        pltpu.make_async_copy(adjoint, adjoint_out, sem.at[1]),
        pltpu.make_async_copy(residual, residual_out, sem.at[2]),
    ]
    for copy in copies:
        copy.start()
    for copy in copies:
        copy.wait()


def per_device(
    nz,
    excitation,
    near_blocks,
    source_basis,
    target_basis,
    coupling,
    pair_rank,
    far_link,
    focal_kernel,
    focal_target,
    focal_owner,
):
    nt = lax.axis_size("tile")
    ns = lax.axis_size("src")
    nq = nt // nz
    focal_count = focal_target.shape[0]
    group = nz * PAIR
    spread = nq * PAIR
    fgroup = nz * 8
    width = 2 * TILE
    most = max(nz, nq)
    lines = (focal_count + 127) // 128
    owner = jnp.pad(focal_owner, (0, lines * 128 - focal_count), constant_values=-1)
    vmem = pl.BlockSpec(memory_space=pltpu.VMEM)
    anywhere = pl.BlockSpec(memory_space=pl.ANY)
    dma = pltpu.SemaphoreType.DMA
    both = 2 * ROWS
    field, residual, adjoint = pl.pallas_call(
        functools.partial(kernel, nz, nq, ns),
        out_shape=(
            jax.ShapeDtypeStruct((both, width), F32),
            jax.ShapeDtypeStruct((1, 8), F32),
            jax.ShapeDtypeStruct((both, width), F32),
        ),
        in_specs=[anywhere] * 10,
        out_specs=(anywhere, vmem, anywhere),
        scratch_shapes=[
            pltpu.VMEM((both, width), F32),
            pltpu.VMEM((both, width), F32),
            pltpu.VMEM((2, 3, 2, TILE, TILE), BF16),
            pltpu.VMEM((2, focal_count, width), BF16),
            pltpu.VMEM((2, PAIR, TILE), BF16),
            pltpu.VMEM((2, PAIR, TILE), BF16),
            pltpu.VMEM((2, PAIR, nq * group), BF16),
            pltpu.VMEM((2, 2 * nt), jnp.int32),
            pltpu.VMEM((2, 2 * nt), jnp.int32),
            pltpu.VMEM((1, focal_count), F32),
            pltpu.VMEM((lines, 128), jnp.int32),
            pltpu.VMEM((4, both, width), BF16),
            pltpu.VMEM((2, 2, both, TILE), BF16),
            pltpu.VMEM((both, width), F32),
            pltpu.VMEM((nq, PAIR, group), BF16),
            pltpu.VMEM((2, spread, group), BF16),
            pltpu.VMEM((2, group, spread), BF16),
            pltpu.VMEM((3, most * PAIR, both), BF16),
            pltpu.VMEM((3, most * PAIR, both), BF16),
            pltpu.VMEM((3, most, PAIR, both), BF16),
            pltpu.VMEM((focal_count, both), BF16),
            pltpu.VMEM((nq, fgroup, both), BF16),
            pltpu.VMEM((fgroup, both), F32),
            pltpu.VMEM((nz, 8, both), F32),
            pltpu.VMEM((8, 128), F32),
            pltpu.VMEM((ns, fgroup, 128), F32),
            pltpu.VMEM((fgroup, both), F32),
            pltpu.VMEM((focal_count, both), BF16),
            pltpu.VMEM((both, focal_count), BF16),
            pltpu.VMEM((8, 128), F32),
            pltpu.VMEM((nq, 8, 128), F32),
            pltpu.VMEM((2, both, TILE), BF16),
            pltpu.VMEM((2, both, TILE), BF16),
            dma((13,)),
            dma((2, 2)),
            dma((2, 2)),
            dma((nq,)),
            dma((nq,)),
            dma((3, most)),
            dma((3, most)),
            dma((3, most)),
            dma((3, most)),
            dma((nq,)),
            dma((nq,)),
            dma((nz,)),
            dma((nz,)),
            dma((ns, nz)),
            dma((ns, nz)),
            dma((nz,)),
            dma((nz,)),
            dma((nq,)),
            dma((nq,)),
            dma((nq,)),
            dma((nq,)),
            dma((nq,)),
            dma((nq,)),
            dma((2,)),
            dma((2,)),
        ],
        compiler_params=pltpu.CompilerParams(
            collective_id=0, has_side_effects=True, vmem_limit_bytes=56 * 1024 * 1024
        ),
    )(
        excitation.reshape(both, width),
        near_blocks,
        source_basis.reshape(2, PAIR, TILE),
        target_basis.reshape(2, PAIR, TILE),
        jnp.swapaxes(coupling, 1, 2),
        pair_rank.T,
        far_link.T,
        focal_kernel,
        focal_target.reshape(1, focal_count),
        owner.reshape(lines, 128),
    )
    field, residual, adjoint = pl.pallas_call(
        hand_out,
        out_shape=(
            jax.ShapeDtypeStruct((both, width), F32),
            jax.ShapeDtypeStruct((1, 8), F32),
            jax.ShapeDtypeStruct((both, width), F32),
        ),
        in_specs=[anywhere] * 3,
        out_specs=[anywhere] * 3,
        scratch_shapes=[dma((3,))],
    )(field, residual, adjoint)
    return (
        field.reshape(2, ROWS, width),
        residual.reshape(8),
        adjoint.reshape(2, ROWS, width),
    )


def solution(mesh):
    nt = mesh.shape["tile"]
    nz = 8 if nt % 8 == 0 and nt > 8 else 2
    return jax.shard_map(
        functools.partial(per_device, nz),
        mesh=mesh,
        in_specs=(
            P(None, "src", "tile"),
            P("tile", None, None, None, None),
            P("tile", None, None, None),
            P("tile", None, None, None),
            P(None, None, "tile"),
            P(None, "tile"),
            P(None, "tile"),
            P(None, None, "tile"),
            P(),
            P(),
        ),
        out_specs=(P(None, "src", "tile"), P("tile"), P(None, "src", "tile")),
        check_vma=False,
    )
```

```python
import functools

import jax
import jax.numpy as jnp
from jax import lax
from jax.experimental import pallas as pl
from jax.experimental.pallas import tpu as pltpu
from jax.sharding import PartitionSpec as P

TILE = 512
RANK = 24
PAIR = 2 * RANK
ROWS = 128
DAMPING = 0.8
HALF = 256
F32 = jnp.float32
BF16 = jnp.bfloat16


def dot(left, right):
    return lax.dot_general(left, right, (((1,), (0,)), ((), ())), preferred_element_type=F32)


def dot_nt(left, right):
    return lax.dot_general(left, right, (((1,), (1,)), ((), ())), preferred_element_type=F32)


def rows_joined(by_re, by_im):
    return jnp.concatenate(
        [by_re[:ROWS] - by_im[ROWS:], by_re[ROWS:] + by_im[:ROWS]], axis=0
    )


def lanes_joined(by_re, by_im):
    return jnp.concatenate(
        [by_re[:, :ROWS] - by_im[:, ROWS:], by_re[:, ROWS:] + by_im[:, :ROWS]], axis=1
    )


def aligned(start, size, unit):
    return pl.ds(pl.multiple_of(start, unit), size)


def kernel(
    nz,
    nq,
    ns,
    exc_hbm,
    near_hbm,
    sbasis_hbm,
    tbasis_hbm,
    coup_hbm,
    rank_hbm,
    link_hbm,
    fk_hbm,
    target_hbm,
    owner_hbm,
    field_out,
    res_out,
    adj_out,
    field,
    adjoint,
    near,
    fk,
    sbasis,
    tbasis,
    coup,
    rank,
    link,
    target,
    owner,
    vb,
    halo,
    nacc,
    mt_send,
    mt,
    mback,
    gath,
    part,
    parts_in,
    fsend,
    fparts,
    fz,
    fzparts,
    isum,
    iparts,
    wg,
    wt,
    rrow,
    rgath,
    edge_send,
    edge_in,
    local_sem,
    s_halo,
    r_halo,
    s_mt,
    r_mt,
    s_gath,
    r_gath,
    s_part,
    r_part,
    s_f,
    r_f,
    s_fz,
    r_fz,
    s_i,
    r_i,
    s_sib,
    r_sib,
    s_wg,
    r_wg,
    s_rr,
    r_rr,
    s_edge,
    r_edge,
):
    t = lax.axis_index("tile")
    s = lax.axis_index("src")
    nt = nz * nq
    q = t // nz
    z = t - q * nz
    tiles = 2 * nt
    group = nz * PAIR
    spread = nq * PAIR
    fgroup = nz * 8
    focal_count = nt * 8

    def z_peer(d):
        return q * nz + lax.rem(z + d, nz)

    def q_peer(d):
        return lax.rem(q + d, nq) * nz + z

    left = lax.rem(t + nt - 1, nt)
    right = lax.rem(t + 1, nt)

    barrier = pltpu.get_barrier_semaphore()
    count = 0
    for d in range(1, nq):
        pl.semaphore_signal(barrier, inc=1, device_id={"tile": q_peer(d), "src": s})
        count += 1
    for other in (left, right):
        pl.semaphore_signal(barrier, inc=1, device_id={"tile": other, "src": s})
        count += 1
    for d in range(1, nz):
        pl.semaphore_signal(barrier, inc=1, device_id={"tile": z_peer(d), "src": s})
        count += 1
    for e in range(1, ns):
        pl.semaphore_signal(barrier, inc=1, device_id={"tile": t, "src": lax.rem(s + e, ns)})
        count += 1
    core = lax.rem(s, 2)
    sibling = s + 1 - 2 * core

    loads = {}
    for k, (name, source, place) in enumerate(
        (
            ("exc", exc_hbm, vb.at[0]),
            ("sbasis", sbasis_hbm, sbasis),
            ("rank", rank_hbm, rank),
            ("link", link_hbm, link),
            ("coup", coup_hbm, coup),
            ("near", near_hbm, near),
            ("tbasis", tbasis_hbm, tbasis),
            ("fk", fk_hbm, fk),
            ("target", target_hbm, target),
            ("owner", owner_hbm, owner),
        )
    ):
        loads[name] = pltpu.make_async_copy(source, place, local_sem.at[k])
        loads[name].start()

    pending = []

    def send(src_ref, dst_ref, send_sem, recv_sem, tile=None, src=None):
        copy = pltpu.make_async_remote_copy(
            src_ref=src_ref,
            dst_ref=dst_ref,
            send_sem=send_sem,
            recv_sem=recv_sem,
            device_id={"tile": t if tile is None else tile, "src": s if src is None else src},
        )
        copy.start()
        pending.append(copy)

    def arrived(ref, send_sem, recv_sem):
        pltpu.make_async_remote_copy(
            src_ref=ref,
            dst_ref=ref,
            send_sem=send_sem,
            recv_sem=recv_sem,
            device_id={"tile": right, "src": s},
        ).wait_recv()

    def far_order(n):
        return sorted(range(1, n), key=lambda d: -min(d, n - d))

    def own_slice(index):
        return aligned(index * PAIR, PAIR, 16)

    def projected(x, basis):
        pieces = []
        for l in range(2):
            both = dot_nt(basis[l], x[:, l * TILE : (l + 1) * TILE])
            pieces.append(lanes_joined(both[:RANK], both[RANK:]))
        return jnp.concatenate(pieces, axis=0).astype(BF16)

    def gather(stage, value, along_z):
        n, mine = (nz, z) if along_z else (nq, q)
        here = gath.at[stage, own_slice(mine)]
        gath[stage, own_slice(mine), :] = value
        for d in far_order(n):
            send(
                here,
                here,
                s_gath.at[stage, d],
                r_gath.at[stage, d],
                tile=z_peer(d) if along_z else q_peer(d),
            )

    def gathered(stage, along_z):
        n, mine = (nz, z) if along_z else (nq, q)
        for d in range(1, n):
            sender = lax.rem(mine + n - d, n)
            arrived(
                gath.at[stage, own_slice(sender)], s_gath.at[stage, d], r_gath.at[stage, d]
            )

    def scatter(stage, value, along_z):
        n, mine = (nz, z) if along_z else (nq, q)
        part[stage] = value.astype(BF16)
        for d in far_order(n):
            owner_of = lax.rem(mine + d, n)
            send(
                part.at[stage, own_slice(owner_of)],
                parts_in.at[stage, d],
                s_part.at[stage, d],
                r_part.at[stage, d],
                tile=z_peer(d) if along_z else q_peer(d),
            )

    def scattered(stage, along_z):
        n, mine = (nz, z) if along_z else (nq, q)
        total = part[stage, own_slice(mine), :].astype(F32)
        for d in range(1, n):
            arrived(parts_in.at[stage, d], s_part.at[stage, d], r_part.at[stage, d])
            total = total + parts_in[stage, d].astype(F32)
        return total.astype(BF16).astype(F32)

    def expanded(coefficients, basis, l):
        piece = coefficients[l * RANK : (l + 1) * RANK]
        turned = jnp.concatenate([-piece[:, ROWS:], piece[:, :ROWS]], axis=1)
        stacked = jnp.concatenate([piece, turned], axis=0)
        return dot(jnp.transpose(stacked).astype(BF16), basis[l])

    def send_halo(stage):
        send(
            vb.at[stage, :, TILE : 2 * TILE],
            halo.at[stage, 0],
            s_halo.at[stage, 0],
            r_halo.at[stage, 0],
            tile=right,
        )
        send(
            vb.at[stage, :, 0:TILE],
            halo.at[stage, 1],
            s_halo.at[stage, 1],
            r_halo.at[stage, 1],
            tile=left,
        )

    loads["exc"].wait()
    loads["sbasis"].wait()
    first_coeff = projected(vb[0], sbasis)
    loads["rank"].wait()
    loads["link"].wait()

    level = lax.broadcasted_iota(jnp.int32, (RANK, tiles), 0)
    source_tile = lax.broadcasted_iota(jnp.int32, (1, tiles), 1)
    limits = []
    for l in range(2):
        gap = t * 2 + l - source_tile
        is_near = (
            (gap == 0)
            | (gap == 1)
            | (gap == -1)
            | (gap == tiles - 1)
            | (gap == 1 - tiles)
        )
        here = jnp.where((link[l : l + 1, :] == 1) & ~is_near, rank[l : l + 1, :], 0)
        wide = jnp.broadcast_to(here, (RANK, tiles))
        limits.append(jnp.where(level < wide, wide, 0).astype(F32))
    limits.append(
        jnp.broadcast_to(source_tile, (16, tiles)).astype(F32)
    )
    limit_rows = jnp.concatenate(limits, axis=0).astype(BF16)

    pl.semaphore_wait(barrier, count)

    gather(0, first_coeff, True)
    send_halo(0)

    loads["coup"].wait()
    tile_row = lax.broadcasted_iota(jnp.int32, (tiles, group), 0)
    lane = lax.broadcasted_iota(jnp.int32, (tiles, group), 1)
    lane_row = lax.broadcasted_iota(jnp.int32, (1, group), 1)
    for d in far_order(nq) + [0]:
        to = lax.rem(q + d, nq)
        offset = lane - (tile_row - to * (2 * nz)) * RANK
        pick = jnp.where((offset >= 0) & (offset < RANK), 1.0, 0.0).astype(BF16)
        limit = dot(limit_rows, pick)
        position = (lane_row + to * group).astype(F32) - limit[PAIR : PAIR + 1, :] * float(RANK)
        keep = position < limit[:PAIR]
        for c in range(2) if d == 0 else (core,):
            block = coup[c, :, aligned(to * group, group, 128)]
            block = jnp.where(keep, block.astype(F32), 0.0).astype(BF16)
            if d == 0:
                mt[c, own_slice(q), :] = block
            else:
                mt_send[d] = block
        if d != 0:
            send(
                mt_send.at[d],
                mt.at[core, own_slice(q), :],
                s_mt.at[d],
                r_mt.at[d],
                tile=q_peer(d),
            )

    def near_own(stage):
        @pl.loop(0, 4)
        def _(step):
            i = step // 2
            cols = aligned((step % 2) * HALF, HALF, HALF)
            by_re = jnp.zeros((2 * ROWS, HALF), F32)
            by_im = jnp.zeros((2 * ROWS, HALF), F32)
            for l in range(2):
                x = vb[stage, :, l * TILE : (l + 1) * TILE]
                by_re = by_re + dot(x, near[i, l - i + 1, 0, :, cols])
                by_im = by_im + dot(x, near[i, l - i + 1, 1, :, cols])
            nacc[:, aligned(step * HALF, HALF, HALF)] = rows_joined(by_re, by_im)

    def near_halo(stage):
        @pl.loop(0, 4)
        def _(step):
            i = step // 2
            cols = aligned((step % 2) * HALF, HALF, HALF)
            x = halo[stage, i]
            by_re = dot(x, near[i, 2 * i, 0, :, cols])
            by_im = dot(x, near[i, 2 * i, 1, :, cols])
            out = aligned(step * HALF, HALF, HALF)
            nacc[:, out] = nacc[:, out] + rows_joined(by_re, by_im)

    loads["near"].wait()
    for stage in range(2):
        if stage == 1:
            gather(1, projected(vb[1], sbasis), True)
            send_halo(1)
        near_own(stage)
        if stage == 0:
            for d in range(1, nq):
                here = mt.at[core, own_slice(lax.rem(q + nq - d, nq)), :]
                arrived(here, s_mt.at[d], r_mt.at[d])
                send(here, here, s_sib.at[d], r_sib.at[d], src=sibling)
        gathered(stage, True)
        if stage == 0:
            for d in range(1, nq):
                here = mt.at[1 - core, own_slice(lax.rem(q + nq - d, nq)), :]
                arrived(here, s_sib.at[d], r_sib.at[d])
        coefficients = gath[stage, :group, :]
        scatter(
            stage,
            lanes_joined(dot(mt[0], coefficients), dot(mt[1], coefficients)),
            False,
        )
        for side in range(2):
            arrived(halo.at[stage, side], s_halo.at[stage, side], r_halo.at[stage, side])
        near_halo(stage)
        if stage == 0:
            for c in range(2):
                mback[c] = jnp.transpose(mt[c].astype(F32)).astype(BF16)
            loads["tbasis"].wait()
        coupled = scattered(stage, False)
        for l in range(2):
            cols = slice(l * TILE, (l + 1) * TILE)
            added = nacc[:, cols] + expanded(coupled, tbasis, l)
            right_side = vb[0, :, cols].astype(F32)
            if stage == 0:
                value = right_side - DAMPING * added
            else:
                before = field[:, cols]
                value = before + DAMPING * (right_side - (before + added))
            field[:, cols] = value
            vb[stage + 1, :, cols] = value.astype(BF16)

    field_copy = pltpu.make_async_copy(field, field_out, local_sem.at[10])
    field_copy.start()

    loads["fk"].wait()
    x = vb[2]
    fsend[...] = lanes_joined(dot_nt(fk[0], x), dot_nt(fk[1], x)).astype(BF16)

    def f_rows(index):
        return aligned(index * fgroup, fgroup, 16)

    for d in far_order(nq):
        send(
            fsend.at[f_rows(lax.rem(q + d, nq))],
            fparts.at[d],
            s_f.at[d],
            r_f.at[d],
            tile=q_peer(d),
        )
    total = fsend[f_rows(q), :].astype(F32)
    for d in range(1, nq):
        arrived(fparts.at[d], s_f.at[d], r_f.at[d])
        total = total + fparts[d].astype(F32)
    fz[...] = total.astype(BF16)
    for d in far_order(nz):
        send(fz, fzparts.at[d], s_fz.at[d], r_fz.at[d], tile=z_peer(d))
    row = lax.broadcasted_iota(jnp.int32, (fgroup, 128), 0)
    lane128 = lax.broadcasted_iota(jnp.int32, (fgroup, 128), 1)
    shift = lax.rem(q * fgroup, 128)
    diagonal = lane128 == row + shift
    loads["target"].wait()
    wanted = target[pl.ds(q * fgroup // 128, 1), :]
    focal = fz[...].astype(F32)
    for d in range(1, nz):
        arrived(fzparts.at[d], s_fz.at[d], r_fz.at[d])
        focal = focal + fzparts[d].astype(F32)
    square = focal * focal
    strength = jnp.sum(square[:, :ROWS] + square[:, ROWS:], axis=1, keepdims=True)
    line = jnp.sum(jnp.where(diagonal, strength, 0.0), axis=0, keepdims=True)
    isum[...] = jnp.broadcast_to(line, (8, 128))
    for e in far_order(ns):
        send(isum, iparts.at[e], s_i.at[e], r_i.at[e], src=lax.rem(s + e, ns))
    strength = line
    for e in range(1, ns):
        arrived(iparts.at[e], s_i.at[e], r_i.at[e])
        strength = strength + iparts[e, :1, :]
    in_line = lane128[:1] - shift
    in_line = (in_line >= 0) & (in_line < fgroup)
    flat = jnp.where(in_line, jnp.tanh(strength / (2.0 * ROWS * ns)) - wanted, 0.0)
    residual = jnp.sum(jnp.where(diagonal, flat, 0.0), axis=1, keepdims=True)
    f16 = aligned(q * fgroup, fgroup, 16)
    wg[f16, :] = jnp.concatenate(
        [residual * focal[:, :ROWS], -residual * focal[:, ROWS:]], axis=1
    ).astype(BF16)
    for d in far_order(nq):
        here = wg.at[f16]
        send(here, here, s_wg.at[d], r_wg.at[d], tile=q_peer(d))
    rrow[...] = jnp.broadcast_to(flat, (8, 128))
    rgath[q] = jnp.broadcast_to(flat, (8, 128))
    for d in far_order(nq):
        send(rrow, rgath.at[q], s_rr.at[d], r_rr.at[d], tile=q_peer(d))
    for d in range(1, nq):
        sender = lax.rem(q + nq - d, nq)
        arrived(wg.at[aligned(sender * fgroup, fgroup, 16)], s_wg.at[d], r_wg.at[d])
    wt[...] = jnp.transpose(wg[...].astype(F32)).astype(BF16)

    scale = float(tiles * TILE / focal_count) ** 0.5

    @pl.loop(0, 4)
    def _(step):
        cols = aligned(step * HALF, HALF, HALF)
        w = wt[...]
        u = rows_joined(dot(w, fk[0, :, cols]), dot(w, fk[1, :, cols])) * scale
        adjoint[:, cols] = u
        vb[3, :, cols] = u.astype(BF16)

    gather(2, projected(vb[3], tbasis), False)

    @pl.loop(0, 4)
    def _(step):
        i = step // 2
        half = aligned((step % 2) * HALF, HALF, HALF)
        x = vb[3, :, aligned(i * TILE, TILE, TILE)]
        by_re = dot_nt(x, near[i, 2 * i, 0, half, :])
        by_im = dot_nt(x, near[i, 2 * i, 1, half, :])
        edge_send[i, :, half] = rows_joined(by_re, by_im).astype(BF16)

    send(edge_send.at[0], edge_in.at[1], s_edge.at[0], r_edge.at[1], tile=left)
    send(edge_send.at[1], edge_in.at[0], s_edge.at[1], r_edge.at[0], tile=right)

    gathered(2, False)
    coefficients = gath[2, :spread, :]
    scatter(
        2,
        lanes_joined(dot(mback[0], coefficients), dot(mback[1], coefficients)),
        True,
    )

    @pl.loop(0, 4)
    def _(step):
        m = step // 2
        half = aligned((step % 2) * HALF, HALF, HALF)
        by_re = jnp.zeros((2 * ROWS, HALF), F32)
        by_im = jnp.zeros((2 * ROWS, HALF), F32)
        for i in range(2):
            x = vb[3, :, i * TILE : (i + 1) * TILE]
            by_re = by_re + dot_nt(x, near[i, m - i + 1, 0, half, :])
            by_im = by_im + dot_nt(x, near[i, m - i + 1, 1, half, :])
        nacc[:, aligned(step * HALF, HALF, HALF)] = rows_joined(by_re, by_im)

    for side in range(2):
        arrived(edge_in.at[side], s_edge.at[side], r_edge.at[side])
    back = scattered(2, True)
    adjoint_copies = []
    for l in range(2):
        cols = slice(l * TILE, (l + 1) * TILE)
        added = nacc[:, cols] + edge_in[l].astype(F32) + expanded(back, sbasis, l)
        adjoint[:, cols] = adjoint[:, cols] - DAMPING * added
        copy = pltpu.make_async_copy(
            adjoint.at[:, cols], adj_out.at[:, cols], local_sem.at[11 + l]
        )
        copy.start()
        adjoint_copies.append(copy)

    lines = (focal_count + 127) // 128
    for d in range(1, nq):
        sender = lax.rem(q + nq - d, nq)
        arrived(rgath.at[sender], s_rr.at[d], r_rr.at[d])
    loads["owner"].wait()
    mine = lax.broadcasted_iota(jnp.int32, (8, 128), 0) + t * 8
    found = jnp.zeros((8, 128), F32)
    for line in range(lines):
        values = jnp.zeros((8, 128), F32)
        for other in range(nq):
            if other * fgroup // 128 == line:
                values = values + rgath[other]
        owners = jnp.broadcast_to(owner[line : line + 1, :], (8, 128))
        found = found + jnp.where(owners == mine, values, 0.0)
    column = jnp.broadcast_to(jnp.sum(found, axis=1, keepdims=True), (8, 128))
    diagonal = lax.broadcasted_iota(jnp.int32, (8, 128), 0) == lax.broadcasted_iota(
        jnp.int32, (8, 128), 1
    )
    line = jnp.sum(jnp.where(diagonal, column, 0.0), axis=0, keepdims=True)
    res_out[...] = line[:, :8]

    for copy in pending:
        copy.wait_send()
    field_copy.wait()
    for copy in adjoint_copies:
        copy.wait()


CHUNKS = 4


def hand_out(field, residual, adjoint, field_out, residual_out, adjoint_out, held, in_sem, out_sem):
    residual_out[...] = residual[...]
    rows = held.shape[1] // CHUNKS
    loads, stores = [], []
    for k, (source, target) in enumerate(((field, field_out), (adjoint, adjoint_out))):
        for c in range(CHUNKS):
            part = pl.ds(c * rows, rows)
            here = held.at[k, part]
            loads.append(pltpu.make_async_copy(source.at[part], here, in_sem.at[k, c]))
            stores.append(pltpu.make_async_copy(here, target.at[part], out_sem.at[k, c]))
    for copy in loads:
        copy.start()
    for load, store in zip(loads, stores):
        load.wait()
        store.start()
    for store in stores:
        store.wait()


def per_device(
    nz,
    excitation,
    near_blocks,
    source_basis,
    target_basis,
    coupling,
    pair_rank,
    far_link,
    focal_kernel,
    focal_target,
    focal_owner,
):
    nt = lax.axis_size("tile")
    ns = lax.axis_size("src")
    nq = nt // nz
    focal_count = focal_target.shape[0]
    group = nz * PAIR
    spread = nq * PAIR
    fgroup = nz * 8
    width = 2 * TILE
    most = max(nz, nq)
    lines = (focal_count + 127) // 128
    wanted = jnp.pad(focal_target, (0, lines * 128 - focal_count))
    owner = jnp.pad(focal_owner, (0, lines * 128 - focal_count), constant_values=-1)
    vmem = pl.BlockSpec(memory_space=pltpu.VMEM)
    anywhere = pl.BlockSpec(memory_space=pl.ANY)
    dma = pltpu.SemaphoreType.DMA
    both = 2 * ROWS
    field, residual, adjoint = pl.pallas_call(
        functools.partial(kernel, nz, nq, ns),
        out_shape=(
            jax.ShapeDtypeStruct((both, width), F32),
            jax.ShapeDtypeStruct((1, 8), F32),
            jax.ShapeDtypeStruct((both, width), F32),
        ),
        in_specs=[anywhere] * 10,
        out_specs=(anywhere, vmem, anywhere),
        scratch_shapes=[
            pltpu.VMEM((both, width), F32),
            pltpu.VMEM((both, width), F32),
            pltpu.VMEM((2, 3, 2, TILE, TILE), BF16),
            pltpu.VMEM((2, focal_count, width), BF16),
            pltpu.VMEM((2, PAIR, TILE), BF16),
            pltpu.VMEM((2, PAIR, TILE), BF16),
            pltpu.VMEM((2, PAIR, nq * group), BF16),
            pltpu.VMEM((2, 2 * nt), jnp.int32),
            pltpu.VMEM((2, 2 * nt), jnp.int32),
            pltpu.VMEM((lines, 128), F32),
            pltpu.VMEM((lines, 128), jnp.int32),
            pltpu.VMEM((4, both, width), BF16),
            pltpu.VMEM((2, 2, both, TILE), BF16),
            pltpu.VMEM((both, width), F32),
            pltpu.VMEM((nq, PAIR, group), BF16),
            pltpu.VMEM((2, spread, group), BF16),
            pltpu.VMEM((2, group, spread), BF16),
            pltpu.VMEM((3, most * PAIR, both), BF16),
            pltpu.VMEM((3, most * PAIR, both), BF16),
            pltpu.VMEM((3, most, PAIR, both), BF16),
            pltpu.VMEM((focal_count, both), BF16),
            pltpu.VMEM((nq, fgroup, both), BF16),
            pltpu.VMEM((fgroup, both), BF16),
            pltpu.VMEM((nz, fgroup, both), BF16),
            pltpu.VMEM((8, 128), F32),
            pltpu.VMEM((ns, 8, 128), F32),
            pltpu.VMEM((focal_count, both), BF16),
            pltpu.VMEM((both, focal_count), BF16),
            pltpu.VMEM((8, 128), F32),
            pltpu.VMEM((nq, 8, 128), F32),
            pltpu.VMEM((2, both, TILE), BF16),
            pltpu.VMEM((2, both, TILE), BF16),
            dma((13,)),
            dma((2, 2)),
            dma((2, 2)),
            dma((nq,)),
            dma((nq,)),
            dma((3, most)),
            dma((3, most)),
            dma((3, most)),
            dma((3, most)),
            dma((nq,)),
            dma((nq,)),
            dma((nz,)),
            dma((nz,)),
            dma((ns,)),
            dma((ns,)),
            dma((nq,)),
            dma((nq,)),
            dma((nq,)),
            dma((nq,)),
            dma((nq,)),
            dma((nq,)),
            dma((2,)),
            dma((2,)),
        ],
        compiler_params=pltpu.CompilerParams(
            collective_id=0, has_side_effects=True, vmem_limit_bytes=56 * 1024 * 1024
        ),
    )(
        excitation.reshape(both, width),
        near_blocks,
        source_basis.reshape(2, PAIR, TILE),
        target_basis.reshape(2, PAIR, TILE),
        jnp.swapaxes(coupling, 1, 2),
        pair_rank.T,
        far_link.T,
        focal_kernel,
        wanted.reshape(lines, 128),
        owner.reshape(lines, 128),
    )
    field, residual, adjoint = pl.pallas_call(
        hand_out,
        out_shape=(
            jax.ShapeDtypeStruct((both, width), F32),
            jax.ShapeDtypeStruct((1, 8), F32),
            jax.ShapeDtypeStruct((both, width), F32),
        ),
        in_specs=[anywhere, vmem, anywhere],
        out_specs=[anywhere, vmem, anywhere],
        scratch_shapes=[
            pltpu.VMEM((2, both, width), F32),
            dma((2, CHUNKS)),
            dma((2, CHUNKS)),
        ],
        compiler_params=pltpu.CompilerParams(vmem_limit_bytes=56 * 1024 * 1024),
    )(field, residual, adjoint)
    return (
        field.reshape(2, ROWS, width),
        residual.reshape(8),
        adjoint.reshape(2, ROWS, width),
    )


def solution(mesh):
    nt = mesh.shape["tile"]
    nz = 8 if nt % 8 == 0 and nt > 8 else 2
    return jax.shard_map(
        functools.partial(per_device, nz),
        mesh=mesh,
        in_specs=(
            P(None, "src", "tile"),
            P("tile", None, None, None, None),
            P("tile", None, None, None),
            P("tile", None, None, None),
            P(None, None, "tile"),
            P(None, "tile"),
            P(None, "tile"),
            P(None, None, "tile"),
            P(),
            P(),
        ),
        out_specs=(P(None, "src", "tile"), P("tile"), P(None, "src", "tile")),
        check_vma=False,
    )
```

```python
import functools

import jax
import jax.numpy as jnp
from jax import lax
from jax.experimental import pallas as pl
from jax.experimental.pallas import tpu as pltpu
from jax.sharding import PartitionSpec as P

TILE = 512
RANK = 24
PAIR = 2 * RANK
ROWS = 128
DAMPING = 0.8
HALF = 256
F32 = jnp.float32
BF16 = jnp.bfloat16


def dot(left, right):
    return lax.dot_general(left, right, (((1,), (0,)), ((), ())), preferred_element_type=F32)


def dot_nt(left, right):
    return lax.dot_general(left, right, (((1,), (1,)), ((), ())), preferred_element_type=F32)


def rows_joined(by_re, by_im):
    shape = by_re.shape
    blocks = (shape[0] // ROWS, 2, ROWS // 2, shape[1])
    by_re, by_im = by_re.reshape(blocks), by_im.reshape(blocks)
    re = by_re[:, 0] - by_im[:, 1]
    im = by_re[:, 1] + by_im[:, 0]
    return jnp.stack([re, im], axis=1).reshape(shape)


def turned(x):
    lane = lax.broadcasted_iota(jnp.int32, (1, ROWS), 1)
    sign = jnp.where(lane < ROWS // 2, -1.0, 1.0)
    blocks = [
        pltpu.roll(x[:, k : k + ROWS], ROWS // 2, 1) * sign for k in range(0, x.shape[1], ROWS)
    ]
    return blocks[0] if len(blocks) == 1 else jnp.concatenate(blocks, axis=1)


def lanes_joined(by_re, by_im):
    return by_re + turned(by_im)


def half_of(h):
    return slice(0, 2 * ROWS) if h is None else slice(h * ROWS, (h + 1) * ROWS)


def aligned(start, size, unit):
    return pl.ds(pl.multiple_of(start, unit), size)


def kernel(
    nz,
    nq,
    ns,
    exc_hbm,
    near_hbm,
    sbasis_hbm,
    tbasis_hbm,
    coup_hbm,
    rank_hbm,
    link_hbm,
    fk_hbm,
    target_hbm,
    owner_hbm,
    field_out,
    res_out,
    adj_out,
    field,
    adjoint,
    near,
    fk,
    sbasis,
    tbasis,
    coup,
    rank,
    link,
    target,
    owner,
    vb,
    halo,
    nacc,
    mt_send,
    mt,
    mback,
    gath,
    part,
    parts_in,
    fsend,
    fparts,
    fz,
    fzparts,
    isum,
    iparts,
    wg,
    wt,
    rrow,
    rgath,
    edge_send,
    edge_in,
    local_sem,
    s_halo,
    r_halo,
    s_mt,
    r_mt,
    s_gath,
    r_gath,
    s_part,
    r_part,
    s_f,
    r_f,
    s_fz,
    r_fz,
    s_i,
    r_i,
    s_sib,
    r_sib,
    s_wg,
    r_wg,
    s_rr,
    r_rr,
    s_edge,
    r_edge,
):
    t = lax.axis_index("tile")
    s = lax.axis_index("src")
    nt = nz * nq
    q = t // nz
    z = t - q * nz
    tiles = 2 * nt
    group = nz * PAIR
    spread = nq * PAIR
    fgroup = nz * 8
    focal_count = nt * 8

    def z_peer(d):
        return q * nz + lax.rem(z + d, nz)

    def q_peer(d):
        return lax.rem(q + d, nq) * nz + z

    left = lax.rem(t + nt - 1, nt)
    right = lax.rem(t + 1, nt)

    barrier = pltpu.get_barrier_semaphore()
    count = 0
    for d in range(1, nq):
        pl.semaphore_signal(barrier, inc=1, device_id={"tile": q_peer(d), "src": s})
        count += 1
    for other in (left, right):
        pl.semaphore_signal(barrier, inc=1, device_id={"tile": other, "src": s})
        count += 1
    for d in range(1, nz):
        pl.semaphore_signal(barrier, inc=1, device_id={"tile": z_peer(d), "src": s})
        count += 1
    for e in range(1, ns):
        pl.semaphore_signal(barrier, inc=1, device_id={"tile": t, "src": lax.rem(s + e, ns)})
        count += 1
    core = lax.rem(s, 2)
    sibling = s + 1 - 2 * core

    half = ROWS // 2
    loads = {}
    for k, (name, source, place) in enumerate(
        (
            *(
                (
                    ("exc", h, c),
                    exc_hbm.at[c, h * half : (h + 1) * half],
                    vb.at[0, (2 * h + c) * half : (2 * h + c + 1) * half],
                )
                for h in range(2)
                for c in range(2)
            ),
            ("sbasis", sbasis_hbm, sbasis),
            ("rank", rank_hbm, rank),
            ("link", link_hbm, link),
            ("coup", coup_hbm, coup),
            ("near", near_hbm, near),
            ("tbasis", tbasis_hbm, tbasis),
            ("fk", fk_hbm, fk),
            ("target", target_hbm, target),
            ("owner", owner_hbm, owner),
        )
    ):
        loads[name] = pltpu.make_async_copy(source, place, local_sem.at[k])
        loads[name].start()

    pending = []

    def send(src_ref, dst_ref, send_sem, recv_sem, tile=None, src=None):
        copy = pltpu.make_async_remote_copy(
            src_ref=src_ref,
            dst_ref=dst_ref,
            send_sem=send_sem,
            recv_sem=recv_sem,
            device_id={"tile": t if tile is None else tile, "src": s if src is None else src},
        )
        copy.start()
        pending.append(copy)

    def arrived(ref, send_sem, recv_sem):
        pltpu.make_async_remote_copy(
            src_ref=ref,
            dst_ref=ref,
            send_sem=send_sem,
            recv_sem=recv_sem,
            device_id={"tile": right, "src": s},
        ).wait_recv()

    def far_order(n):
        return sorted(range(1, n), key=lambda d: -min(d, n - d))

    def own_slice(index):
        return aligned(index * PAIR, PAIR, 16)

    def projected(x, basis):
        pieces = []
        for l in range(2):
            both = dot_nt(basis[l], x[:, l * TILE : (l + 1) * TILE])
            pieces.append(lanes_joined(both[:RANK], both[RANK:]))
        return jnp.concatenate(pieces, axis=0).astype(BF16)

    def gather(stage, h, value, along_z):
        n, mine = (nz, z) if along_z else (nq, q)
        lanes = half_of(h)
        here = gath.at[stage, own_slice(mine), lanes]
        gath[stage, own_slice(mine), lanes] = value
        for d in far_order(n):
            send(
                here,
                here,
                s_gath.at[stage, h or 0, d],
                r_gath.at[stage, h or 0, d],
                tile=z_peer(d) if along_z else q_peer(d),
            )

    def gathered(stage, h, along_z):
        n, mine = (nz, z) if along_z else (nq, q)
        for d in range(1, n):
            sender = lax.rem(mine + n - d, n)
            arrived(
                gath.at[stage, own_slice(sender), half_of(h)],
                s_gath.at[stage, h or 0, d],
                r_gath.at[stage, h or 0, d],
            )
        return gath[stage, : n * PAIR, half_of(h)]

    def scatter(stage, h, value, along_z):
        n, mine = (nz, z) if along_z else (nq, q)
        lanes = half_of(h)
        part[stage, :, lanes] = value.astype(BF16)
        for d in far_order(n):
            owner_of = lax.rem(mine + d, n)
            send(
                part.at[stage, own_slice(owner_of), lanes],
                parts_in.at[stage, d, :, lanes],
                s_part.at[stage, h or 0, d],
                r_part.at[stage, h or 0, d],
                tile=z_peer(d) if along_z else q_peer(d),
            )

    def scattered(stage, h, along_z):
        n, mine = (nz, z) if along_z else (nq, q)
        lanes = half_of(h)
        total = part[stage, own_slice(mine), lanes].astype(F32)
        for d in range(1, n):
            arrived(
                parts_in.at[stage, d, :, lanes],
                s_part.at[stage, h or 0, d],
                r_part.at[stage, h or 0, d],
            )
            total = total + parts_in[stage, d, :, lanes].astype(F32)
        return total.astype(BF16).astype(F32)

    def expanded(coefficients, basis, l):
        piece = coefficients[l * RANK : (l + 1) * RANK]
        stacked = jnp.concatenate([piece, turned(piece)], axis=0)
        return dot(jnp.transpose(stacked).astype(BF16), basis[l])

    def send_halo(stage, h):
        rows = half_of(h)
        send(
            vb.at[stage, rows, TILE : 2 * TILE],
            halo.at[stage, 0, rows],
            s_halo.at[stage, h, 0],
            r_halo.at[stage, h, 0],
            tile=right,
        )
        send(
            vb.at[stage, rows, 0:TILE],
            halo.at[stage, 1, rows],
            s_halo.at[stage, h, 1],
            r_halo.at[stage, h, 1],
            tile=left,
        )

    for h in range(2):
        for c in range(2):
            loads["exc", h, c].wait()
    loads["sbasis"].wait()
    first_coeff = projected(vb[0], sbasis)
    loads["rank"].wait()
    loads["link"].wait()

    level = lax.broadcasted_iota(jnp.int32, (RANK, tiles), 0)
    source_tile = lax.broadcasted_iota(jnp.int32, (1, tiles), 1)
    limits = []
    for l in range(2):
        gap = t * 2 + l - source_tile
        is_near = (
            (gap == 0)
            | (gap == 1)
            | (gap == -1)
            | (gap == tiles - 1)
            | (gap == 1 - tiles)
        )
        here = jnp.where((link[l : l + 1, :] == 1) & ~is_near, rank[l : l + 1, :], 0)
        wide = jnp.broadcast_to(here, (RANK, tiles))
        limits.append(jnp.where(level < wide, wide, 0).astype(F32))
    limits.append(
        jnp.broadcast_to(source_tile, (16, tiles)).astype(F32)
    )
    limit_rows = jnp.concatenate(limits, axis=0).astype(BF16)

    pl.semaphore_wait(barrier, count)

    for h in range(2):
        gather(0, h, first_coeff[:, half_of(h)], True)
        send_halo(0, h)

    loads["coup"].wait()
    tile_row = lax.broadcasted_iota(jnp.int32, (tiles, group), 0)
    lane = lax.broadcasted_iota(jnp.int32, (tiles, group), 1)
    lane_row = lax.broadcasted_iota(jnp.int32, (1, group), 1)
    for d in far_order(nq) + [0]:
        to = lax.rem(q + d, nq)
        offset = lane - (tile_row - to * (2 * nz)) * RANK
        pick = jnp.where((offset >= 0) & (offset < RANK), 1.0, 0.0).astype(BF16)
        limit = dot(limit_rows, pick)
        position = (lane_row + to * group).astype(F32) - limit[PAIR : PAIR + 1, :] * float(RANK)
        keep = position < limit[:PAIR]
        for c in range(2) if d == 0 else (core,):
            block = coup[c, :, aligned(to * group, group, 128)]
            block = jnp.where(keep, block.astype(F32), 0.0).astype(BF16)
            if d == 0:
                mt[c, own_slice(q), :] = block
            else:
                mt_send[d] = block
        if d != 0:
            send(
                mt_send.at[d],
                mt.at[core, own_slice(q), :],
                s_mt.at[d],
                r_mt.at[d],
                tile=q_peer(d),
            )

    def near_own(stage, h):
        rows = half_of(h)

        @pl.loop(0, 4)
        def _(step):
            i = step // 2
            cols = aligned((step % 2) * HALF, HALF, HALF)
            by_re = by_im = 0.0
            for l in range(2):
                x = vb[stage, rows, l * TILE : (l + 1) * TILE]
                by_re = by_re + dot(x, near[i, l - i + 1, 0, :, cols])
                by_im = by_im + dot(x, near[i, l - i + 1, 1, :, cols])
            nacc[rows, aligned(step * HALF, HALF, HALF)] = rows_joined(by_re, by_im)

    def near_halo(stage, h):
        rows = half_of(h)
        for side in range(2):
            arrived(
                halo.at[stage, side, rows],
                s_halo.at[stage, h, side],
                r_halo.at[stage, h, side],
            )

        @pl.loop(0, 4)
        def _(step):
            i = step // 2
            cols = aligned((step % 2) * HALF, HALF, HALF)
            x = halo[stage, i, rows]
            by_re = dot(x, near[i, 2 * i, 0, :, cols])
            by_im = dot(x, near[i, 2 * i, 1, :, cols])
            out = aligned(step * HALF, HALF, HALF)
            nacc[rows, out] = nacc[rows, out] + rows_joined(by_re, by_im)

    def couple(stage, h):
        coefficients = gathered(stage, h, True)
        scatter(
            stage, h, lanes_joined(dot(mt[0], coefficients), dot(mt[1], coefficients)), False
        )

    def updated(stage, h):
        near_halo(stage, h)
        coupled = scattered(stage, h, False)
        rows = half_of(h)
        for l in range(2):
            cols = slice(l * TILE, (l + 1) * TILE)
            added = nacc[rows, cols] + expanded(coupled, tbasis, l)
            right_side = vb[0, rows, cols].astype(F32)
            if stage == 0:
                value = right_side - DAMPING * added
            else:
                before = field[rows, cols]
                value = before + DAMPING * (right_side - (before + added))
            field[rows, cols] = value
            vb[stage + 1, rows, cols] = value.astype(BF16)

    loads["near"].wait()
    near_own(0, None)
    for d in range(1, nq):
        here = mt.at[core, own_slice(lax.rem(q + nq - d, nq)), :]
        arrived(here, s_mt.at[d], r_mt.at[d])
        send(here, here, s_sib.at[d], r_sib.at[d], src=sibling)
    for d in range(1, nq):
        here = mt.at[1 - core, own_slice(lax.rem(q + nq - d, nq)), :]
        arrived(here, s_sib.at[d], r_sib.at[d])
    for h in range(2):
        couple(0, h)
    for c in range(2):
        mback[c] = jnp.transpose(mt[c].astype(F32)).astype(BF16)
    loads["tbasis"].wait()
    for h in range(2):
        updated(0, h)
        gather(1, h, projected(vb[1, half_of(h)], sbasis), True)
        send_halo(1, h)
    for h in range(2):
        near_own(1, h)
        couple(1, h)
    loads["fk"].wait()
    copies = []

    def f_rows(index):
        return aligned(index * fgroup, fgroup, 16)

    for h in range(2):
        updated(1, h)
        for c in range(2):
            copy = pltpu.make_async_copy(
                field.at[(2 * h + c) * half : (2 * h + c + 1) * half],
                field_out.at[c, h * half : (h + 1) * half],
                local_sem.at[13 + 2 * h + c],
            )
            copy.start()
            copies.append(copy)
        lanes = half_of(h)
        x = vb[2, lanes]
        fsend[:, lanes] = lanes_joined(dot_nt(fk[0], x), dot_nt(fk[1], x)).astype(BF16)
        for d in far_order(nq):
            send(
                fsend.at[f_rows(lax.rem(q + d, nq)), lanes],
                fparts.at[d, :, lanes],
                s_f.at[h, d],
                r_f.at[h, d],
                tile=q_peer(d),
            )
    for h in range(2):
        lanes = half_of(h)
        total = fsend[f_rows(q), lanes].astype(F32)
        for d in range(1, nq):
            arrived(fparts.at[d, :, lanes], s_f.at[h, d], r_f.at[h, d])
            total = total + fparts[d, :, lanes].astype(F32)
        fz[:, lanes] = total.astype(BF16)
        for d in far_order(nz):
            send(
                fz.at[:, lanes],
                fzparts.at[d, :, lanes],
                s_fz.at[h, d],
                r_fz.at[h, d],
                tile=z_peer(d),
            )
    row = lax.broadcasted_iota(jnp.int32, (fgroup, 128), 0)
    lane128 = lax.broadcasted_iota(jnp.int32, (fgroup, 128), 1)
    shift = lax.rem(q * fgroup, 128)
    diagonal = lane128 == row + shift
    loads["target"].wait()
    wanted = target[pl.ds(q * fgroup // 128, 1), :]
    focal = fz[...].astype(F32)
    for d in range(1, nz):
        for h in range(2):
            arrived(fzparts.at[d, :, half_of(h)], s_fz.at[h, d], r_fz.at[h, d])
        focal = focal + fzparts[d].astype(F32)
    square = focal * focal
    strength = jnp.sum(square[:, :ROWS] + square[:, ROWS:], axis=1, keepdims=True)
    line = jnp.sum(jnp.where(diagonal, strength, 0.0), axis=0, keepdims=True)
    isum[...] = jnp.broadcast_to(line, (8, 128))
    for e in far_order(ns):
        send(isum, iparts.at[e], s_i.at[e], r_i.at[e], src=lax.rem(s + e, ns))
    strength = line
    for e in range(1, ns):
        arrived(iparts.at[e], s_i.at[e], r_i.at[e])
        strength = strength + iparts[e, :1, :]
    in_line = lane128[:1] - shift
    in_line = (in_line >= 0) & (in_line < fgroup)
    flat = jnp.where(in_line, jnp.tanh(strength / (2.0 * ROWS * ns)) - wanted, 0.0)
    residual = jnp.sum(jnp.where(diagonal, flat, 0.0), axis=1, keepdims=True)
    f16 = aligned(q * fgroup, fgroup, 16)
    sign = jnp.where(lane128[:1] < ROWS // 2, 1.0, -1.0)
    sign = jnp.concatenate([sign, sign], axis=1)
    wg[f16, :] = (residual * focal * sign).astype(BF16)
    for d in far_order(nq):
        here = wg.at[f16]
        send(here, here, s_wg.at[d], r_wg.at[d], tile=q_peer(d))
    rrow[...] = jnp.broadcast_to(flat, (8, 128))
    rgath[q] = jnp.broadcast_to(flat, (8, 128))
    for d in far_order(nq):
        send(rrow, rgath.at[q], s_rr.at[d], r_rr.at[d], tile=q_peer(d))
    for d in range(1, nq):
        sender = lax.rem(q + nq - d, nq)
        arrived(wg.at[aligned(sender * fgroup, fgroup, 16)], s_wg.at[d], r_wg.at[d])
    wt[...] = jnp.transpose(wg[...].astype(F32)).astype(BF16)

    scale = float(tiles * TILE / focal_count) ** 0.5

    @pl.loop(0, 4)
    def _(step):
        cols = aligned(step * HALF, HALF, HALF)
        w = wt[...]
        u = rows_joined(dot(w, fk[0, :, cols]), dot(w, fk[1, :, cols])) * scale
        adjoint[:, cols] = u
        vb[3, :, cols] = u.astype(BF16)

    gather(2, None, projected(vb[3], tbasis), False)

    @pl.loop(0, 4)
    def _(step):
        i = step // 2
        half = aligned((step % 2) * HALF, HALF, HALF)
        x = vb[3, :, aligned(i * TILE, TILE, TILE)]
        by_re = dot_nt(x, near[i, 2 * i, 0, half, :])
        by_im = dot_nt(x, near[i, 2 * i, 1, half, :])
        edge_send[i, :, half] = rows_joined(by_re, by_im).astype(BF16)

    send(edge_send.at[0], edge_in.at[1], s_edge.at[0], r_edge.at[1], tile=left)
    send(edge_send.at[1], edge_in.at[0], s_edge.at[1], r_edge.at[0], tile=right)

    coefficients = gathered(2, None, False)
    scatter(
        2,
        None,
        lanes_joined(dot(mback[0], coefficients), dot(mback[1], coefficients)),
        True,
    )

    @pl.loop(0, 4)
    def _(step):
        m = step // 2
        half = aligned((step % 2) * HALF, HALF, HALF)
        by_re = jnp.zeros((2 * ROWS, HALF), F32)
        by_im = jnp.zeros((2 * ROWS, HALF), F32)
        for i in range(2):
            x = vb[3, :, i * TILE : (i + 1) * TILE]
            by_re = by_re + dot_nt(x, near[i, m - i + 1, 0, half, :])
            by_im = by_im + dot_nt(x, near[i, m - i + 1, 1, half, :])
        nacc[:, aligned(step * HALF, HALF, HALF)] = rows_joined(by_re, by_im)

    for side in range(2):
        arrived(edge_in.at[side], s_edge.at[side], r_edge.at[side])
    back = scattered(2, None, True)
    for l in range(2):
        cols = slice(l * TILE, (l + 1) * TILE)
        added = nacc[:, cols] + edge_in[l].astype(F32) + expanded(back, sbasis, l)
        adjoint[:, cols] = adjoint[:, cols] - DAMPING * added
        for k in range(4):
            copy = pltpu.make_async_copy(
                adjoint.at[k * half : (k + 1) * half, cols],
                adj_out.at[k % 2, (k // 2) * half : (k // 2 + 1) * half, cols],
                local_sem.at[17 + 4 * l + k],
            )
            copy.start()
            copies.append(copy)

    lines = (focal_count + 127) // 128
    for d in range(1, nq):
        sender = lax.rem(q + nq - d, nq)
        arrived(rgath.at[sender], s_rr.at[d], r_rr.at[d])
    loads["owner"].wait()
    mine = lax.broadcasted_iota(jnp.int32, (8, 128), 0) + t * 8
    found = jnp.zeros((8, 128), F32)
    for line in range(lines):
        values = jnp.zeros((8, 128), F32)
        for other in range(nq):
            if other * fgroup // 128 == line:
                values = values + rgath[other]
        owners = jnp.broadcast_to(owner[line : line + 1, :], (8, 128))
        found = found + jnp.where(owners == mine, values, 0.0)
    column = jnp.broadcast_to(jnp.sum(found, axis=1, keepdims=True), (8, 128))
    diagonal = lax.broadcasted_iota(jnp.int32, (8, 128), 0) == lax.broadcasted_iota(
        jnp.int32, (8, 128), 1
    )
    line = jnp.sum(jnp.where(diagonal, column, 0.0), axis=0, keepdims=True)
    res_out[...] = line[:, :8]

    for copy in pending:
        copy.wait_send()
    for copy in copies:
        copy.wait()


CHUNKS = 2


def hand_out(field, residual, adjoint, field_out, residual_out, adjoint_out, held, in_sem, out_sem):
    residual_out[...] = residual[...]
    rows = held.shape[2] // CHUNKS
    loads, stores = [], []
    for k, (source, target) in enumerate(((field, field_out), (adjoint, adjoint_out))):
        for c in range(2 * CHUNKS):
            part = pl.ds((c // 2) * rows, rows)
            here = held.at[k, c % 2, part]
            loads.append(pltpu.make_async_copy(source.at[c % 2, part], here, in_sem.at[k, c]))
            stores.append(pltpu.make_async_copy(here, target.at[c % 2, part], out_sem.at[k, c]))
    for copy in loads:
        copy.start()
    for load, store in zip(loads, stores):
        load.wait()
        store.start()
    for store in stores:
        store.wait()


def per_device(
    nz,
    excitation,
    near_blocks,
    source_basis,
    target_basis,
    coupling,
    pair_rank,
    far_link,
    focal_kernel,
    focal_target,
    focal_owner,
):
    nt = lax.axis_size("tile")
    ns = lax.axis_size("src")
    nq = nt // nz
    focal_count = focal_target.shape[0]
    group = nz * PAIR
    spread = nq * PAIR
    fgroup = nz * 8
    width = 2 * TILE
    most = max(nz, nq)
    lines = (focal_count + 127) // 128
    wanted = jnp.pad(focal_target, (0, lines * 128 - focal_count))
    owner = jnp.pad(focal_owner, (0, lines * 128 - focal_count), constant_values=-1)
    vmem = pl.BlockSpec(memory_space=pltpu.VMEM)
    anywhere = pl.BlockSpec(memory_space=pl.ANY)
    dma = pltpu.SemaphoreType.DMA
    both = 2 * ROWS
    field, residual, adjoint = pl.pallas_call(
        functools.partial(kernel, nz, nq, ns),
        out_shape=(
            jax.ShapeDtypeStruct((2, ROWS, width), F32),
            jax.ShapeDtypeStruct((1, 8), F32),
            jax.ShapeDtypeStruct((2, ROWS, width), F32),
        ),
        in_specs=[anywhere] * 10,
        out_specs=(anywhere, vmem, anywhere),
        scratch_shapes=[
            pltpu.VMEM((both, width), F32),
            pltpu.VMEM((both, width), F32),
            pltpu.VMEM((2, 3, 2, TILE, TILE), BF16),
            pltpu.VMEM((2, focal_count, width), BF16),
            pltpu.VMEM((2, PAIR, TILE), BF16),
            pltpu.VMEM((2, PAIR, TILE), BF16),
            pltpu.VMEM((2, PAIR, nq * group), BF16),
            pltpu.VMEM((2, 2 * nt), jnp.int32),
            pltpu.VMEM((2, 2 * nt), jnp.int32),
            pltpu.VMEM((lines, 128), F32),
            pltpu.VMEM((lines, 128), jnp.int32),
            pltpu.VMEM((4, both, width), BF16),
            pltpu.VMEM((2, 2, both, TILE), BF16),
            pltpu.VMEM((both, width), F32),
            pltpu.VMEM((nq, PAIR, group), BF16),
            pltpu.VMEM((2, spread, group), BF16),
            pltpu.VMEM((2, group, spread), BF16),
            pltpu.VMEM((3, most * PAIR, both), BF16),
            pltpu.VMEM((3, most * PAIR, both), BF16),
            pltpu.VMEM((3, most, PAIR, both), BF16),
            pltpu.VMEM((focal_count, both), BF16),
            pltpu.VMEM((nq, fgroup, both), BF16),
            pltpu.VMEM((fgroup, both), BF16),
            pltpu.VMEM((nz, fgroup, both), BF16),
            pltpu.VMEM((8, 128), F32),
            pltpu.VMEM((ns, 8, 128), F32),
            pltpu.VMEM((focal_count, both), BF16),
            pltpu.VMEM((both, focal_count), BF16),
            pltpu.VMEM((8, 128), F32),
            pltpu.VMEM((nq, 8, 128), F32),
            pltpu.VMEM((2, both, TILE), BF16),
            pltpu.VMEM((2, both, TILE), BF16),
            dma((25,)),
            dma((2, 2, 2)),
            dma((2, 2, 2)),
            dma((nq,)),
            dma((nq,)),
            dma((3, 2, most)),
            dma((3, 2, most)),
            dma((3, 2, most)),
            dma((3, 2, most)),
            dma((2, nq)),
            dma((2, nq)),
            dma((2, nz)),
            dma((2, nz)),
            dma((ns,)),
            dma((ns,)),
            dma((nq,)),
            dma((nq,)),
            dma((nq,)),
            dma((nq,)),
            dma((nq,)),
            dma((nq,)),
            dma((2,)),
            dma((2,)),
        ],
        compiler_params=pltpu.CompilerParams(
            collective_id=0, has_side_effects=True, vmem_limit_bytes=56 * 1024 * 1024
        ),
    )(
        excitation,
        near_blocks,
        source_basis.reshape(2, PAIR, TILE),
        target_basis.reshape(2, PAIR, TILE),
        jnp.swapaxes(coupling, 1, 2),
        pair_rank.T,
        far_link.T,
        focal_kernel,
        wanted.reshape(lines, 128),
        owner.reshape(lines, 128),
    )
    field, residual, adjoint = pl.pallas_call(
        hand_out,
        out_shape=(
            jax.ShapeDtypeStruct((2, ROWS, width), F32),
            jax.ShapeDtypeStruct((1, 8), F32),
            jax.ShapeDtypeStruct((2, ROWS, width), F32),
        ),
        in_specs=[anywhere, vmem, anywhere],
        out_specs=[anywhere, vmem, anywhere],
        scratch_shapes=[
            pltpu.VMEM((2, 2, ROWS, width), F32),
            dma((2, 2 * CHUNKS)),
            dma((2, 2 * CHUNKS)),
        ],
        compiler_params=pltpu.CompilerParams(vmem_limit_bytes=56 * 1024 * 1024),
    )(field, residual, adjoint)
    return (
        field,
        residual.reshape(8),
        adjoint,
    )


def solution(mesh):
    nt = mesh.shape["tile"]
    nz = 8 if nt % 8 == 0 and nt > 8 else 2
    return jax.shard_map(
        functools.partial(per_device, nz),
        mesh=mesh,
        in_specs=(
            P(None, "src", "tile"),
            P("tile", None, None, None, None),
            P("tile", None, None, None),
            P("tile", None, None, None),
            P(None, None, "tile"),
            P(None, "tile"),
            P(None, "tile"),
            P(None, None, "tile"),
            P(),
            P(),
        ),
        out_specs=(P(None, "src", "tile"), P("tile"), P(None, "src", "tile")),
        check_vma=False,
    )
```

```python
import functools

import jax
import jax.numpy as jnp
from jax import lax
from jax.experimental import pallas as pl
from jax.experimental.pallas import tpu as pltpu
from jax.sharding import PartitionSpec as P

TILE = 512
RANK = 24
PAIR = 2 * RANK
ROWS = 128
DAMPING = 0.8
HALF = 256
F32 = jnp.float32
BF16 = jnp.bfloat16


def dot(left, right):
    return lax.dot_general(left, right, (((1,), (0,)), ((), ())), preferred_element_type=F32)


def dot_nt(left, right):
    return lax.dot_general(left, right, (((1,), (1,)), ((), ())), preferred_element_type=F32)


def rows_joined(by_re, by_im):
    shape = by_re.shape
    blocks = (shape[0] // ROWS, 2, ROWS // 2, shape[1])
    by_re, by_im = by_re.reshape(blocks), by_im.reshape(blocks)
    re = by_re[:, 0] - by_im[:, 1]
    im = by_re[:, 1] + by_im[:, 0]
    return jnp.stack([re, im], axis=1).reshape(shape)


def turned(x):
    lane = lax.broadcasted_iota(jnp.int32, (1, ROWS), 1)
    sign = jnp.where(lane < ROWS // 2, -1.0, 1.0)
    blocks = [
        pltpu.roll(x[:, k : k + ROWS], ROWS // 2, 1) * sign for k in range(0, x.shape[1], ROWS)
    ]
    return blocks[0] if len(blocks) == 1 else jnp.concatenate(blocks, axis=1)


def lanes_joined(by_re, by_im):
    return by_re + turned(by_im)


def half_of(h):
    return slice(0, 2 * ROWS) if h is None else slice(h * ROWS, (h + 1) * ROWS)


def aligned(start, size, unit):
    return pl.ds(pl.multiple_of(start, unit), size)


def kernel(
    nz,
    nq,
    ns,
    exc_hbm,
    near_hbm,
    sbasis_hbm,
    tbasis_hbm,
    coup_hbm,
    rank_hbm,
    link_hbm,
    fk_hbm,
    target_hbm,
    owner_hbm,
    field_out,
    res_out,
    adj_out,
    field,
    adjoint,
    near,
    fk,
    sbasis,
    tbasis,
    coup,
    rank,
    link,
    target,
    owner,
    vb,
    halo,
    nacc,
    mt_send,
    mt,
    mback,
    gath,
    part,
    parts_in,
    fsend,
    fparts,
    fz,
    fzparts,
    isum,
    iparts,
    wg,
    wt,
    rrow,
    rgath,
    edge_send,
    edge_in,
    seen,
    seen_own,
    local_sem,
    s_halo,
    r_halo,
    s_mt,
    r_mt,
    s_gath,
    r_gath,
    s_part,
    r_part,
    s_f,
    r_f,
    s_fz,
    r_fz,
    s_i,
    r_i,
    s_sib,
    r_sib,
    s_seen,
    r_seen,
    s_pass,
    r_pass,
    s_wg,
    r_wg,
    s_rr,
    r_rr,
    s_edge,
    r_edge,
):
    t = lax.axis_index("tile")
    s = lax.axis_index("src")
    nt = nz * nq
    q = t // nz
    z = t - q * nz
    tiles = 2 * nt
    group = nz * PAIR
    spread = nq * PAIR
    fgroup = nz * 8
    focal_count = nt * 8

    def z_peer(d):
        return q * nz + lax.rem(z + d, nz)

    def q_peer(d):
        return lax.rem(q + d, nq) * nz + z

    left = lax.rem(t + nt - 1, nt)
    right = lax.rem(t + 1, nt)

    barrier = pltpu.get_barrier_semaphore()
    count = 0
    for d in range(1, nq):
        pl.semaphore_signal(barrier, inc=1, device_id={"tile": q_peer(d), "src": s})
        count += 1
    for other in (left, right):
        pl.semaphore_signal(barrier, inc=1, device_id={"tile": other, "src": s})
        count += 1
    for d in range(1, nz):
        pl.semaphore_signal(barrier, inc=1, device_id={"tile": z_peer(d), "src": s})
        count += 1
    for e in range(1, ns):
        pl.semaphore_signal(barrier, inc=1, device_id={"tile": t, "src": lax.rem(s + e, ns)})
        count += 1
    core = lax.rem(s, 2)
    sibling = s + 1 - 2 * core

    half = ROWS // 2
    loads = {}
    for k, (name, source, place) in enumerate(
        (
            *(
                (
                    ("exc", h, c),
                    exc_hbm.at[c, h * half : (h + 1) * half],
                    vb.at[0, (2 * h + c) * half : (2 * h + c + 1) * half],
                )
                for h in range(2)
                for c in range(2)
            ),
            ("sbasis", sbasis_hbm, sbasis),
            ("rank", rank_hbm, rank),
            ("link", link_hbm, link),
            ("coup", coup_hbm, coup),
            ("near", near_hbm, near),
            ("tbasis", tbasis_hbm, tbasis),
            ("fk", fk_hbm, fk),
            ("target", target_hbm, target),
            ("owner", owner_hbm, owner),
        )
    ):
        loads[name] = pltpu.make_async_copy(source, place, local_sem.at[k])
        if name in ("exc", "sbasis", "rank", "link", "coup") or name[0] == "exc":
            loads[name].start()

    pending = []

    def send(src_ref, dst_ref, send_sem, recv_sem, tile=None, src=None):
        copy = pltpu.make_async_remote_copy(
            src_ref=src_ref,
            dst_ref=dst_ref,
            send_sem=send_sem,
            recv_sem=recv_sem,
            device_id={"tile": t if tile is None else tile, "src": s if src is None else src},
        )
        copy.start()
        pending.append(copy)

    def arrived(ref, send_sem, recv_sem):
        pltpu.make_async_remote_copy(
            src_ref=ref,
            dst_ref=ref,
            send_sem=send_sem,
            recv_sem=recv_sem,
            device_id={"tile": right, "src": s},
        ).wait_recv()

    def far_order(n):
        return sorted(range(1, n), key=lambda d: -min(d, n - d))

    def own_slice(index):
        return aligned(index * PAIR, PAIR, 16)

    def projected(x, basis):
        pieces = []
        for l in range(2):
            both = dot_nt(basis[l], x[:, l * TILE : (l + 1) * TILE])
            pieces.append(lanes_joined(both[:RANK], both[RANK:]))
        return jnp.concatenate(pieces, axis=0).astype(BF16)

    def gather(stage, h, value, along_z):
        n, mine = (nz, z) if along_z else (nq, q)
        lanes = half_of(h)
        here = gath.at[stage, own_slice(mine), lanes]
        gath[stage, own_slice(mine), lanes] = value
        for d in far_order(n):
            send(
                here,
                here,
                s_gath.at[stage, h or 0, d],
                r_gath.at[stage, h or 0, d],
                tile=z_peer(d) if along_z else q_peer(d),
            )

    def gathered(stage, h, along_z):
        n, mine = (nz, z) if along_z else (nq, q)
        for d in range(1, n):
            sender = lax.rem(mine + n - d, n)
            arrived(
                gath.at[stage, own_slice(sender), half_of(h)],
                s_gath.at[stage, h or 0, d],
                r_gath.at[stage, h or 0, d],
            )
        return gath[stage, : n * PAIR, half_of(h)]

    def scatter(stage, h, value, along_z):
        n, mine = (nz, z) if along_z else (nq, q)
        lanes = half_of(h)
        part[stage, :, lanes] = value.astype(BF16)
        for d in far_order(n):
            owner_of = lax.rem(mine + d, n)
            send(
                part.at[stage, own_slice(owner_of), lanes],
                parts_in.at[stage, d, :, lanes],
                s_part.at[stage, h or 0, d],
                r_part.at[stage, h or 0, d],
                tile=z_peer(d) if along_z else q_peer(d),
            )

    def scattered(stage, h, along_z):
        n, mine = (nz, z) if along_z else (nq, q)
        lanes = half_of(h)
        total = part[stage, own_slice(mine), lanes].astype(F32)
        for d in range(1, n):
            arrived(
                parts_in.at[stage, d, :, lanes],
                s_part.at[stage, h or 0, d],
                r_part.at[stage, h or 0, d],
            )
            total = total + parts_in[stage, d, :, lanes].astype(F32)
        return total.astype(BF16).astype(F32)

    def expanded(coefficients, basis, l):
        piece = coefficients[l * RANK : (l + 1) * RANK]
        stacked = jnp.concatenate([piece, turned(piece)], axis=0)
        return dot(jnp.transpose(stacked).astype(BF16), basis[l])

    def send_halo(stage, h):
        rows = half_of(h)
        send(
            vb.at[stage, rows, TILE : 2 * TILE],
            halo.at[stage, 0, rows],
            s_halo.at[stage, h, 0],
            r_halo.at[stage, h, 0],
            tile=right,
        )
        send(
            vb.at[stage, rows, 0:TILE],
            halo.at[stage, 1, rows],
            s_halo.at[stage, h, 1],
            r_halo.at[stage, h, 1],
            tile=left,
        )

    for h in range(2):
        for c in range(2):
            loads["exc", h, c].wait()
    loads["sbasis"].wait()
    loads["near"].start()
    first_coeff = projected(vb[0], sbasis)
    loads["rank"].wait()
    loads["link"].wait()

    level = lax.broadcasted_iota(jnp.int32, (RANK, tiles), 0)
    source_tile = lax.broadcasted_iota(jnp.int32, (1, tiles), 1)
    limits = []
    for l in range(2):
        gap = t * 2 + l - source_tile
        is_near = (
            (gap == 0)
            | (gap == 1)
            | (gap == -1)
            | (gap == tiles - 1)
            | (gap == 1 - tiles)
        )
        here = jnp.where((link[l : l + 1, :] == 1) & ~is_near, rank[l : l + 1, :], 0)
        wide = jnp.broadcast_to(here, (RANK, tiles))
        limits.append(jnp.where(level < wide, wide, 0).astype(F32))
    limits.append(
        jnp.broadcast_to(source_tile, (16, tiles)).astype(F32)
    )
    limit_rows = jnp.concatenate(limits, axis=0).astype(BF16)

    loads["coup"].wait()
    tile_row = lax.broadcasted_iota(jnp.int32, (tiles, group), 0)
    lane = lax.broadcasted_iota(jnp.int32, (tiles, group), 1)
    lane_row = lax.broadcasted_iota(jnp.int32, (1, group), 1)
    for d in far_order(nq) + [0]:
        to = lax.rem(q + d, nq)
        offset = lane - (tile_row - to * (2 * nz)) * RANK
        pick = jnp.where((offset >= 0) & (offset < RANK), 1.0, 0.0).astype(BF16)
        limit = dot(limit_rows, pick)
        position = (lane_row + to * group).astype(F32) - limit[PAIR : PAIR + 1, :] * float(RANK)
        keep = position < limit[:PAIR]
        for c in range(2) if d == 0 else (core,):
            block = coup[c, :, aligned(to * group, group, 128)]
            block = jnp.where(keep, block.astype(F32), 0.0).astype(BF16)
            if d == 0:
                mt[c, own_slice(q), :] = block
            else:
                mt_send[d] = block

    pl.semaphore_wait(barrier, count)

    for h in range(2):
        gather(0, h, first_coeff[:, half_of(h)], True)
    for d in far_order(nq):
        send(
            mt_send.at[d],
            mt.at[core, own_slice(q), :],
            s_mt.at[d],
            r_mt.at[d],
            tile=q_peer(d),
        )
    for h in range(2):
        send_halo(0, h)
    for name in ("tbasis", "fk", "target", "owner"):
        loads[name].start()

    def near_own(stage, h):
        rows = half_of(h)

        @pl.loop(0, 4)
        def _(step):
            i = step // 2
            cols = aligned((step % 2) * HALF, HALF, HALF)
            by_re = by_im = 0.0
            for l in range(2):
                x = vb[stage, rows, l * TILE : (l + 1) * TILE]
                by_re = by_re + dot(x, near[i, l - i + 1, 0, :, cols])
                by_im = by_im + dot(x, near[i, l - i + 1, 1, :, cols])
            nacc[rows, aligned(step * HALF, HALF, HALF)] = rows_joined(by_re, by_im)

    def near_halo(stage, h):
        rows = half_of(h)
        for side in range(2):
            arrived(
                halo.at[stage, side, rows],
                s_halo.at[stage, h, side],
                r_halo.at[stage, h, side],
            )

        @pl.loop(0, 4)
        def _(step):
            i = step // 2
            cols = aligned((step % 2) * HALF, HALF, HALF)
            x = halo[stage, i, rows]
            by_re = dot(x, near[i, 2 * i, 0, :, cols])
            by_im = dot(x, near[i, 2 * i, 1, :, cols])
            out = aligned(step * HALF, HALF, HALF)
            nacc[rows, out] = nacc[rows, out] + rows_joined(by_re, by_im)

    def couple(stage, h):
        coefficients = gathered(stage, h, True)
        scatter(
            stage, h, lanes_joined(dot(mt[0], coefficients), dot(mt[1], coefficients)), False
        )

    def updated(stage, h):
        near_halo(stage, h)
        coupled = scattered(stage, h, False)
        rows = half_of(h)
        for l in range(2):
            cols = slice(l * TILE, (l + 1) * TILE)
            added = nacc[rows, cols] + expanded(coupled, tbasis, l)
            right_side = vb[0, rows, cols].astype(F32)
            if stage == 0:
                value = right_side - DAMPING * added
            else:
                before = field[rows, cols]
                value = before + DAMPING * (right_side - (before + added))
            field[rows, cols] = value
            vb[stage + 1, rows, cols] = value.astype(BF16)

    loads["near"].wait()
    near_own(0, None)
    for d in range(1, nq):
        here = mt.at[core, own_slice(lax.rem(q + nq - d, nq)), :]
        arrived(here, s_mt.at[d], r_mt.at[d])
        send(here, here, s_sib.at[d], r_sib.at[d], src=sibling)
    for d in range(1, nq):
        here = mt.at[1 - core, own_slice(lax.rem(q + nq - d, nq)), :]
        arrived(here, s_sib.at[d], r_sib.at[d])
    for h in range(2):
        couple(0, h)
    for c in range(2):
        mback[c] = jnp.transpose(mt[c].astype(F32)).astype(BF16)
    loads["tbasis"].wait()
    for h in range(2):
        updated(0, h)
        gather(1, h, projected(vb[1, half_of(h)], sbasis), True)
        send_halo(1, h)
    for h in range(2):
        near_own(1, h)
        couple(1, h)
    loads["fk"].wait()
    for l in range(2):
        cols = slice(l * TILE, (l + 1) * TILE)
        by_re = dot_nt(tbasis[l], fk[0, :, cols])
        by_im = dot_nt(tbasis[l], fk[1, :, cols])
        seen_own[0, l * RANK : (l + 1) * RANK] = by_re[:RANK] - by_im[RANK:]
        seen_own[1, l * RANK : (l + 1) * RANK] = by_im[:RANK] + by_re[RANK:]
    seen[:, own_slice(q), :] = seen_own[...].astype(BF16)
    for d in far_order(nq):
        here = seen.at[core, own_slice(q), :]
        send(here, here, s_seen.at[d], r_seen.at[d], tile=q_peer(d))
    copies = []

    def f_rows(index):
        return aligned(index * fgroup, fgroup, 16)

    for h in range(2):
        updated(1, h)
        for c in range(2):
            copy = pltpu.make_async_copy(
                field.at[(2 * h + c) * half : (2 * h + c + 1) * half],
                field_out.at[c, h * half : (h + 1) * half],
                local_sem.at[13 + 2 * h + c],
            )
            copy.start()
            copies.append(copy)
        lanes = half_of(h)
        x = vb[2, lanes]
        fsend[:, lanes] = lanes_joined(dot_nt(fk[0], x), dot_nt(fk[1], x)).astype(BF16)
        for d in far_order(nq):
            send(
                fsend.at[f_rows(lax.rem(q + d, nq)), lanes],
                fparts.at[d, :, lanes],
                s_f.at[h, d],
                r_f.at[h, d],
                tile=q_peer(d),
            )
    for h in range(2):
        lanes = half_of(h)
        total = fsend[f_rows(q), lanes].astype(F32)
        for d in range(1, nq):
            arrived(fparts.at[d, :, lanes], s_f.at[h, d], r_f.at[h, d])
            total = total + fparts[d, :, lanes].astype(F32)
        fz[:, lanes] = total.astype(BF16)
        for d in far_order(nz):
            send(
                fz.at[:, lanes],
                fzparts.at[d, :, lanes],
                s_fz.at[h, d],
                r_fz.at[h, d],
                tile=z_peer(d),
            )
    for d in range(1, nq):
        here = seen.at[core, own_slice(lax.rem(q + nq - d, nq)), :]
        arrived(here, s_seen.at[d], r_seen.at[d])
        send(here, here, s_pass.at[d], r_pass.at[d], src=sibling)
    row = lax.broadcasted_iota(jnp.int32, (fgroup, 128), 0)
    lane128 = lax.broadcasted_iota(jnp.int32, (fgroup, 128), 1)
    shift = lax.rem(q * fgroup, 128)
    diagonal = lane128 == row + shift
    loads["target"].wait()
    wanted = target[pl.ds(q * fgroup // 128, 1), :]
    focal = fz[...].astype(F32)
    for d in range(1, nz):
        for h in range(2):
            arrived(fzparts.at[d, :, half_of(h)], s_fz.at[h, d], r_fz.at[h, d])
        focal = focal + fzparts[d].astype(F32)
    square = focal * focal
    strength = jnp.sum(square[:, :ROWS] + square[:, ROWS:], axis=1, keepdims=True)
    line = jnp.sum(jnp.where(diagonal, strength, 0.0), axis=0, keepdims=True)
    isum[...] = jnp.broadcast_to(line, (8, 128))
    for e in far_order(ns):
        send(isum, iparts.at[e], s_i.at[e], r_i.at[e], src=lax.rem(s + e, ns))
    strength = line
    for e in range(1, ns):
        arrived(iparts.at[e], s_i.at[e], r_i.at[e])
        strength = strength + iparts[e, :1, :]
    in_line = lane128[:1] - shift
    in_line = (in_line >= 0) & (in_line < fgroup)
    flat = jnp.where(in_line, jnp.tanh(strength / (2.0 * ROWS * ns)) - wanted, 0.0)
    residual = jnp.sum(jnp.where(diagonal, flat, 0.0), axis=1, keepdims=True)
    f16 = aligned(q * fgroup, fgroup, 16)
    sign = jnp.where(lane128[:1] < ROWS // 2, 1.0, -1.0)
    sign = jnp.concatenate([sign, sign], axis=1)
    wg[f16, :] = (residual * focal * sign).astype(BF16)
    for d in far_order(nq):
        here = wg.at[f16]
        send(here, here, s_wg.at[d], r_wg.at[d], tile=q_peer(d))
    rrow[...] = jnp.broadcast_to(flat, (8, 128))
    rgath[q] = jnp.broadcast_to(flat, (8, 128))
    for d in far_order(nq):
        send(rrow, rgath.at[q], s_rr.at[d], r_rr.at[d], tile=q_peer(d))
    for d in range(1, nq):
        sender = lax.rem(q + nq - d, nq)
        arrived(wg.at[aligned(sender * fgroup, fgroup, 16)], s_wg.at[d], r_wg.at[d])
    wt[...] = jnp.transpose(wg[...].astype(F32)).astype(BF16)

    scale = float(tiles * TILE / focal_count) ** 0.5

    for i in range(2):
        w = wt[...]
        for k in range(2):
            cols = slice((2 * i + k) * HALF, (2 * i + k + 1) * HALF)
            u = rows_joined(dot(w, fk[0, :, cols]), dot(w, fk[1, :, cols])) * scale
            adjoint[:, cols] = u
            vb[3, :, cols] = u.astype(BF16)
        x = vb[3, :, i * TILE : (i + 1) * TILE]
        by_re = dot_nt(x, near[i, 2 * i, 0])
        by_im = dot_nt(x, near[i, 2 * i, 1])
        edge_send[i] = rows_joined(by_re, by_im).astype(BF16)
        send(
            edge_send.at[i],
            edge_in.at[1 - i],
            s_edge.at[i],
            r_edge.at[1 - i],
            tile=right if i else left,
        )

    for d in range(1, nq):
        here = seen.at[1 - core, own_slice(lax.rem(q + nq - d, nq)), :]
        arrived(here, s_pass.at[d], r_pass.at[d])
    w = wg[...]
    coefficients = (lanes_joined(dot(seen[0], w), dot(seen[1], w)) * scale).astype(BF16)
    scatter(
        2,
        None,
        lanes_joined(dot(mback[0], coefficients), dot(mback[1], coefficients)),
        True,
    )

    @pl.loop(0, 4)
    def _(step):
        m = step // 2
        half = aligned((step % 2) * HALF, HALF, HALF)
        by_re = jnp.zeros((2 * ROWS, HALF), F32)
        by_im = jnp.zeros((2 * ROWS, HALF), F32)
        for i in range(2):
            x = vb[3, :, i * TILE : (i + 1) * TILE]
            by_re = by_re + dot_nt(x, near[i, m - i + 1, 0, half, :])
            by_im = by_im + dot_nt(x, near[i, m - i + 1, 1, half, :])
        nacc[:, aligned(step * HALF, HALF, HALF)] = rows_joined(by_re, by_im)

    for side in range(2):
        arrived(edge_in.at[side], s_edge.at[side], r_edge.at[side])
    back = scattered(2, None, True)
    for l in range(2):
        cols = slice(l * TILE, (l + 1) * TILE)
        added = nacc[:, cols] + edge_in[l].astype(F32) + expanded(back, sbasis, l)
        adjoint[:, cols] = adjoint[:, cols] - DAMPING * added
        for k in range(4):
            copy = pltpu.make_async_copy(
                adjoint.at[k * half : (k + 1) * half, cols],
                adj_out.at[k % 2, (k // 2) * half : (k // 2 + 1) * half, cols],
                local_sem.at[17 + 4 * l + k],
            )
            copy.start()
            copies.append(copy)

    lines = (focal_count + 127) // 128
    for d in range(1, nq):
        sender = lax.rem(q + nq - d, nq)
        arrived(rgath.at[sender], s_rr.at[d], r_rr.at[d])
    loads["owner"].wait()
    mine = lax.broadcasted_iota(jnp.int32, (8, 128), 0) + t * 8
    found = jnp.zeros((8, 128), F32)
    for line in range(lines):
        values = jnp.zeros((8, 128), F32)
        for other in range(nq):
            if other * fgroup // 128 == line:
                values = values + rgath[other]
        owners = jnp.broadcast_to(owner[line : line + 1, :], (8, 128))
        found = found + jnp.where(owners == mine, values, 0.0)
    column = jnp.broadcast_to(jnp.sum(found, axis=1, keepdims=True), (8, 128))
    diagonal = lax.broadcasted_iota(jnp.int32, (8, 128), 0) == lax.broadcasted_iota(
        jnp.int32, (8, 128), 1
    )
    line = jnp.sum(jnp.where(diagonal, column, 0.0), axis=0, keepdims=True)
    res_out[...] = line[:, :8]

    for copy in pending:
        copy.wait_send()
    for copy in copies:
        copy.wait()


CHUNKS = 2


def hand_out(field, residual, adjoint, field_out, residual_out, adjoint_out, held, in_sem, out_sem):
    residual_out[...] = residual[...]
    rows = held.shape[2] // CHUNKS
    loads, stores = [], []
    for k, (source, target) in enumerate(((field, field_out), (adjoint, adjoint_out))):
        for c in range(2 * CHUNKS):
            part = pl.ds((c // 2) * rows, rows)
            here = held.at[k, c % 2, part]
            loads.append(pltpu.make_async_copy(source.at[c % 2, part], here, in_sem.at[k, c]))
            stores.append(pltpu.make_async_copy(here, target.at[c % 2, part], out_sem.at[k, c]))
    for copy in loads:
        copy.start()
    for load, store in zip(loads, stores):
        load.wait()
        store.start()
    for store in stores:
        store.wait()


def per_device(
    nz,
    excitation,
    near_blocks,
    source_basis,
    target_basis,
    coupling,
    pair_rank,
    far_link,
    focal_kernel,
    focal_target,
    focal_owner,
):
    nt = lax.axis_size("tile")
    ns = lax.axis_size("src")
    nq = nt // nz
    focal_count = focal_target.shape[0]
    group = nz * PAIR
    spread = nq * PAIR
    fgroup = nz * 8
    width = 2 * TILE
    most = max(nz, nq)
    lines = (focal_count + 127) // 128
    wanted = jnp.pad(focal_target, (0, lines * 128 - focal_count))
    owner = jnp.pad(focal_owner, (0, lines * 128 - focal_count), constant_values=-1)
    vmem = pl.BlockSpec(memory_space=pltpu.VMEM)
    anywhere = pl.BlockSpec(memory_space=pl.ANY)
    dma = pltpu.SemaphoreType.DMA
    both = 2 * ROWS
    field, residual, adjoint = pl.pallas_call(
        functools.partial(kernel, nz, nq, ns),
        out_shape=(
            jax.ShapeDtypeStruct((2, ROWS, width), F32),
            jax.ShapeDtypeStruct((1, 8), F32),
            jax.ShapeDtypeStruct((2, ROWS, width), F32),
        ),
        in_specs=[anywhere] * 10,
        out_specs=(anywhere, vmem, anywhere),
        scratch_shapes=[
            pltpu.VMEM((both, width), F32),
            pltpu.VMEM((both, width), F32),
            pltpu.VMEM((2, 3, 2, TILE, TILE), BF16),
            pltpu.VMEM((2, focal_count, width), BF16),
            pltpu.VMEM((2, PAIR, TILE), BF16),
            pltpu.VMEM((2, PAIR, TILE), BF16),
            pltpu.VMEM((2, PAIR, nq * group), BF16),
            pltpu.VMEM((2, 2 * nt), jnp.int32),
            pltpu.VMEM((2, 2 * nt), jnp.int32),
            pltpu.VMEM((lines, 128), F32),
            pltpu.VMEM((lines, 128), jnp.int32),
            pltpu.VMEM((4, both, width), BF16),
            pltpu.VMEM((2, 2, both, TILE), BF16),
            pltpu.VMEM((both, width), F32),
            pltpu.VMEM((nq, PAIR, group), BF16),
            pltpu.VMEM((2, spread, group), BF16),
            pltpu.VMEM((2, group, spread), BF16),
            pltpu.VMEM((3, most * PAIR, both), BF16),
            pltpu.VMEM((3, most * PAIR, both), BF16),
            pltpu.VMEM((3, most, PAIR, both), BF16),
            pltpu.VMEM((focal_count, both), BF16),
            pltpu.VMEM((nq, fgroup, both), BF16),
            pltpu.VMEM((fgroup, both), BF16),
            pltpu.VMEM((nz, fgroup, both), BF16),
            pltpu.VMEM((8, 128), F32),
            pltpu.VMEM((ns, 8, 128), F32),
            pltpu.VMEM((focal_count, both), BF16),
            pltpu.VMEM((both, focal_count), BF16),
            pltpu.VMEM((8, 128), F32),
            pltpu.VMEM((nq, 8, 128), F32),
            pltpu.VMEM((2, both, TILE), BF16),
            pltpu.VMEM((2, both, TILE), BF16),
            pltpu.VMEM((2, spread, focal_count), BF16),
            pltpu.VMEM((2, PAIR, focal_count), F32),
            dma((25,)),
            dma((2, 2, 2)),
            dma((2, 2, 2)),
            dma((nq,)),
            dma((nq,)),
            dma((3, 2, most)),
            dma((3, 2, most)),
            dma((3, 2, most)),
            dma((3, 2, most)),
            dma((2, nq)),
            dma((2, nq)),
            dma((2, nz)),
            dma((2, nz)),
            dma((ns,)),
            dma((ns,)),
            dma((nq,)),
            dma((nq,)),
            dma((nq,)),
            dma((nq,)),
            dma((nq,)),
            dma((nq,)),
            dma((nq,)),
            dma((nq,)),
            dma((nq,)),
            dma((nq,)),
            dma((2,)),
            dma((2,)),
        ],
        compiler_params=pltpu.CompilerParams(
            collective_id=0, has_side_effects=True, vmem_limit_bytes=56 * 1024 * 1024
        ),
    )(
        excitation,
        near_blocks,
        source_basis.reshape(2, PAIR, TILE),
        target_basis.reshape(2, PAIR, TILE),
        jnp.swapaxes(coupling, 1, 2),
        pair_rank.T,
        far_link.T,
        focal_kernel,
        wanted.reshape(lines, 128),
        owner.reshape(lines, 128),
    )
    field, residual, adjoint = pl.pallas_call(
        hand_out,
        out_shape=(
            jax.ShapeDtypeStruct((2, ROWS, width), F32),
            jax.ShapeDtypeStruct((1, 8), F32),
            jax.ShapeDtypeStruct((2, ROWS, width), F32),
        ),
        in_specs=[anywhere, vmem, anywhere],
        out_specs=[anywhere, vmem, anywhere],
        scratch_shapes=[
            pltpu.VMEM((2, 2, ROWS, width), F32),
            dma((2, 2 * CHUNKS)),
            dma((2, 2 * CHUNKS)),
        ],
        compiler_params=pltpu.CompilerParams(vmem_limit_bytes=56 * 1024 * 1024),
    )(field, residual, adjoint)
    return (
        field,
        residual.reshape(8),
        adjoint,
    )


def solution(mesh):
    nt = mesh.shape["tile"]
    nz = 8 if nt % 8 == 0 and nt > 8 else 2
    return jax.shard_map(
        functools.partial(per_device, nz),
        mesh=mesh,
        in_specs=(
            P(None, "src", "tile"),
            P("tile", None, None, None, None),
            P("tile", None, None, None),
            P("tile", None, None, None),
            P(None, None, "tile"),
            P(None, "tile"),
            P(None, "tile"),
            P(None, None, "tile"),
            P(),
            P(),
        ),
        out_specs=(P(None, "src", "tile"), P("tile"), P(None, "src", "tile")),
        check_vma=False,
    )
```

```python
import functools

import jax
import jax.numpy as jnp
from jax import lax
from jax.experimental import pallas as pl
from jax.experimental.pallas import tpu as pltpu
from jax.sharding import PartitionSpec as P

TILE = 512
RANK = 24
PAIR = 2 * RANK
ROWS = 128
DAMPING = 0.8
HALF = 256
F32 = jnp.float32
BF16 = jnp.bfloat16


def dot(left, right):
    return lax.dot_general(left, right, (((1,), (0,)), ((), ())), preferred_element_type=F32)


def dot_nt(left, right):
    return lax.dot_general(left, right, (((1,), (1,)), ((), ())), preferred_element_type=F32)


def rows_joined(by_re, by_im):
    shape = by_re.shape
    blocks = (shape[0] // ROWS, 2, ROWS // 2, shape[1])
    by_re, by_im = by_re.reshape(blocks), by_im.reshape(blocks)
    re = by_re[:, 0] - by_im[:, 1]
    im = by_re[:, 1] + by_im[:, 0]
    return jnp.stack([re, im], axis=1).reshape(shape)


def turned(x):
    lane = lax.broadcasted_iota(jnp.int32, (1, ROWS), 1)
    sign = jnp.where(lane < ROWS // 2, -1.0, 1.0)
    blocks = [
        pltpu.roll(x[:, k : k + ROWS], ROWS // 2, 1) * sign for k in range(0, x.shape[1], ROWS)
    ]
    return blocks[0] if len(blocks) == 1 else jnp.concatenate(blocks, axis=1)


def lanes_joined(by_re, by_im):
    return by_re + turned(by_im)


def half_of(h):
    return slice(0, 2 * ROWS) if h is None else slice(h * ROWS, (h + 1) * ROWS)


def aligned(start, size, unit):
    return pl.ds(pl.multiple_of(start, unit), size)


def kernel(
    nz,
    nq,
    ns,
    exc_hbm,
    near_hbm,
    sbasis_hbm,
    tbasis_hbm,
    coup_hbm,
    rank_hbm,
    link_hbm,
    fk_hbm,
    target_hbm,
    owner_hbm,
    field_out,
    res_out,
    adj_out,
    field,
    adjoint,
    near,
    fk,
    sbasis,
    tbasis,
    coup,
    rank,
    link,
    target,
    owner,
    vb,
    halo,
    nacc,
    mt_send,
    mt,
    mback,
    gath,
    part,
    parts_in,
    fsend,
    fparts,
    fz,
    fzparts,
    isum,
    iparts,
    wg,
    wt,
    rrow,
    rgath,
    edge_send,
    edge_in,
    seen,
    seen_own,
    local_sem,
    s_halo,
    r_halo,
    s_mt,
    r_mt,
    s_gath,
    r_gath,
    s_part,
    r_part,
    s_f,
    r_f,
    s_fz,
    r_fz,
    s_i,
    r_i,
    s_sib,
    r_sib,
    s_seen,
    r_seen,
    s_pass,
    r_pass,
    s_wg,
    r_wg,
    s_rr,
    r_rr,
    s_edge,
    r_edge,
    s_over,
    r_over,
):
    t = lax.axis_index("tile")
    s = lax.axis_index("src")
    nt = nz * nq
    q = t // nz
    z = t - q * nz
    tiles = 2 * nt
    group = nz * PAIR
    spread = nq * PAIR
    fgroup = nz * 8
    focal_count = nt * 8

    def z_peer(d):
        return q * nz + lax.rem(z + d, nz)

    def q_peer(d):
        return lax.rem(q + d, nq) * nz + z

    left = lax.rem(t + nt - 1, nt)
    right = lax.rem(t + 1, nt)

    barrier = pltpu.get_barrier_semaphore()
    count = 0
    for d in range(1, nq):
        pl.semaphore_signal(barrier, inc=1, device_id={"tile": q_peer(d), "src": s})
        count += 1
    for other in (left, right):
        pl.semaphore_signal(barrier, inc=1, device_id={"tile": other, "src": s})
        count += 1
    for d in range(1, nz):
        pl.semaphore_signal(barrier, inc=1, device_id={"tile": z_peer(d), "src": s})
        count += 1
    for e in range(1, ns):
        pl.semaphore_signal(barrier, inc=1, device_id={"tile": t, "src": lax.rem(s + e, ns)})
        count += 1
    core = lax.rem(s, 2)
    sibling = s + 1 - 2 * core

    half = ROWS // 2
    loads = {}
    for k, (name, source, place) in enumerate(
        (
            *(
                (
                    ("exc", h, c),
                    exc_hbm.at[c, h * half : (h + 1) * half],
                    vb.at[0, (2 * h + c) * half : (2 * h + c + 1) * half],
                )
                for h in range(2)
                for c in range(2)
            ),
            ("sbasis", sbasis_hbm, sbasis),
            ("rank", rank_hbm, rank),
            ("link", link_hbm, link),
            ("coup", coup_hbm, coup),
            ("near", near_hbm, near),
            ("tbasis", tbasis_hbm, tbasis),
            ("fk", fk_hbm, fk),
            ("target", target_hbm, target),
            ("owner", owner_hbm, owner),
        )
    ):
        loads[name] = pltpu.make_async_copy(source, place, local_sem.at[k])
        if name in ("exc", "sbasis", "rank", "link", "coup") or name[0] == "exc":
            loads[name].start()

    pending = []

    def send(src_ref, dst_ref, send_sem, recv_sem, tile=None, src=None):
        copy = pltpu.make_async_remote_copy(
            src_ref=src_ref,
            dst_ref=dst_ref,
            send_sem=send_sem,
            recv_sem=recv_sem,
            device_id={"tile": t if tile is None else tile, "src": s if src is None else src},
        )
        copy.start()
        pending.append(copy)

    def arrived(ref, send_sem, recv_sem):
        pltpu.make_async_remote_copy(
            src_ref=ref,
            dst_ref=ref,
            send_sem=send_sem,
            recv_sem=recv_sem,
            device_id={"tile": right, "src": s},
        ).wait_recv()

    def far_order(n):
        return sorted(range(1, n), key=lambda d: -min(d, n - d))

    def own_slice(index):
        return aligned(index * PAIR, PAIR, 16)

    def projected(x, basis):
        pieces = []
        for l in range(2):
            both = dot_nt(basis[l], x[:, l * TILE : (l + 1) * TILE])
            pieces.append(lanes_joined(both[:RANK], both[RANK:]))
        return jnp.concatenate(pieces, axis=0).astype(BF16)

    def gather(stage, h, value, along_z):
        n, mine = (nz, z) if along_z else (nq, q)
        lanes = half_of(h)
        here = gath.at[stage, own_slice(mine), lanes]
        gath[stage, own_slice(mine), lanes] = value
        for d in far_order(n):
            send(
                here,
                here,
                s_gath.at[stage, h or 0, d],
                r_gath.at[stage, h or 0, d],
                tile=z_peer(d) if along_z else q_peer(d),
            )

    def gathered(stage, h, along_z):
        n, mine = (nz, z) if along_z else (nq, q)
        for d in range(1, n):
            sender = lax.rem(mine + n - d, n)
            arrived(
                gath.at[stage, own_slice(sender), half_of(h)],
                s_gath.at[stage, h or 0, d],
                r_gath.at[stage, h or 0, d],
            )
        return gath[stage, : n * PAIR, half_of(h)]

    def scatter(stage, h, value, along_z):
        n, mine = (nz, z) if along_z else (nq, q)
        lanes = half_of(h)
        part[stage, :, lanes] = value.astype(BF16)
        for d in far_order(n):
            owner_of = lax.rem(mine + d, n)
            send(
                part.at[stage, own_slice(owner_of), lanes],
                parts_in.at[stage, d, :, lanes],
                s_part.at[stage, h or 0, d],
                r_part.at[stage, h or 0, d],
                tile=z_peer(d) if along_z else q_peer(d),
            )

    def scattered(stage, h, along_z):
        n, mine = (nz, z) if along_z else (nq, q)
        lanes = half_of(h)
        total = part[stage, own_slice(mine), lanes].astype(F32)
        for d in range(1, n):
            arrived(
                parts_in.at[stage, d, :, lanes],
                s_part.at[stage, h or 0, d],
                r_part.at[stage, h or 0, d],
            )
            total = total + parts_in[stage, d, :, lanes].astype(F32)
        return total.astype(BF16).astype(F32)

    def expanded(coefficients, basis, l):
        piece = coefficients[l * RANK : (l + 1) * RANK]
        stacked = jnp.concatenate([piece, turned(piece)], axis=0)
        return dot(jnp.transpose(stacked).astype(BF16), basis[l])

    def send_halo(stage, h):
        rows = half_of(h)
        send(
            vb.at[stage, rows, TILE : 2 * TILE],
            halo.at[stage, 0, rows],
            s_halo.at[stage, h, 0],
            r_halo.at[stage, h, 0],
            tile=right,
        )
        send(
            vb.at[stage, rows, 0:TILE],
            halo.at[stage, 1, rows],
            s_halo.at[stage, h, 1],
            r_halo.at[stage, h, 1],
            tile=left,
        )

    for h in range(2):
        for c in range(2):
            loads["exc", h, c].wait()
    loads["sbasis"].wait()
    loads["near"].start()
    first_coeff = projected(vb[0], sbasis)
    loads["rank"].wait()
    loads["link"].wait()

    level = lax.broadcasted_iota(jnp.int32, (RANK, tiles), 0)
    source_tile = lax.broadcasted_iota(jnp.int32, (1, tiles), 1)
    limits = []
    for l in range(2):
        gap = t * 2 + l - source_tile
        is_near = (
            (gap == 0)
            | (gap == 1)
            | (gap == -1)
            | (gap == tiles - 1)
            | (gap == 1 - tiles)
        )
        here = jnp.where((link[l : l + 1, :] == 1) & ~is_near, rank[l : l + 1, :], 0)
        wide = jnp.broadcast_to(here, (RANK, tiles))
        limits.append(jnp.where(level < wide, wide, 0).astype(F32))
    limits.append(
        jnp.broadcast_to(source_tile, (16, tiles)).astype(F32)
    )
    limit_rows = jnp.concatenate(limits, axis=0).astype(BF16)

    loads["coup"].wait()
    tile_row = lax.broadcasted_iota(jnp.int32, (tiles, group), 0)
    lane = lax.broadcasted_iota(jnp.int32, (tiles, group), 1)
    lane_row = lax.broadcasted_iota(jnp.int32, (1, group), 1)
    for d in far_order(nq) + [0]:
        to = lax.rem(q + d, nq)
        offset = lane - (tile_row - to * (2 * nz)) * RANK
        pick = jnp.where((offset >= 0) & (offset < RANK), 1.0, 0.0).astype(BF16)
        limit = dot(limit_rows, pick)
        position = (lane_row + to * group).astype(F32) - limit[PAIR : PAIR + 1, :] * float(RANK)
        keep = position < limit[:PAIR]
        for c in range(2) if d == 0 else (core,):
            block = coup[c, :, aligned(to * group, group, 128)]
            block = jnp.where(keep, block.astype(F32), 0.0).astype(BF16)
            if d == 0:
                mt[c, own_slice(q), :] = block
            else:
                mt_send[d] = block

    pl.semaphore_wait(barrier, count)

    for h in range(2):
        gather(0, h, first_coeff[:, half_of(h)], True)
    for d in far_order(nq):
        send(
            mt_send.at[d],
            mt.at[core, own_slice(q), :],
            s_mt.at[d],
            r_mt.at[d],
            tile=q_peer(d),
        )
    for h in range(2):
        send_halo(0, h)
    for name in ("tbasis", "fk", "target", "owner"):
        loads[name].start()

    def near_own(stage, h):
        rows = half_of(h)

        @pl.loop(0, 4)
        def _(step):
            i = step // 2
            cols = aligned((step % 2) * HALF, HALF, HALF)
            by_re = by_im = 0.0
            for l in range(2):
                x = vb[stage, rows, l * TILE : (l + 1) * TILE]
                by_re = by_re + dot(x, near[i, l - i + 1, 0, :, cols])
                by_im = by_im + dot(x, near[i, l - i + 1, 1, :, cols])
            nacc[rows, aligned(step * HALF, HALF, HALF)] = rows_joined(by_re, by_im)

    def near_halo(stage, h):
        rows = half_of(h)
        for side in range(2):
            arrived(
                halo.at[stage, side, rows],
                s_halo.at[stage, h, side],
                r_halo.at[stage, h, side],
            )

        @pl.loop(0, 4)
        def _(step):
            i = step // 2
            cols = aligned((step % 2) * HALF, HALF, HALF)
            x = halo[stage, i, rows]
            by_re = dot(x, near[i, 2 * i, 0, :, cols])
            by_im = dot(x, near[i, 2 * i, 1, :, cols])
            out = aligned(step * HALF, HALF, HALF)
            nacc[rows, out] = nacc[rows, out] + rows_joined(by_re, by_im)

    def couple(stage, h):
        coefficients = gathered(stage, h, True)
        scatter(
            stage, h, lanes_joined(dot(mt[0], coefficients), dot(mt[1], coefficients)), False
        )

    def updated(stage, h):
        near_halo(stage, h)
        coupled = scattered(stage, h, False)
        rows = half_of(h)
        for l in range(2):
            cols = slice(l * TILE, (l + 1) * TILE)
            added = nacc[rows, cols] + expanded(coupled, tbasis, l)
            right_side = vb[0, rows, cols].astype(F32)
            if stage == 0:
                value = right_side - DAMPING * added
            else:
                before = field[rows, cols]
                value = before + DAMPING * (right_side - (before + added))
            field[rows, cols] = value
            vb[stage + 1, rows, cols] = value.astype(BF16)

    loads["near"].wait()
    near_own(0, None)
    for d in range(1, nq):
        here = mt.at[core, own_slice(lax.rem(q + nq - d, nq)), :]
        arrived(here, s_mt.at[d], r_mt.at[d])
        send(here, here, s_sib.at[d], r_sib.at[d], src=sibling)
    for d in range(1, nq):
        here = mt.at[1 - core, own_slice(lax.rem(q + nq - d, nq)), :]
        arrived(here, s_sib.at[d], r_sib.at[d])
    for h in range(2):
        couple(0, h)
    for c in range(2):
        mback[c] = jnp.transpose(mt[c].astype(F32)).astype(BF16)
    loads["tbasis"].wait()
    for h in range(2):
        updated(0, h)
        gather(1, h, projected(vb[1, half_of(h)], sbasis), True)
        send_halo(1, h)
    for h in range(2):
        near_own(1, h)
        couple(1, h)
    loads["fk"].wait()
    for l in range(2):
        cols = slice(l * TILE, (l + 1) * TILE)
        by_re = dot_nt(tbasis[l], fk[0, :, cols])
        by_im = dot_nt(tbasis[l], fk[1, :, cols])
        seen_own[0, l * RANK : (l + 1) * RANK] = by_re[:RANK] - by_im[RANK:]
        seen_own[1, l * RANK : (l + 1) * RANK] = by_im[:RANK] + by_re[RANK:]
    seen[:, own_slice(q), :] = seen_own[...].astype(BF16)
    flip = jnp.where(core == 0, -1.0, 1.0)

    @pl.loop(0, 4)
    def _(step):
        i = step // 2
        points = aligned((step % 2) * (focal_count // 2), focal_count // 2, 16)
        cols = aligned(i * TILE, TILE, TILE)
        edge_send[i, points, :] = (
            dot_nt(fk[0, points, cols], near[i, 2 * i, core])
            + flip * dot_nt(fk[1, points, cols], near[i, 2 * i, 1 - core])
        ).astype(BF16)

    copies = []

    def f_rows(index):
        return aligned(index * fgroup, fgroup, 16)

    for h in range(2):
        updated(1, h)
        for c in range(2):
            copy = pltpu.make_async_copy(
                field.at[(2 * h + c) * half : (2 * h + c + 1) * half],
                field_out.at[c, h * half : (h + 1) * half],
                local_sem.at[13 + 2 * h + c],
            )
            copy.start()
            copies.append(copy)
        lanes = half_of(h)
        x = vb[2, lanes]
        fsend[:, lanes] = lanes_joined(dot_nt(fk[0], x), dot_nt(fk[1], x)).astype(BF16)
        for d in far_order(nq):
            send(
                fsend.at[f_rows(lax.rem(q + d, nq)), lanes],
                fparts.at[d, :, lanes],
                s_f.at[h, d],
                r_f.at[h, d],
                tile=q_peer(d),
            )
    for h in range(2):
        lanes = half_of(h)
        total = fsend[f_rows(q), lanes].astype(F32)
        for d in range(1, nq):
            arrived(fparts.at[d, :, lanes], s_f.at[h, d], r_f.at[h, d])
            total = total + fparts[d, :, lanes].astype(F32)
        fz[:, lanes] = total.astype(BF16)
        for d in far_order(nz):
            send(
                fz.at[:, lanes],
                fzparts.at[d, :, lanes],
                s_fz.at[h, d],
                r_fz.at[h, d],
                tile=z_peer(d),
            )
    for d in far_order(nq):
        here = seen.at[core, own_slice(q), :]
        send(here, here, s_seen.at[d], r_seen.at[d], tile=q_peer(d))
    for i in range(2):
        send(
            edge_send.at[i],
            edge_in.at[1 - i, core],
            s_edge.at[i],
            r_edge.at[1 - i],
            tile=right if i else left,
        )
    row = lax.broadcasted_iota(jnp.int32, (fgroup, 128), 0)
    lane128 = lax.broadcasted_iota(jnp.int32, (fgroup, 128), 1)
    shift = lax.rem(q * fgroup, 128)
    diagonal = lane128 == row + shift
    loads["target"].wait()
    wanted = target[pl.ds(q * fgroup // 128, 1), :]
    focal = fz[...].astype(F32)
    for d in range(1, nz):
        for h in range(2):
            arrived(fzparts.at[d, :, half_of(h)], s_fz.at[h, d], r_fz.at[h, d])
        focal = focal + fzparts[d].astype(F32)
    square = focal * focal
    strength = jnp.sum(square[:, :ROWS] + square[:, ROWS:], axis=1, keepdims=True)
    line = jnp.sum(jnp.where(diagonal, strength, 0.0), axis=0, keepdims=True)
    isum[...] = jnp.broadcast_to(line, (8, 128))
    for e in far_order(ns):
        send(isum, iparts.at[e], s_i.at[e], r_i.at[e], src=lax.rem(s + e, ns))
    strength = line
    for e in range(1, ns):
        arrived(iparts.at[e], s_i.at[e], r_i.at[e])
        strength = strength + iparts[e, :1, :]
    in_line = lane128[:1] - shift
    in_line = (in_line >= 0) & (in_line < fgroup)
    flat = jnp.where(in_line, jnp.tanh(strength / (2.0 * ROWS * ns)) - wanted, 0.0)
    residual = jnp.sum(jnp.where(diagonal, flat, 0.0), axis=1, keepdims=True)
    f16 = aligned(q * fgroup, fgroup, 16)
    sign = jnp.where(lane128[:1] < ROWS // 2, 1.0, -1.0)
    sign = jnp.concatenate([sign, sign], axis=1)
    wg[f16, :] = (residual * focal * sign).astype(BF16)
    for d in far_order(nq):
        here = wg.at[f16]
        send(here, here, s_wg.at[d], r_wg.at[d], tile=q_peer(d))
    rrow[...] = jnp.broadcast_to(flat, (8, 128))
    rgath[q] = jnp.broadcast_to(flat, (8, 128))
    for d in far_order(nq):
        send(rrow, rgath.at[q], s_rr.at[d], r_rr.at[d], tile=q_peer(d))
    for d in range(1, nq):
        here = seen.at[core, own_slice(lax.rem(q + nq - d, nq)), :]
        arrived(here, s_seen.at[d], r_seen.at[d])
        send(here, here, s_pass.at[d], r_pass.at[d], src=sibling)
    for d in range(1, nq):
        sender = lax.rem(q + nq - d, nq)
        arrived(wg.at[aligned(sender * fgroup, fgroup, 16)], s_wg.at[d], r_wg.at[d])
    scale = float(tiles * TILE / focal_count) ** 0.5
    for d in range(1, nq):
        here = seen.at[1 - core, own_slice(lax.rem(q + nq - d, nq)), :]
        arrived(here, s_pass.at[d], r_pass.at[d])
    w = wg[...]
    coefficients = (lanes_joined(dot(seen[0], w), dot(seen[1], w)) * scale).astype(BF16)
    scatter(
        2,
        None,
        lanes_joined(dot(mback[0], coefficients), dot(mback[1], coefficients)),
        True,
    )
    wt[...] = jnp.transpose(wg[...].astype(F32)).astype(BF16)

    @pl.loop(0, 4)
    def _(step):
        cols = aligned(step * HALF, HALF, HALF)
        w = wt[...]
        u = rows_joined(dot(w, fk[0, :, cols]), dot(w, fk[1, :, cols])) * scale
        adjoint[:, cols] = u
        vb[3, :, cols] = u.astype(BF16)

    for side in range(2):
        here = edge_in.at[side, core]
        arrived(here, s_edge.at[side], r_edge.at[side])
        send(here, here, s_over.at[side], r_over.at[side], src=sibling)

    @pl.loop(0, 4)
    def _(step):
        m = step // 2
        half = aligned((step % 2) * HALF, HALF, HALF)
        by_re = jnp.zeros((2 * ROWS, HALF), F32)
        by_im = jnp.zeros((2 * ROWS, HALF), F32)
        for i in range(2):
            x = vb[3, :, i * TILE : (i + 1) * TILE]
            by_re = by_re + dot_nt(x, near[i, m - i + 1, 0, half, :])
            by_im = by_im + dot_nt(x, near[i, m - i + 1, 1, half, :])
        nacc[:, aligned(step * HALF, HALF, HALF)] = rows_joined(by_re, by_im)

    for side in range(2):
        arrived(edge_in.at[side, 1 - core], s_over.at[side], r_over.at[side])

    @pl.loop(0, 4)
    def _(step):
        side = step // 2
        cols = aligned((step % 2) * HALF, HALF, HALF)
        w = wt[...]
        edge = rows_joined(dot(w, edge_in[side, 0, :, cols]), dot(w, edge_in[side, 1, :, cols]))
        out = aligned(step * HALF, HALF, HALF)
        nacc[:, out] = nacc[:, out] + edge * scale

    back = scattered(2, None, True)
    for l in range(2):
        cols = slice(l * TILE, (l + 1) * TILE)
        added = nacc[:, cols] + expanded(back, sbasis, l)
        adjoint[:, cols] = adjoint[:, cols] - DAMPING * added
        for k in range(4):
            copy = pltpu.make_async_copy(
                adjoint.at[k * half : (k + 1) * half, cols],
                adj_out.at[k % 2, (k // 2) * half : (k // 2 + 1) * half, cols],
                local_sem.at[17 + 4 * l + k],
            )
            copy.start()
            copies.append(copy)

    lines = (focal_count + 127) // 128
    for d in range(1, nq):
        sender = lax.rem(q + nq - d, nq)
        arrived(rgath.at[sender], s_rr.at[d], r_rr.at[d])
    loads["owner"].wait()
    mine = lax.broadcasted_iota(jnp.int32, (8, 128), 0) + t * 8
    found = jnp.zeros((8, 128), F32)
    for line in range(lines):
        values = jnp.zeros((8, 128), F32)
        for other in range(nq):
            if other * fgroup // 128 == line:
                values = values + rgath[other]
        owners = jnp.broadcast_to(owner[line : line + 1, :], (8, 128))
        found = found + jnp.where(owners == mine, values, 0.0)
    column = jnp.broadcast_to(jnp.sum(found, axis=1, keepdims=True), (8, 128))
    diagonal = lax.broadcasted_iota(jnp.int32, (8, 128), 0) == lax.broadcasted_iota(
        jnp.int32, (8, 128), 1
    )
    line = jnp.sum(jnp.where(diagonal, column, 0.0), axis=0, keepdims=True)
    res_out[...] = line[:, :8]

    for copy in pending:
        copy.wait_send()
    for copy in copies:
        copy.wait()


CHUNKS = 2


def hand_out(field, residual, adjoint, field_out, residual_out, adjoint_out, held, in_sem, out_sem):
    residual_out[...] = residual[...]
    rows = held.shape[2] // CHUNKS
    loads, stores = [], []
    for k, (source, target) in enumerate(((field, field_out), (adjoint, adjoint_out))):
        for c in range(2 * CHUNKS):
            part = pl.ds((c // 2) * rows, rows)
            here = held.at[k, c % 2, part]
            loads.append(pltpu.make_async_copy(source.at[c % 2, part], here, in_sem.at[k, c]))
            stores.append(pltpu.make_async_copy(here, target.at[c % 2, part], out_sem.at[k, c]))
    for copy in loads:
        copy.start()
    for load, store in zip(loads, stores):
        load.wait()
        store.start()
    for store in stores:
        store.wait()


def per_device(
    nz,
    excitation,
    near_blocks,
    source_basis,
    target_basis,
    coupling,
    pair_rank,
    far_link,
    focal_kernel,
    focal_target,
    focal_owner,
):
    nt = lax.axis_size("tile")
    ns = lax.axis_size("src")
    nq = nt // nz
    focal_count = focal_target.shape[0]
    group = nz * PAIR
    spread = nq * PAIR
    fgroup = nz * 8
    width = 2 * TILE
    most = max(nz, nq)
    lines = (focal_count + 127) // 128
    wanted = jnp.pad(focal_target, (0, lines * 128 - focal_count))
    owner = jnp.pad(focal_owner, (0, lines * 128 - focal_count), constant_values=-1)
    vmem = pl.BlockSpec(memory_space=pltpu.VMEM)
    anywhere = pl.BlockSpec(memory_space=pl.ANY)
    dma = pltpu.SemaphoreType.DMA
    both = 2 * ROWS
    field, residual, adjoint = pl.pallas_call(
        functools.partial(kernel, nz, nq, ns),
        out_shape=(
            jax.ShapeDtypeStruct((2, ROWS, width), F32),
            jax.ShapeDtypeStruct((1, 8), F32),
            jax.ShapeDtypeStruct((2, ROWS, width), F32),
        ),
        in_specs=[anywhere] * 10,
        out_specs=(anywhere, vmem, anywhere),
        scratch_shapes=[
            pltpu.VMEM((both, width), F32),
            pltpu.VMEM((both, width), F32),
            pltpu.VMEM((2, 3, 2, TILE, TILE), BF16),
            pltpu.VMEM((2, focal_count, width), BF16),
            pltpu.VMEM((2, PAIR, TILE), BF16),
            pltpu.VMEM((2, PAIR, TILE), BF16),
            pltpu.VMEM((2, PAIR, nq * group), BF16),
            pltpu.VMEM((2, 2 * nt), jnp.int32),
            pltpu.VMEM((2, 2 * nt), jnp.int32),
            pltpu.VMEM((lines, 128), F32),
            pltpu.VMEM((lines, 128), jnp.int32),
            pltpu.VMEM((4, both, width), BF16),
            pltpu.VMEM((2, 2, both, TILE), BF16),
            pltpu.VMEM((both, width), F32),
            pltpu.VMEM((nq, PAIR, group), BF16),
            pltpu.VMEM((2, spread, group), BF16),
            pltpu.VMEM((2, group, spread), BF16),
            pltpu.VMEM((3, most * PAIR, both), BF16),
            pltpu.VMEM((3, most * PAIR, both), BF16),
            pltpu.VMEM((3, most, PAIR, both), BF16),
            pltpu.VMEM((focal_count, both), BF16),
            pltpu.VMEM((nq, fgroup, both), BF16),
            pltpu.VMEM((fgroup, both), BF16),
            pltpu.VMEM((nz, fgroup, both), BF16),
            pltpu.VMEM((8, 128), F32),
            pltpu.VMEM((ns, 8, 128), F32),
            pltpu.VMEM((focal_count, both), BF16),
            pltpu.VMEM((both, focal_count), BF16),
            pltpu.VMEM((8, 128), F32),
            pltpu.VMEM((nq, 8, 128), F32),
            pltpu.VMEM((2, focal_count, TILE), BF16),
            pltpu.VMEM((2, 2, focal_count, TILE), BF16),
            pltpu.VMEM((2, spread, focal_count), BF16),
            pltpu.VMEM((2, PAIR, focal_count), F32),
            dma((25,)),
            dma((2, 2, 2)),
            dma((2, 2, 2)),
            dma((nq,)),
            dma((nq,)),
            dma((3, 2, most)),
            dma((3, 2, most)),
            dma((3, 2, most)),
            dma((3, 2, most)),
            dma((2, nq)),
            dma((2, nq)),
            dma((2, nz)),
            dma((2, nz)),
            dma((ns,)),
            dma((ns,)),
            dma((nq,)),
            dma((nq,)),
            dma((nq,)),
            dma((nq,)),
            dma((nq,)),
            dma((nq,)),
            dma((nq,)),
            dma((nq,)),
            dma((nq,)),
            dma((nq,)),
            dma((2,)),
            dma((2,)),
            dma((2,)),
            dma((2,)),
        ],
        compiler_params=pltpu.CompilerParams(
            collective_id=0, has_side_effects=True, vmem_limit_bytes=56 * 1024 * 1024
        ),
    )(
        excitation,
        near_blocks,
        source_basis.reshape(2, PAIR, TILE),
        target_basis.reshape(2, PAIR, TILE),
        jnp.swapaxes(coupling, 1, 2),
        pair_rank.T,
        far_link.T,
        focal_kernel,
        wanted.reshape(lines, 128),
        owner.reshape(lines, 128),
    )
    field, residual, adjoint = pl.pallas_call(
        hand_out,
        out_shape=(
            jax.ShapeDtypeStruct((2, ROWS, width), F32),
            jax.ShapeDtypeStruct((1, 8), F32),
            jax.ShapeDtypeStruct((2, ROWS, width), F32),
        ),
        in_specs=[anywhere, vmem, anywhere],
        out_specs=[anywhere, vmem, anywhere],
        scratch_shapes=[
            pltpu.VMEM((2, 2, ROWS, width), F32),
            dma((2, 2 * CHUNKS)),
            dma((2, 2 * CHUNKS)),
        ],
        compiler_params=pltpu.CompilerParams(vmem_limit_bytes=56 * 1024 * 1024),
    )(field, residual, adjoint)
    return (
        field,
        residual.reshape(8),
        adjoint,
    )


def solution(mesh):
    nt = mesh.shape["tile"]
    nz = 8 if nt % 8 == 0 and nt > 8 else 2
    return jax.shard_map(
        functools.partial(per_device, nz),
        mesh=mesh,
        in_specs=(
            P(None, "src", "tile"),
            P("tile", None, None, None, None),
            P("tile", None, None, None),
            P("tile", None, None, None),
            P(None, None, "tile"),
            P(None, "tile"),
            P(None, "tile"),
            P(None, None, "tile"),
            P(),
            P(),
        ),
        out_specs=(P(None, "src", "tile"), P("tile"), P(None, "src", "tile")),
        check_vma=False,
    )
```

```python
import functools

import jax
import jax.numpy as jnp
from jax import lax
from jax.experimental import pallas as pl
from jax.experimental.pallas import tpu as pltpu
from jax.sharding import PartitionSpec as P

TILE = 512
RANK = 24
PAIR = 2 * RANK
ROWS = 128
DAMPING = 0.8
HALF = 256
F32 = jnp.float32
BF16 = jnp.bfloat16


def dot(left, right):
    return lax.dot_general(left, right, (((1,), (0,)), ((), ())), preferred_element_type=F32)


def dot_nt(left, right):
    return lax.dot_general(left, right, (((1,), (1,)), ((), ())), preferred_element_type=F32)


def rows_joined(by_re, by_im):
    shape = by_re.shape
    blocks = (shape[0] // ROWS, 2, ROWS // 2, shape[1])
    by_re, by_im = by_re.reshape(blocks), by_im.reshape(blocks)
    re = by_re[:, 0] - by_im[:, 1]
    im = by_re[:, 1] + by_im[:, 0]
    return jnp.stack([re, im], axis=1).reshape(shape)


def turned(x):
    lane = lax.broadcasted_iota(jnp.int32, (1, ROWS), 1)
    sign = jnp.where(lane < ROWS // 2, -1.0, 1.0)
    blocks = [
        pltpu.roll(x[:, k : k + ROWS], ROWS // 2, 1) * sign for k in range(0, x.shape[1], ROWS)
    ]
    return blocks[0] if len(blocks) == 1 else jnp.concatenate(blocks, axis=1)


def lanes_joined(by_re, by_im):
    return by_re + turned(by_im)


def half_of(h):
    return slice(0, 2 * ROWS) if h is None else slice(h * ROWS, (h + 1) * ROWS)


def aligned(start, size, unit):
    return pl.ds(pl.multiple_of(start, unit), size)


def kernel(
    nz,
    nq,
    ns,
    exc_hbm,
    near_hbm,
    sbasis_hbm,
    tbasis_hbm,
    coup_hbm,
    rank_hbm,
    link_hbm,
    fk_hbm,
    target_hbm,
    owner_hbm,
    field_out,
    res_out,
    adj_out,
    field,
    adjoint,
    near,
    fk,
    sbasis,
    tbasis,
    coup,
    rank,
    link,
    target,
    owner,
    vb,
    halo,
    nacc,
    mt_send,
    mt,
    mback,
    gath,
    part,
    parts_in,
    fsend,
    fparts,
    fz,
    fzparts,
    isum,
    iparts,
    wg,
    wt,
    rrow,
    rgath,
    edge_send,
    edge_in,
    seen,
    seen_own,
    local_sem,
    s_halo,
    r_halo,
    s_mt,
    r_mt,
    s_gath,
    r_gath,
    s_part,
    r_part,
    s_f,
    r_f,
    s_fz,
    r_fz,
    s_i,
    r_i,
    s_sib,
    r_sib,
    s_seen,
    r_seen,
    s_pass,
    r_pass,
    s_wg,
    r_wg,
    s_rr,
    r_rr,
    s_edge,
    r_edge,
):
    t = lax.axis_index("tile")
    s = lax.axis_index("src")
    nt = nz * nq
    q = t // nz
    z = t - q * nz
    tiles = 2 * nt
    group = nz * PAIR
    spread = nq * PAIR
    fgroup = nz * 8
    focal_count = nt * 8

    def z_peer(d):
        return q * nz + lax.rem(z + d, nz)

    def q_peer(d):
        return lax.rem(q + d, nq) * nz + z

    left = lax.rem(t + nt - 1, nt)
    right = lax.rem(t + 1, nt)

    barrier = pltpu.get_barrier_semaphore()
    count = 0
    for d in range(1, nq):
        pl.semaphore_signal(barrier, inc=1, device_id={"tile": q_peer(d), "src": s})
        count += 1
    for other in (left, right):
        pl.semaphore_signal(barrier, inc=1, device_id={"tile": other, "src": s})
        count += 1
    for d in range(1, nz):
        pl.semaphore_signal(barrier, inc=1, device_id={"tile": z_peer(d), "src": s})
        count += 1
    for e in range(1, ns):
        pl.semaphore_signal(barrier, inc=1, device_id={"tile": t, "src": lax.rem(s + e, ns)})
        count += 1
    core = lax.rem(s, 2)
    sibling = s + 1 - 2 * core

    half = ROWS // 2
    loads = {}
    for k, (name, source, place) in enumerate(
        (
            *(
                (
                    ("exc", h, c),
                    exc_hbm.at[c, h * half : (h + 1) * half],
                    vb.at[0, (2 * h + c) * half : (2 * h + c + 1) * half],
                )
                for h in range(2)
                for c in range(2)
            ),
            ("sbasis", sbasis_hbm, sbasis),
            ("rank", rank_hbm, rank),
            ("link", link_hbm, link),
            ("coup", coup_hbm, coup),
            ("near", near_hbm, near),
            ("tbasis", tbasis_hbm, tbasis),
            ("fk", fk_hbm, fk),
            ("target", target_hbm, target),
            ("owner", owner_hbm, owner),
        )
    ):
        loads[name] = pltpu.make_async_copy(source, place, local_sem.at[k])
        if name in ("exc", "sbasis", "rank", "link", "coup") or name[0] == "exc":
            loads[name].start()

    pending = []

    def send(src_ref, dst_ref, send_sem, recv_sem, tile=None, src=None):
        copy = pltpu.make_async_remote_copy(
            src_ref=src_ref,
            dst_ref=dst_ref,
            send_sem=send_sem,
            recv_sem=recv_sem,
            device_id={"tile": t if tile is None else tile, "src": s if src is None else src},
        )
        copy.start()
        pending.append(copy)

    def arrived(ref, send_sem, recv_sem):
        pltpu.make_async_remote_copy(
            src_ref=ref,
            dst_ref=ref,
            send_sem=send_sem,
            recv_sem=recv_sem,
            device_id={"tile": right, "src": s},
        ).wait_recv()

    def far_order(n):
        return sorted(range(1, n), key=lambda d: -min(d, n - d))

    def own_slice(index):
        return aligned(index * PAIR, PAIR, 16)

    def projected(x, basis):
        pieces = []
        for l in range(2):
            both = dot_nt(basis[l], x[:, l * TILE : (l + 1) * TILE])
            pieces.append(lanes_joined(both[:RANK], both[RANK:]))
        return jnp.concatenate(pieces, axis=0).astype(BF16)

    def gather(stage, h, value, along_z):
        n, mine = (nz, z) if along_z else (nq, q)
        lanes = half_of(h)
        here = gath.at[stage, own_slice(mine), lanes]
        gath[stage, own_slice(mine), lanes] = value
        for d in far_order(n):
            send(
                here,
                here,
                s_gath.at[stage, h or 0, d],
                r_gath.at[stage, h or 0, d],
                tile=z_peer(d) if along_z else q_peer(d),
            )

    def gathered(stage, h, along_z):
        n, mine = (nz, z) if along_z else (nq, q)
        for d in range(1, n):
            sender = lax.rem(mine + n - d, n)
            arrived(
                gath.at[stage, own_slice(sender), half_of(h)],
                s_gath.at[stage, h or 0, d],
                r_gath.at[stage, h or 0, d],
            )
        return gath[stage, : n * PAIR, half_of(h)]

    def scatter(stage, h, value, along_z):
        n, mine = (nz, z) if along_z else (nq, q)
        lanes = half_of(h)
        part[stage, :, lanes] = value.astype(BF16)
        for d in far_order(n):
            owner_of = lax.rem(mine + d, n)
            send(
                part.at[stage, own_slice(owner_of), lanes],
                parts_in.at[stage, d, :, lanes],
                s_part.at[stage, h or 0, d],
                r_part.at[stage, h or 0, d],
                tile=z_peer(d) if along_z else q_peer(d),
            )

    def scattered(stage, h, along_z):
        n, mine = (nz, z) if along_z else (nq, q)
        lanes = half_of(h)
        total = part[stage, own_slice(mine), lanes].astype(F32)
        for d in range(1, n):
            arrived(
                parts_in.at[stage, d, :, lanes],
                s_part.at[stage, h or 0, d],
                r_part.at[stage, h or 0, d],
            )
            total = total + parts_in[stage, d, :, lanes].astype(F32)
        return total.astype(BF16).astype(F32)

    def expanded(coefficients, basis, l):
        piece = coefficients[l * RANK : (l + 1) * RANK]
        stacked = jnp.concatenate([piece, turned(piece)], axis=0)
        return dot(jnp.transpose(stacked).astype(BF16), basis[l])

    def send_halo(stage, h):
        rows = half_of(h)
        send(
            vb.at[stage, rows, TILE : 2 * TILE],
            halo.at[stage, 0, rows],
            s_halo.at[stage, h, 0],
            r_halo.at[stage, h, 0],
            tile=right,
        )
        send(
            vb.at[stage, rows, 0:TILE],
            halo.at[stage, 1, rows],
            s_halo.at[stage, h, 1],
            r_halo.at[stage, h, 1],
            tile=left,
        )

    for h in range(2):
        for c in range(2):
            loads["exc", h, c].wait()
    loads["sbasis"].wait()
    loads["near"].start()
    first_coeff = projected(vb[0], sbasis)
    loads["rank"].wait()
    loads["link"].wait()

    level = lax.broadcasted_iota(jnp.int32, (RANK, tiles), 0)
    source_tile = lax.broadcasted_iota(jnp.int32, (1, tiles), 1)
    limits = []
    for l in range(2):
        gap = t * 2 + l - source_tile
        is_near = (
            (gap == 0)
            | (gap == 1)
            | (gap == -1)
            | (gap == tiles - 1)
            | (gap == 1 - tiles)
        )
        here = jnp.where((link[l : l + 1, :] == 1) & ~is_near, rank[l : l + 1, :], 0)
        wide = jnp.broadcast_to(here, (RANK, tiles))
        limits.append(jnp.where(level < wide, wide, 0).astype(F32))
    limits.append(
        jnp.broadcast_to(source_tile, (16, tiles)).astype(F32)
    )
    limit_rows = jnp.concatenate(limits, axis=0).astype(BF16)

    loads["coup"].wait()
    tile_row = lax.broadcasted_iota(jnp.int32, (tiles, group), 0)
    lane = lax.broadcasted_iota(jnp.int32, (tiles, group), 1)
    lane_row = lax.broadcasted_iota(jnp.int32, (1, group), 1)
    for d in far_order(nq) + [0]:
        to = lax.rem(q + d, nq)
        offset = lane - (tile_row - to * (2 * nz)) * RANK
        pick = jnp.where((offset >= 0) & (offset < RANK), 1.0, 0.0).astype(BF16)
        limit = dot(limit_rows, pick)
        position = (lane_row + to * group).astype(F32) - limit[PAIR : PAIR + 1, :] * float(RANK)
        keep = position < limit[:PAIR]
        for c in range(2) if d == 0 else (core,):
            block = coup[c, :, aligned(to * group, group, 128)]
            block = jnp.where(keep, block.astype(F32), 0.0).astype(BF16)
            if d == 0:
                mt[c, own_slice(q), :] = block
            else:
                mt_send[d] = block

    pl.semaphore_wait(barrier, count)

    for h in range(2):
        gather(0, h, first_coeff[:, half_of(h)], True)
        send_halo(0, h)
    for d in far_order(nq):
        send(
            mt_send.at[d],
            mt.at[core, own_slice(q), :],
            s_mt.at[d],
            r_mt.at[d],
            tile=q_peer(d),
        )
    for name in ("tbasis", "fk", "target", "owner"):
        loads[name].start()

    def near_own(stage, h):
        rows = half_of(h)

        @pl.loop(0, 4)
        def _(step):
            i = step // 2
            cols = aligned((step % 2) * HALF, HALF, HALF)
            by_re = by_im = 0.0
            for l in range(2):
                x = vb[stage, rows, l * TILE : (l + 1) * TILE]
                by_re = by_re + dot(x, near[i, l - i + 1, 0, :, cols])
                by_im = by_im + dot(x, near[i, l - i + 1, 1, :, cols])
            nacc[rows, aligned(step * HALF, HALF, HALF)] = rows_joined(by_re, by_im)

    def near_halo(stage, h):
        rows = half_of(h)
        for side in range(2):
            arrived(
                halo.at[stage, side, rows],
                s_halo.at[stage, h, side],
                r_halo.at[stage, h, side],
            )

        @pl.loop(0, 4)
        def _(step):
            i = step // 2
            cols = aligned((step % 2) * HALF, HALF, HALF)
            x = halo[stage, i, rows]
            by_re = dot(x, near[i, 2 * i, 0, :, cols])
            by_im = dot(x, near[i, 2 * i, 1, :, cols])
            out = aligned(step * HALF, HALF, HALF)
            nacc[rows, out] = nacc[rows, out] + rows_joined(by_re, by_im)

    def couple(stage, h):
        coefficients = gathered(stage, h, True)
        scatter(
            stage, h, lanes_joined(dot(mt[0], coefficients), dot(mt[1], coefficients)), False
        )

    def updated(stage, h):
        near_halo(stage, h)
        coupled = scattered(stage, h, False)
        rows = half_of(h)
        for l in range(2):
            cols = slice(l * TILE, (l + 1) * TILE)
            added = nacc[rows, cols] + expanded(coupled, tbasis, l)
            right_side = vb[0, rows, cols].astype(F32)
            if stage == 0:
                value = right_side - DAMPING * added
            else:
                before = field[rows, cols]
                value = before + DAMPING * (right_side - (before + added))
            field[rows, cols] = value
            vb[stage + 1, rows, cols] = value.astype(BF16)

    loads["near"].wait()
    near_own(0, None)
    for d in range(1, nq):
        here = mt.at[core, own_slice(lax.rem(q + nq - d, nq)), :]
        arrived(here, s_mt.at[d], r_mt.at[d])
        send(here, here, s_sib.at[d], r_sib.at[d], src=sibling)
    for d in range(1, nq):
        here = mt.at[1 - core, own_slice(lax.rem(q + nq - d, nq)), :]
        arrived(here, s_sib.at[d], r_sib.at[d])
    for h in range(2):
        couple(0, h)
    for c in range(2):
        mback[c] = jnp.transpose(mt[c].astype(F32)).astype(BF16)
    loads["tbasis"].wait()
    for h in range(2):
        updated(0, h)
        gather(1, h, projected(vb[1, half_of(h)], sbasis), True)
        send_halo(1, h)
    for h in range(2):
        near_own(1, h)
        couple(1, h)
    loads["fk"].wait()
    for l in range(2):
        cols = slice(l * TILE, (l + 1) * TILE)
        by_re = dot_nt(tbasis[l], fk[0, :, cols])
        by_im = dot_nt(tbasis[l], fk[1, :, cols])
        seen_own[0, l * RANK : (l + 1) * RANK] = by_re[:RANK] - by_im[RANK:]
        seen_own[1, l * RANK : (l + 1) * RANK] = by_im[:RANK] + by_re[RANK:]
    seen[:, own_slice(q), :] = seen_own[...].astype(BF16)
    copies = []

    def f_rows(index):
        return aligned(index * fgroup, fgroup, 16)

    for h in range(2):
        updated(1, h)
        for c in range(2):
            copy = pltpu.make_async_copy(
                field.at[(2 * h + c) * half : (2 * h + c + 1) * half],
                field_out.at[c, h * half : (h + 1) * half],
                local_sem.at[13 + 2 * h + c],
            )
            copy.start()
            copies.append(copy)
        lanes = half_of(h)
        x = vb[2, lanes]
        fsend[:, lanes] = lanes_joined(dot_nt(fk[0], x), dot_nt(fk[1], x)).astype(BF16)
        for d in far_order(nq):
            send(
                fsend.at[f_rows(lax.rem(q + d, nq)), lanes],
                fparts.at[d, :, lanes],
                s_f.at[h, d],
                r_f.at[h, d],
                tile=q_peer(d),
            )
    for h in range(2):
        lanes = half_of(h)
        total = fsend[f_rows(q), lanes].astype(F32)
        for d in range(1, nq):
            arrived(fparts.at[d, :, lanes], s_f.at[h, d], r_f.at[h, d])
            total = total + fparts[d, :, lanes].astype(F32)
        fz[:, lanes] = total.astype(BF16)
        for d in far_order(nz):
            send(
                fz.at[:, lanes],
                fzparts.at[d, :, lanes],
                s_fz.at[h, d],
                r_fz.at[h, d],
                tile=z_peer(d),
            )
    for d in far_order(nq):
        here = seen.at[core, own_slice(q), :]
        send(here, here, s_seen.at[d], r_seen.at[d], tile=q_peer(d))
    row = lax.broadcasted_iota(jnp.int32, (fgroup, 128), 0)
    lane128 = lax.broadcasted_iota(jnp.int32, (fgroup, 128), 1)
    shift = lax.rem(q * fgroup, 128)
    diagonal = lane128 == row + shift
    loads["target"].wait()
    wanted = target[pl.ds(q * fgroup // 128, 1), :]
    focal = fz[...].astype(F32)
    for d in range(1, nz):
        for h in range(2):
            arrived(fzparts.at[d, :, half_of(h)], s_fz.at[h, d], r_fz.at[h, d])
        focal = focal + fzparts[d].astype(F32)
    square = focal * focal
    strength = jnp.sum(square[:, :ROWS] + square[:, ROWS:], axis=1, keepdims=True)
    line = jnp.sum(jnp.where(diagonal, strength, 0.0), axis=0, keepdims=True)
    isum[...] = jnp.broadcast_to(line, (8, 128))
    for e in far_order(ns):
        send(isum, iparts.at[e], s_i.at[e], r_i.at[e], src=lax.rem(s + e, ns))
    strength = line
    for e in range(1, ns):
        arrived(iparts.at[e], s_i.at[e], r_i.at[e])
        strength = strength + iparts[e, :1, :]
    in_line = lane128[:1] - shift
    in_line = (in_line >= 0) & (in_line < fgroup)
    flat = jnp.where(in_line, jnp.tanh(strength / (2.0 * ROWS * ns)) - wanted, 0.0)
    residual = jnp.sum(jnp.where(diagonal, flat, 0.0), axis=1, keepdims=True)
    f16 = aligned(q * fgroup, fgroup, 16)
    sign = jnp.where(lane128[:1] < ROWS // 2, 1.0, -1.0)
    sign = jnp.concatenate([sign, sign], axis=1)
    wg[f16, :] = (residual * focal * sign).astype(BF16)
    for d in far_order(nq):
        here = wg.at[f16]
        send(here, here, s_wg.at[d], r_wg.at[d], tile=q_peer(d))
    rrow[...] = jnp.broadcast_to(flat, (8, 128))
    rgath[q] = jnp.broadcast_to(flat, (8, 128))
    for d in far_order(nq):
        send(rrow, rgath.at[q], s_rr.at[d], r_rr.at[d], tile=q_peer(d))
    for d in range(1, nq):
        here = seen.at[core, own_slice(lax.rem(q + nq - d, nq)), :]
        arrived(here, s_seen.at[d], r_seen.at[d])
        send(here, here, s_pass.at[d], r_pass.at[d], src=sibling)
    for d in range(1, nq):
        sender = lax.rem(q + nq - d, nq)
        arrived(wg.at[aligned(sender * fgroup, fgroup, 16)], s_wg.at[d], r_wg.at[d])
    wt[...] = jnp.transpose(wg[...].astype(F32)).astype(BF16)

    scale = float(tiles * TILE / focal_count) ** 0.5

    for i in range(2):
        w = wt[...]
        for k in range(2):
            cols = slice((2 * i + k) * HALF, (2 * i + k + 1) * HALF)
            u = rows_joined(dot(w, fk[0, :, cols]), dot(w, fk[1, :, cols])) * scale
            adjoint[:, cols] = u
            vb[3, :, cols] = u.astype(BF16)
        x = vb[3, :, i * TILE : (i + 1) * TILE]
        by_re = dot_nt(x, near[i, 2 * i, 0])
        by_im = dot_nt(x, near[i, 2 * i, 1])
        edge_send[i] = rows_joined(by_re, by_im).astype(BF16)
        send(
            edge_send.at[i],
            edge_in.at[1 - i],
            s_edge.at[i],
            r_edge.at[1 - i],
            tile=right if i else left,
        )

    for d in range(1, nq):
        here = seen.at[1 - core, own_slice(lax.rem(q + nq - d, nq)), :]
        arrived(here, s_pass.at[d], r_pass.at[d])
    w = wg[...]
    coefficients = (lanes_joined(dot(seen[0], w), dot(seen[1], w)) * scale).astype(BF16)
    scatter(
        2,
        None,
        lanes_joined(dot(mback[0], coefficients), dot(mback[1], coefficients)),
        True,
    )

    @pl.loop(0, 4)
    def _(step):
        m = step // 2
        half = aligned((step % 2) * HALF, HALF, HALF)
        by_re = jnp.zeros((2 * ROWS, HALF), F32)
        by_im = jnp.zeros((2 * ROWS, HALF), F32)
        for i in range(2):
            x = vb[3, :, i * TILE : (i + 1) * TILE]
            by_re = by_re + dot_nt(x, near[i, m - i + 1, 0, half, :])
            by_im = by_im + dot_nt(x, near[i, m - i + 1, 1, half, :])
        nacc[:, aligned(step * HALF, HALF, HALF)] = rows_joined(by_re, by_im)

    for side in range(2):
        arrived(edge_in.at[side], s_edge.at[side], r_edge.at[side])
    back = scattered(2, None, True)
    for l in range(2):
        cols = slice(l * TILE, (l + 1) * TILE)
        added = nacc[:, cols] + edge_in[l].astype(F32) + expanded(back, sbasis, l)
        adjoint[:, cols] = adjoint[:, cols] - DAMPING * added
        for k in range(4):
            copy = pltpu.make_async_copy(
                adjoint.at[k * half : (k + 1) * half, cols],
                adj_out.at[k % 2, (k // 2) * half : (k // 2 + 1) * half, cols],
                local_sem.at[17 + 4 * l + k],
            )
            copy.start()
            copies.append(copy)

    lines = (focal_count + 127) // 128
    for d in range(1, nq):
        sender = lax.rem(q + nq - d, nq)
        arrived(rgath.at[sender], s_rr.at[d], r_rr.at[d])
    loads["owner"].wait()
    mine = lax.broadcasted_iota(jnp.int32, (8, 128), 0) + t * 8
    found = jnp.zeros((8, 128), F32)
    for line in range(lines):
        values = jnp.zeros((8, 128), F32)
        for other in range(nq):
            if other * fgroup // 128 == line:
                values = values + rgath[other]
        owners = jnp.broadcast_to(owner[line : line + 1, :], (8, 128))
        found = found + jnp.where(owners == mine, values, 0.0)
    column = jnp.broadcast_to(jnp.sum(found, axis=1, keepdims=True), (8, 128))
    diagonal = lax.broadcasted_iota(jnp.int32, (8, 128), 0) == lax.broadcasted_iota(
        jnp.int32, (8, 128), 1
    )
    line = jnp.sum(jnp.where(diagonal, column, 0.0), axis=0, keepdims=True)
    res_out[...] = line[:, :8]

    for copy in pending:
        copy.wait_send()
    for copy in copies:
        copy.wait()


CHUNKS = 2


def hand_out(field, residual, adjoint, field_out, residual_out, adjoint_out, held, in_sem, out_sem):
    residual_out[...] = residual[...]
    rows = held.shape[2] // CHUNKS
    loads, stores = [], []
    for k, (source, target) in enumerate(((field, field_out), (adjoint, adjoint_out))):
        for c in range(2 * CHUNKS):
            part = pl.ds((c // 2) * rows, rows)
            here = held.at[k, c % 2, part]
            loads.append(pltpu.make_async_copy(source.at[c % 2, part], here, in_sem.at[k, c]))
            stores.append(pltpu.make_async_copy(here, target.at[c % 2, part], out_sem.at[k, c]))
    for copy in loads:
        copy.start()
    for load, store in zip(loads, stores):
        load.wait()
        store.start()
    for store in stores:
        store.wait()


def per_device(
    nz,
    excitation,
    near_blocks,
    source_basis,
    target_basis,
    coupling,
    pair_rank,
    far_link,
    focal_kernel,
    focal_target,
    focal_owner,
):
    nt = lax.axis_size("tile")
    ns = lax.axis_size("src")
    nq = nt // nz
    focal_count = focal_target.shape[0]
    group = nz * PAIR
    spread = nq * PAIR
    fgroup = nz * 8
    width = 2 * TILE
    most = max(nz, nq)
    lines = (focal_count + 127) // 128
    wanted = jnp.pad(focal_target, (0, lines * 128 - focal_count))
    owner = jnp.pad(focal_owner, (0, lines * 128 - focal_count), constant_values=-1)
    vmem = pl.BlockSpec(memory_space=pltpu.VMEM)
    anywhere = pl.BlockSpec(memory_space=pl.ANY)
    dma = pltpu.SemaphoreType.DMA
    both = 2 * ROWS
    field, residual, adjoint = pl.pallas_call(
        functools.partial(kernel, nz, nq, ns),
        out_shape=(
            jax.ShapeDtypeStruct((2, ROWS, width), F32),
            jax.ShapeDtypeStruct((1, 8), F32),
            jax.ShapeDtypeStruct((2, ROWS, width), F32),
        ),
        in_specs=[anywhere] * 10,
        out_specs=(anywhere, vmem, anywhere),
        scratch_shapes=[
            pltpu.VMEM((both, width), F32),
            pltpu.VMEM((both, width), F32),
            pltpu.VMEM((2, 3, 2, TILE, TILE), BF16),
            pltpu.VMEM((2, focal_count, width), BF16),
            pltpu.VMEM((2, PAIR, TILE), BF16),
            pltpu.VMEM((2, PAIR, TILE), BF16),
            pltpu.VMEM((2, PAIR, nq * group), BF16),
            pltpu.VMEM((2, 2 * nt), jnp.int32),
            pltpu.VMEM((2, 2 * nt), jnp.int32),
            pltpu.VMEM((lines, 128), F32),
            pltpu.VMEM((lines, 128), jnp.int32),
            pltpu.VMEM((4, both, width), BF16),
            pltpu.VMEM((2, 2, both, TILE), BF16),
            pltpu.VMEM((both, width), F32),
            pltpu.VMEM((nq, PAIR, group), BF16),
            pltpu.VMEM((2, spread, group), BF16),
            pltpu.VMEM((2, group, spread), BF16),
            pltpu.VMEM((3, most * PAIR, both), BF16),
            pltpu.VMEM((3, most * PAIR, both), BF16),
            pltpu.VMEM((3, most, PAIR, both), BF16),
            pltpu.VMEM((focal_count, both), BF16),
            pltpu.VMEM((nq, fgroup, both), BF16),
            pltpu.VMEM((fgroup, both), BF16),
            pltpu.VMEM((nz, fgroup, both), BF16),
            pltpu.VMEM((8, 128), F32),
            pltpu.VMEM((ns, 8, 128), F32),
            pltpu.VMEM((focal_count, both), BF16),
            pltpu.VMEM((both, focal_count), BF16),
            pltpu.VMEM((8, 128), F32),
            pltpu.VMEM((nq, 8, 128), F32),
            pltpu.VMEM((2, both, TILE), BF16),
            pltpu.VMEM((2, both, TILE), BF16),
            pltpu.VMEM((2, spread, focal_count), BF16),
            pltpu.VMEM((2, PAIR, focal_count), F32),
            dma((25,)),
            dma((2, 2, 2)),
            dma((2, 2, 2)),
            dma((nq,)),
            dma((nq,)),
            dma((3, 2, most)),
            dma((3, 2, most)),
            dma((3, 2, most)),
            dma((3, 2, most)),
            dma((2, nq)),
            dma((2, nq)),
            dma((2, nz)),
            dma((2, nz)),
            dma((ns,)),
            dma((ns,)),
            dma((nq,)),
            dma((nq,)),
            dma((nq,)),
            dma((nq,)),
            dma((nq,)),
            dma((nq,)),
            dma((nq,)),
            dma((nq,)),
            dma((nq,)),
            dma((nq,)),
            dma((2,)),
            dma((2,)),
        ],
        compiler_params=pltpu.CompilerParams(
            collective_id=0, has_side_effects=True, vmem_limit_bytes=56 * 1024 * 1024
        ),
    )(
        excitation,
        near_blocks,
        source_basis.reshape(2, PAIR, TILE),
        target_basis.reshape(2, PAIR, TILE),
        jnp.swapaxes(coupling, 1, 2),
        pair_rank.T,
        far_link.T,
        focal_kernel,
        wanted.reshape(lines, 128),
        owner.reshape(lines, 128),
    )
    field, residual, adjoint = pl.pallas_call(
        hand_out,
        out_shape=(
            jax.ShapeDtypeStruct((2, ROWS, width), F32),
            jax.ShapeDtypeStruct((1, 8), F32),
            jax.ShapeDtypeStruct((2, ROWS, width), F32),
        ),
        in_specs=[anywhere, vmem, anywhere],
        out_specs=[anywhere, vmem, anywhere],
        scratch_shapes=[
            pltpu.VMEM((2, 2, ROWS, width), F32),
            dma((2, 2 * CHUNKS)),
            dma((2, 2 * CHUNKS)),
        ],
        compiler_params=pltpu.CompilerParams(vmem_limit_bytes=56 * 1024 * 1024),
    )(field, residual, adjoint)
    return (
        field,
        residual.reshape(8),
        adjoint,
    )


def solution(mesh):
    nt = mesh.shape["tile"]
    nz = 8 if nt % 8 == 0 and nt > 8 else 2
    return jax.shard_map(
        functools.partial(per_device, nz),
        mesh=mesh,
        in_specs=(
            P(None, "src", "tile"),
            P("tile", None, None, None, None),
            P("tile", None, None, None),
            P("tile", None, None, None),
            P(None, None, "tile"),
            P(None, "tile"),
            P(None, "tile"),
            P(None, None, "tile"),
            P(),
            P(),
        ),
        out_specs=(P(None, "src", "tile"), P("tile"), P(None, "src", "tile")),
        check_vma=False,
    )
```

```python
import functools

import jax
import jax.numpy as jnp
from jax import lax
from jax.experimental import pallas as pl
from jax.experimental.pallas import tpu as pltpu
from jax.sharding import PartitionSpec as P

TILE = 512
RANK = 24
PAIR = 2 * RANK
ROWS = 128
DAMPING = 0.8
HALF = 256
F32 = jnp.float32
BF16 = jnp.bfloat16


def dot(left, right):
    return lax.dot_general(left, right, (((1,), (0,)), ((), ())), preferred_element_type=F32)


def dot_nt(left, right):
    return lax.dot_general(left, right, (((1,), (1,)), ((), ())), preferred_element_type=F32)


def rows_joined(by_re, by_im):
    shape = by_re.shape
    blocks = (shape[0] // ROWS, 2, ROWS // 2, shape[1])
    by_re, by_im = by_re.reshape(blocks), by_im.reshape(blocks)
    re = by_re[:, 0] - by_im[:, 1]
    im = by_re[:, 1] + by_im[:, 0]
    return jnp.stack([re, im], axis=1).reshape(shape)


def turned(x):
    lane = lax.broadcasted_iota(jnp.int32, (1, ROWS), 1)
    sign = jnp.where(lane < ROWS // 2, -1.0, 1.0)
    blocks = [
        pltpu.roll(x[:, k : k + ROWS], ROWS // 2, 1) * sign for k in range(0, x.shape[1], ROWS)
    ]
    return blocks[0] if len(blocks) == 1 else jnp.concatenate(blocks, axis=1)


def lanes_joined(by_re, by_im):
    return by_re + turned(by_im)


def half_of(h):
    return slice(0, 2 * ROWS) if h is None else slice(h * ROWS, (h + 1) * ROWS)


def aligned(start, size, unit):
    return pl.ds(pl.multiple_of(start, unit), size)


def kernel(
    nz,
    nq,
    ns,
    exc_hbm,
    near_hbm,
    sbasis_hbm,
    tbasis_hbm,
    coup_hbm,
    rank_hbm,
    link_hbm,
    fk_hbm,
    target_hbm,
    owner_hbm,
    field_out,
    res_out,
    adj_out,
    field,
    adjoint,
    near,
    fk,
    sbasis,
    tbasis,
    coup,
    rank,
    link,
    target,
    owner,
    vb,
    halo,
    nacc,
    mt_send,
    mt,
    mback,
    gath,
    part,
    parts_in,
    fsend,
    fparts,
    fz,
    fzparts,
    isum,
    iparts,
    wg,
    wt,
    rrow,
    rgath,
    edge_send,
    edge_in,
    seen,
    seen_own,
    local_sem,
    s_halo,
    r_halo,
    s_mt,
    r_mt,
    s_gath,
    r_gath,
    s_part,
    r_part,
    s_f,
    r_f,
    s_fz,
    r_fz,
    s_i,
    r_i,
    s_sib,
    r_sib,
    s_seen,
    r_seen,
    s_pass,
    r_pass,
    s_wg,
    r_wg,
    s_rr,
    r_rr,
    s_edge,
    r_edge,
):
    t = lax.axis_index("tile")
    s = lax.axis_index("src")
    nt = nz * nq
    q = t // nz
    z = t - q * nz
    tiles = 2 * nt
    group = nz * PAIR
    spread = nq * PAIR
    fgroup = nz * 8
    focal_count = nt * 8

    def z_peer(d):
        return q * nz + lax.rem(z + d, nz)

    def q_peer(d):
        return lax.rem(q + d, nq) * nz + z

    left = lax.rem(t + nt - 1, nt)
    right = lax.rem(t + 1, nt)

    barrier = pltpu.get_barrier_semaphore()
    count = 0
    for d in range(1, nq):
        pl.semaphore_signal(barrier, inc=1, device_id={"tile": q_peer(d), "src": s})
        count += 1
    for other in (left, right):
        pl.semaphore_signal(barrier, inc=1, device_id={"tile": other, "src": s})
        count += 1
    for d in range(1, nz):
        pl.semaphore_signal(barrier, inc=1, device_id={"tile": z_peer(d), "src": s})
        count += 1
    for e in range(1, ns):
        pl.semaphore_signal(barrier, inc=1, device_id={"tile": t, "src": lax.rem(s + e, ns)})
        count += 1
    core = lax.rem(s, 2)
    sibling = s + 1 - 2 * core

    half = ROWS // 2
    loads = {}
    for k, (name, source, place) in enumerate(
        (
            *(
                (
                    ("exc", h, c),
                    exc_hbm.at[c, h * half : (h + 1) * half],
                    vb.at[0, (2 * h + c) * half : (2 * h + c + 1) * half],
                )
                for h in range(2)
                for c in range(2)
            ),
            ("sbasis", sbasis_hbm, sbasis),
            ("rank", rank_hbm, rank),
            ("link", link_hbm, link),
            ("coup", coup_hbm, coup),
            ("near", near_hbm, near),
            ("tbasis", tbasis_hbm, tbasis),
            ("fk", fk_hbm, fk),
            ("target", target_hbm, target),
            ("owner", owner_hbm, owner),
        )
    ):
        loads[name] = pltpu.make_async_copy(source, place, local_sem.at[k])
        if name in ("exc", "sbasis", "rank", "link", "coup") or name[0] == "exc":
            loads[name].start()

    pending = []

    def send(src_ref, dst_ref, send_sem, recv_sem, tile=None, src=None):
        copy = pltpu.make_async_remote_copy(
            src_ref=src_ref,
            dst_ref=dst_ref,
            send_sem=send_sem,
            recv_sem=recv_sem,
            device_id={"tile": t if tile is None else tile, "src": s if src is None else src},
        )
        copy.start()
        pending.append(copy)

    def arrived(ref, send_sem, recv_sem):
        pltpu.make_async_remote_copy(
            src_ref=ref,
            dst_ref=ref,
            send_sem=send_sem,
            recv_sem=recv_sem,
            device_id={"tile": right, "src": s},
        ).wait_recv()

    def far_order(n):
        return sorted(range(1, n), key=lambda d: -min(d, n - d))

    def own_slice(index):
        return aligned(index * PAIR, PAIR, 16)

    def projected(x, basis):
        pieces = []
        for l in range(2):
            both = dot_nt(basis[l], x[:, l * TILE : (l + 1) * TILE])
            pieces.append(lanes_joined(both[:RANK], both[RANK:]))
        return jnp.concatenate(pieces, axis=0).astype(BF16)

    def gather(stage, h, value, along_z):
        n, mine = (nz, z) if along_z else (nq, q)
        lanes = half_of(h)
        here = gath.at[stage, own_slice(mine), lanes]
        gath[stage, own_slice(mine), lanes] = value
        for d in far_order(n):
            send(
                here,
                here,
                s_gath.at[stage, h or 0, d],
                r_gath.at[stage, h or 0, d],
                tile=z_peer(d) if along_z else q_peer(d),
            )

    def gathered(stage, h, along_z):
        n, mine = (nz, z) if along_z else (nq, q)
        for d in range(1, n):
            sender = lax.rem(mine + n - d, n)
            arrived(
                gath.at[stage, own_slice(sender), half_of(h)],
                s_gath.at[stage, h or 0, d],
                r_gath.at[stage, h or 0, d],
            )
        return gath[stage, : n * PAIR, half_of(h)]

    def scatter(stage, h, value, along_z):
        n, mine = (nz, z) if along_z else (nq, q)
        lanes = half_of(h)
        part[stage, :, lanes] = value.astype(BF16)
        for d in far_order(n):
            owner_of = lax.rem(mine + d, n)
            send(
                part.at[stage, own_slice(owner_of), lanes],
                parts_in.at[stage, d, :, lanes],
                s_part.at[stage, h or 0, d],
                r_part.at[stage, h or 0, d],
                tile=z_peer(d) if along_z else q_peer(d),
            )

    def scattered(stage, h, along_z):
        n, mine = (nz, z) if along_z else (nq, q)
        lanes = half_of(h)
        total = part[stage, own_slice(mine), lanes].astype(F32)
        for d in range(1, n):
            arrived(
                parts_in.at[stage, d, :, lanes],
                s_part.at[stage, h or 0, d],
                r_part.at[stage, h or 0, d],
            )
            total = total + parts_in[stage, d, :, lanes].astype(F32)
        return total.astype(BF16).astype(F32)

    def expanded(coefficients, basis, l):
        piece = coefficients[l * RANK : (l + 1) * RANK]
        stacked = jnp.concatenate([piece, turned(piece)], axis=0)
        return dot(jnp.transpose(stacked).astype(BF16), basis[l])

    def send_halo(stage, h):
        rows = half_of(h)
        send(
            vb.at[stage, rows, TILE : 2 * TILE],
            halo.at[stage, 0, rows],
            s_halo.at[stage, h, 0],
            r_halo.at[stage, h, 0],
            tile=right,
        )
        send(
            vb.at[stage, rows, 0:TILE],
            halo.at[stage, 1, rows],
            s_halo.at[stage, h, 1],
            r_halo.at[stage, h, 1],
            tile=left,
        )

    for h in range(2):
        for c in range(2):
            loads["exc", h, c].wait()
    loads["sbasis"].wait()
    loads["near"].start()
    first_coeff = projected(vb[0], sbasis)
    loads["rank"].wait()
    loads["link"].wait()

    level = lax.broadcasted_iota(jnp.int32, (RANK, tiles), 0)
    source_tile = lax.broadcasted_iota(jnp.int32, (1, tiles), 1)
    limits = []
    for l in range(2):
        gap = t * 2 + l - source_tile
        is_near = (
            (gap == 0)
            | (gap == 1)
            | (gap == -1)
            | (gap == tiles - 1)
            | (gap == 1 - tiles)
        )
        here = jnp.where((link[l : l + 1, :] == 1) & ~is_near, rank[l : l + 1, :], 0)
        wide = jnp.broadcast_to(here, (RANK, tiles))
        limits.append(jnp.where(level < wide, wide, 0).astype(F32))
    limits.append(
        jnp.broadcast_to(source_tile, (16, tiles)).astype(F32)
    )
    limit_rows = jnp.concatenate(limits, axis=0).astype(BF16)

    loads["coup"].wait()
    tile_row = lax.broadcasted_iota(jnp.int32, (tiles, group), 0)
    lane = lax.broadcasted_iota(jnp.int32, (tiles, group), 1)
    lane_row = lax.broadcasted_iota(jnp.int32, (1, group), 1)
    for d in far_order(nq) + [0]:
        to = lax.rem(q + d, nq)
        offset = lane - (tile_row - to * (2 * nz)) * RANK
        pick = jnp.where((offset >= 0) & (offset < RANK), 1.0, 0.0).astype(BF16)
        limit = dot(limit_rows, pick)
        position = (lane_row + to * group).astype(F32) - limit[PAIR : PAIR + 1, :] * float(RANK)
        keep = position < limit[:PAIR]
        for c in range(2) if d == 0 else (core,):
            block = coup[c, :, aligned(to * group, group, 128)]
            block = jnp.where(keep, block.astype(F32), 0.0).astype(BF16)
            if d == 0:
                mt[c, own_slice(q), :] = block
            else:
                mt_send[d] = block

    pl.semaphore_wait(barrier, count)

    for h in range(2):
        gather(0, h, first_coeff[:, half_of(h)], True)
        send_halo(0, h)
    for d in far_order(nq):
        send(
            mt_send.at[d],
            mt.at[core, own_slice(q), :],
            s_mt.at[d],
            r_mt.at[d],
            tile=q_peer(d),
        )
    for name in ("tbasis", "fk", "target", "owner"):
        loads[name].start()

    def near_own(stage, h):
        rows = half_of(h)

        @pl.loop(0, 4)
        def _(step):
            i = step // 2
            cols = aligned((step % 2) * HALF, HALF, HALF)
            by_re = by_im = 0.0
            for l in range(2):
                x = vb[stage, rows, l * TILE : (l + 1) * TILE]
                by_re = by_re + dot(x, near[i, l - i + 1, 0, :, cols])
                by_im = by_im + dot(x, near[i, l - i + 1, 1, :, cols])
            nacc[rows, aligned(step * HALF, HALF, HALF)] = rows_joined(by_re, by_im)

    def near_halo(stage, h):
        rows = half_of(h)
        for side in range(2):
            arrived(
                halo.at[stage, side, rows],
                s_halo.at[stage, h, side],
                r_halo.at[stage, h, side],
            )

        @pl.loop(0, 4)
        def _(step):
            i = step // 2
            cols = aligned((step % 2) * HALF, HALF, HALF)
            x = halo[stage, i, rows]
            by_re = dot(x, near[i, 2 * i, 0, :, cols])
            by_im = dot(x, near[i, 2 * i, 1, :, cols])
            out = aligned(step * HALF, HALF, HALF)
            nacc[rows, out] = nacc[rows, out] + rows_joined(by_re, by_im)

    def couple(stage, h):
        coefficients = gathered(stage, h, True)
        scatter(
            stage, h, lanes_joined(dot(mt[0], coefficients), dot(mt[1], coefficients)), False
        )

    def updated(stage, h):
        near_halo(stage, h)
        coupled = scattered(stage, h, False)
        rows = half_of(h)
        for l in range(2):
            cols = slice(l * TILE, (l + 1) * TILE)
            added = nacc[rows, cols] + expanded(coupled, tbasis, l)
            right_side = vb[0, rows, cols].astype(F32)
            if stage == 0:
                value = right_side - DAMPING * added
            else:
                before = field[rows, cols]
                value = before + DAMPING * (right_side - (before + added))
            field[rows, cols] = value
            vb[stage + 1, rows, cols] = value.astype(BF16)

    loads["near"].wait()
    near_own(0, None)
    for d in range(1, nq):
        here = mt.at[core, own_slice(lax.rem(q + nq - d, nq)), :]
        arrived(here, s_mt.at[d], r_mt.at[d])
        send(here, here, s_sib.at[d], r_sib.at[d], src=sibling)
    for d in range(1, nq):
        here = mt.at[1 - core, own_slice(lax.rem(q + nq - d, nq)), :]
        arrived(here, s_sib.at[d], r_sib.at[d])
    for h in range(2):
        couple(0, h)
    for c in range(2):
        mback[c] = jnp.transpose(mt[c].astype(F32)).astype(BF16)
    loads["tbasis"].wait()
    for h in range(2):
        updated(0, h)
        gather(1, h, projected(vb[1, half_of(h)], sbasis), True)
        send_halo(1, h)
    for h in range(2):
        near_own(1, h)
        couple(1, h)
    loads["fk"].wait()
    for l in range(2):
        cols = slice(l * TILE, (l + 1) * TILE)
        by_re = dot_nt(tbasis[l], fk[0, :, cols])
        by_im = dot_nt(tbasis[l], fk[1, :, cols])
        seen_own[0, l * RANK : (l + 1) * RANK] = by_re[:RANK] - by_im[RANK:]
        seen_own[1, l * RANK : (l + 1) * RANK] = by_im[:RANK] + by_re[RANK:]
    seen[:, own_slice(q), :] = seen_own[...].astype(BF16)
    copies = []

    def f_rows(index):
        return aligned(index * fgroup, fgroup, 16)

    for h in range(2):
        updated(1, h)
        for c in range(2):
            copy = pltpu.make_async_copy(
                field.at[(2 * h + c) * half : (2 * h + c + 1) * half],
                field_out.at[c, h * half : (h + 1) * half],
                local_sem.at[13 + 2 * h + c],
            )
            copy.start()
            copies.append(copy)
        lanes = half_of(h)
        x = vb[2, lanes]
        fsend[:, lanes] = lanes_joined(dot_nt(fk[0], x), dot_nt(fk[1], x)).astype(BF16)
        for d in far_order(nq):
            send(
                fsend.at[f_rows(lax.rem(q + d, nq)), lanes],
                fparts.at[d, :, lanes],
                s_f.at[h, d],
                r_f.at[h, d],
                tile=q_peer(d),
            )
    for h in range(2):
        lanes = half_of(h)
        total = fsend[f_rows(q), lanes].astype(F32)
        for d in range(1, nq):
            arrived(fparts.at[d, :, lanes], s_f.at[h, d], r_f.at[h, d])
            total = total + fparts[d, :, lanes].astype(F32)
        fz[:, lanes] = total.astype(BF16)
        for d in far_order(nz):
            send(
                fz.at[:, lanes],
                fzparts.at[d, :, lanes],
                s_fz.at[h, d],
                r_fz.at[h, d],
                tile=z_peer(d),
            )
    for d in far_order(nq):
        here = seen.at[core, own_slice(q), :]
        send(here, here, s_seen.at[d], r_seen.at[d], tile=q_peer(d))
    row = lax.broadcasted_iota(jnp.int32, (fgroup, 128), 0)
    lane128 = lax.broadcasted_iota(jnp.int32, (fgroup, 128), 1)
    shift = lax.rem(q * fgroup, 128)
    diagonal = lane128 == row + shift
    loads["target"].wait()
    wanted = target[pl.ds(q * fgroup // 128, 1), :]
    focal = fz[...].astype(F32)
    for d in range(1, nz):
        for h in range(2):
            arrived(fzparts.at[d, :, half_of(h)], s_fz.at[h, d], r_fz.at[h, d])
        focal = focal + fzparts[d].astype(F32)
    square = focal * focal
    strength = jnp.sum(square[:, :ROWS] + square[:, ROWS:], axis=1, keepdims=True)
    line = jnp.sum(jnp.where(diagonal, strength, 0.0), axis=0, keepdims=True)
    isum[...] = jnp.broadcast_to(line, (8, 128))
    for e in far_order(ns):
        send(isum, iparts.at[e], s_i.at[e], r_i.at[e], src=lax.rem(s + e, ns))
    strength = line
    for e in range(1, ns):
        arrived(iparts.at[e], s_i.at[e], r_i.at[e])
        strength = strength + iparts[e, :1, :]
    in_line = lane128[:1] - shift
    in_line = (in_line >= 0) & (in_line < fgroup)
    flat = jnp.where(in_line, jnp.tanh(strength / (2.0 * ROWS * ns)) - wanted, 0.0)
    residual = jnp.sum(jnp.where(diagonal, flat, 0.0), axis=1, keepdims=True)
    f16 = aligned(q * fgroup, fgroup, 16)
    sign = jnp.where(lane128[:1] < ROWS // 2, 1.0, -1.0)
    sign = jnp.concatenate([sign, sign], axis=1)
    wg[f16, :] = (residual * focal * sign).astype(BF16)
    for d in far_order(nq):
        here = wg.at[f16]
        send(here, here, s_wg.at[d], r_wg.at[d], tile=q_peer(d))
    rrow[...] = jnp.broadcast_to(flat, (8, 128))
    rgath[q] = jnp.broadcast_to(flat, (8, 128))
    for d in far_order(nq):
        send(rrow, rgath.at[q], s_rr.at[d], r_rr.at[d], tile=q_peer(d))
    for d in range(1, nq):
        here = seen.at[core, own_slice(lax.rem(q + nq - d, nq)), :]
        arrived(here, s_seen.at[d], r_seen.at[d])
        send(here, here, s_pass.at[d], r_pass.at[d], src=sibling)
    for d in range(1, nq):
        sender = lax.rem(q + nq - d, nq)
        arrived(wg.at[aligned(sender * fgroup, fgroup, 16)], s_wg.at[d], r_wg.at[d])
    wt[...] = jnp.transpose(wg[...].astype(F32)).astype(BF16)

    scale = float(tiles * TILE / focal_count) ** 0.5
    settled = len(pending)

    for i in range(2):
        w = wt[...]
        for k in range(2):
            cols = slice((2 * i + k) * HALF, (2 * i + k + 1) * HALF)
            u = rows_joined(dot(w, fk[0, :, cols]), dot(w, fk[1, :, cols])) * scale
            adjoint[:, cols] = u
            vb[3, :, cols] = u.astype(BF16)
        x = vb[3, :, i * TILE : (i + 1) * TILE]
        by_re = dot_nt(x, near[i, 2 * i, 0])
        by_im = dot_nt(x, near[i, 2 * i, 1])
        edge_send[i] = rows_joined(by_re, by_im).astype(BF16)
        send(
            edge_send.at[i],
            edge_in.at[1 - i],
            s_edge.at[i],
            r_edge.at[1 - i],
            tile=right if i else left,
        )

    for d in range(1, nq):
        here = seen.at[1 - core, own_slice(lax.rem(q + nq - d, nq)), :]
        arrived(here, s_pass.at[d], r_pass.at[d])
    w = wg[...]
    coefficients = (lanes_joined(dot(seen[0], w), dot(seen[1], w)) * scale).astype(BF16)
    scatter(
        2,
        None,
        lanes_joined(dot(mback[0], coefficients), dot(mback[1], coefficients)),
        True,
    )

    @pl.loop(0, 4)
    def _(step):
        m = step // 2
        half = aligned((step % 2) * HALF, HALF, HALF)
        by_re = jnp.zeros((2 * ROWS, HALF), F32)
        by_im = jnp.zeros((2 * ROWS, HALF), F32)
        for i in range(2):
            x = vb[3, :, i * TILE : (i + 1) * TILE]
            by_re = by_re + dot_nt(x, near[i, m - i + 1, 0, half, :])
            by_im = by_im + dot_nt(x, near[i, m - i + 1, 1, half, :])
        nacc[:, aligned(step * HALF, HALF, HALF)] = rows_joined(by_re, by_im)

    for copy in pending[:settled]:
        copy.wait_send()
    for side in range(2):
        arrived(edge_in.at[side], s_edge.at[side], r_edge.at[side])
    back = scattered(2, None, True)
    for l in range(2):
        cols = slice(l * TILE, (l + 1) * TILE)
        added = nacc[:, cols] + edge_in[l].astype(F32) + expanded(back, sbasis, l)
        adjoint[:, cols] = adjoint[:, cols] - DAMPING * added
        for k in range(4):
            copy = pltpu.make_async_copy(
                adjoint.at[k * half : (k + 1) * half, cols],
                adj_out.at[k % 2, (k // 2) * half : (k // 2 + 1) * half, cols],
                local_sem.at[17 + 4 * l + k],
            )
            copy.start()
            copies.append(copy)

    lines = (focal_count + 127) // 128
    for d in range(1, nq):
        sender = lax.rem(q + nq - d, nq)
        arrived(rgath.at[sender], s_rr.at[d], r_rr.at[d])
    loads["owner"].wait()
    mine = lax.broadcasted_iota(jnp.int32, (8, 128), 0) + t * 8
    found = jnp.zeros((8, 128), F32)
    for line in range(lines):
        values = jnp.zeros((8, 128), F32)
        for other in range(nq):
            if other * fgroup // 128 == line:
                values = values + rgath[other]
        owners = jnp.broadcast_to(owner[line : line + 1, :], (8, 128))
        found = found + jnp.where(owners == mine, values, 0.0)
    column = jnp.broadcast_to(jnp.sum(found, axis=1, keepdims=True), (8, 128))
    diagonal = lax.broadcasted_iota(jnp.int32, (8, 128), 0) == lax.broadcasted_iota(
        jnp.int32, (8, 128), 1
    )
    line = jnp.sum(jnp.where(diagonal, column, 0.0), axis=0, keepdims=True)
    res_out[...] = line[:, :8]

    for copy in pending[settled:]:
        copy.wait_send()
    for copy in copies:
        copy.wait()


CHUNKS = 2


def hand_out(field, residual, adjoint, field_out, residual_out, adjoint_out, held, in_sem, out_sem):
    residual_out[...] = residual[...]
    rows = held.shape[2] // CHUNKS
    loads, stores = [], []
    for k, (source, target) in enumerate(((field, field_out), (adjoint, adjoint_out))):
        for c in range(2 * CHUNKS):
            part = pl.ds((c // 2) * rows, rows)
            here = held.at[k, c % 2, part]
            loads.append(pltpu.make_async_copy(source.at[c % 2, part], here, in_sem.at[k, c]))
            stores.append(pltpu.make_async_copy(here, target.at[c % 2, part], out_sem.at[k, c]))
    for copy in loads:
        copy.start()
    for load, store in zip(loads, stores):
        load.wait()
        store.start()
    for store in stores:
        store.wait()


def per_device(
    nz,
    excitation,
    near_blocks,
    source_basis,
    target_basis,
    coupling,
    pair_rank,
    far_link,
    focal_kernel,
    focal_target,
    focal_owner,
):
    nt = lax.axis_size("tile")
    ns = lax.axis_size("src")
    nq = nt // nz
    focal_count = focal_target.shape[0]
    group = nz * PAIR
    spread = nq * PAIR
    fgroup = nz * 8
    width = 2 * TILE
    most = max(nz, nq)
    lines = (focal_count + 127) // 128
    wanted = jnp.pad(focal_target, (0, lines * 128 - focal_count))
    owner = jnp.pad(focal_owner, (0, lines * 128 - focal_count), constant_values=-1)
    vmem = pl.BlockSpec(memory_space=pltpu.VMEM)
    anywhere = pl.BlockSpec(memory_space=pl.ANY)
    dma = pltpu.SemaphoreType.DMA
    both = 2 * ROWS
    field, residual, adjoint = pl.pallas_call(
        functools.partial(kernel, nz, nq, ns),
        out_shape=(
            jax.ShapeDtypeStruct((2, ROWS, width), F32),
            jax.ShapeDtypeStruct((1, 8), F32),
            jax.ShapeDtypeStruct((2, ROWS, width), F32),
        ),
        in_specs=[anywhere] * 10,
        out_specs=(anywhere, vmem, anywhere),
        scratch_shapes=[
            pltpu.VMEM((both, width), F32),
            pltpu.VMEM((both, width), F32),
            pltpu.VMEM((2, 3, 2, TILE, TILE), BF16),
            pltpu.VMEM((2, focal_count, width), BF16),
            pltpu.VMEM((2, PAIR, TILE), BF16),
            pltpu.VMEM((2, PAIR, TILE), BF16),
            pltpu.VMEM((2, PAIR, nq * group), BF16),
            pltpu.VMEM((2, 2 * nt), jnp.int32),
            pltpu.VMEM((2, 2 * nt), jnp.int32),
            pltpu.VMEM((lines, 128), F32),
            pltpu.VMEM((lines, 128), jnp.int32),
            pltpu.VMEM((4, both, width), BF16),
            pltpu.VMEM((2, 2, both, TILE), BF16),
            pltpu.VMEM((both, width), F32),
            pltpu.VMEM((nq, PAIR, group), BF16),
            pltpu.VMEM((2, spread, group), BF16),
            pltpu.VMEM((2, group, spread), BF16),
            pltpu.VMEM((3, most * PAIR, both), BF16),
            pltpu.VMEM((3, most * PAIR, both), BF16),
            pltpu.VMEM((3, most, PAIR, both), BF16),
            pltpu.VMEM((focal_count, both), BF16),
            pltpu.VMEM((nq, fgroup, both), BF16),
            pltpu.VMEM((fgroup, both), BF16),
            pltpu.VMEM((nz, fgroup, both), BF16),
            pltpu.VMEM((8, 128), F32),
            pltpu.VMEM((ns, 8, 128), F32),
            pltpu.VMEM((focal_count, both), BF16),
            pltpu.VMEM((both, focal_count), BF16),
            pltpu.VMEM((8, 128), F32),
            pltpu.VMEM((nq, 8, 128), F32),
            pltpu.VMEM((2, both, TILE), BF16),
            pltpu.VMEM((2, both, TILE), BF16),
            pltpu.VMEM((2, spread, focal_count), BF16),
            pltpu.VMEM((2, PAIR, focal_count), F32),
            dma((25,)),
            dma((2, 2, 2)),
            dma((2, 2, 2)),
            dma((nq,)),
            dma((nq,)),
            dma((3, 2, most)),
            dma((3, 2, most)),
            dma((3, 2, most)),
            dma((3, 2, most)),
            dma((2, nq)),
            dma((2, nq)),
            dma((2, nz)),
            dma((2, nz)),
            dma((ns,)),
            dma((ns,)),
            dma((nq,)),
            dma((nq,)),
            dma((nq,)),
            dma((nq,)),
            dma((nq,)),
            dma((nq,)),
            dma((nq,)),
            dma((nq,)),
            dma((nq,)),
            dma((nq,)),
            dma((2,)),
            dma((2,)),
        ],
        compiler_params=pltpu.CompilerParams(
            collective_id=0, has_side_effects=True, vmem_limit_bytes=56 * 1024 * 1024
        ),
    )(
        excitation,
        near_blocks,
        source_basis.reshape(2, PAIR, TILE),
        target_basis.reshape(2, PAIR, TILE),
        jnp.swapaxes(coupling, 1, 2),
        pair_rank.T,
        far_link.T,
        focal_kernel,
        wanted.reshape(lines, 128),
        owner.reshape(lines, 128),
    )
    field, residual, adjoint = pl.pallas_call(
        hand_out,
        out_shape=(
            jax.ShapeDtypeStruct((2, ROWS, width), F32),
            jax.ShapeDtypeStruct((1, 8), F32),
            jax.ShapeDtypeStruct((2, ROWS, width), F32),
        ),
        in_specs=[anywhere, vmem, anywhere],
        out_specs=[anywhere, vmem, anywhere],
        scratch_shapes=[
            pltpu.VMEM((2, 2, ROWS, width), F32),
            dma((2, 2 * CHUNKS)),
            dma((2, 2 * CHUNKS)),
        ],
        compiler_params=pltpu.CompilerParams(vmem_limit_bytes=56 * 1024 * 1024),
    )(field, residual, adjoint)
    return (
        field,
        residual.reshape(8),
        adjoint,
    )


def solution(mesh):
    nt = mesh.shape["tile"]
    nz = 8 if nt % 8 == 0 and nt > 8 else 2
    return jax.shard_map(
        functools.partial(per_device, nz),
        mesh=mesh,
        in_specs=(
            P(None, "src", "tile"),
            P("tile", None, None, None, None),
            P("tile", None, None, None),
            P("tile", None, None, None),
            P(None, None, "tile"),
            P(None, "tile"),
            P(None, "tile"),
            P(None, None, "tile"),
            P(),
            P(),
        ),
        out_specs=(P(None, "src", "tile"), P("tile"), P(None, "src", "tile")),
        check_vma=False,
    )
```
